128 devices in a mesh: batch: 64 (over x, y_hi, z, core), seq: 2 (over y_lo).
Axes of the slice: x: 4, y: 4 (y_hi: 2, y_lo: 2; y = y_hi * 2 + y_lo), z: 4, core: 2. Of those that a mesh axis runs over, the one named last changes fastest.
Arguments:
- tokens: bfloat16 [64, 4, 64, 768], P('batch', None, 'seq'), may hold values from -6 to 6
- segment_counts: int32 [64], P('batch'), may hold values from 1 to 4, as said below
- ln1_gain: bfloat16 [768], P(('batch', 'seq')), may hold values from 0.5 to 1.5
- ln1_bias: bfloat16 [768], P(('batch', 'seq')), may hold values from -1.75 to 1.75
- w_qkv: bfloat16 [768, 2304], P(('batch', 'seq')), may hold values from -0.21875 to 0.21875
- q_bias: bfloat16 [768], P(('batch', 'seq')), may hold values from -3 to 3
- v_bias: bfloat16 [768], P(('batch', 'seq')), may hold values from -3 to 3
- w_out: bfloat16 [768, 768], P(('batch', 'seq')), may hold values from -1.25 to 1.25
- out_bias: bfloat16 [768], P(('batch', 'seq')), may hold values from -1.75 to 1.75
- ln2_gain: bfloat16 [768], P(('batch', 'seq')), may hold values from 0.5 to 1.5
- ln2_bias: bfloat16 [768], P(('batch', 'seq')), may hold values from -1.75 to 1.75
- w_up: bfloat16 [768, 3072], P(('batch', 'seq')), may hold values from -0.21875 to 0.21875
- up_bias: bfloat16 [3072], P(('batch', 'seq')), may hold values from -3 to 3
- w_down: bfloat16 [3072, 768], P(('batch', 'seq')), may hold values from -0.109375 to 0.109375
- down_bias: bfloat16 [768], P(('batch', 'seq')), may hold values from -1.75 to 1.75
- cotangent: bfloat16 [64, 4, 64, 768], P('batch', None, 'seq'), may hold values from -6 to 6
Outputs:
- block_out: bfloat16 [64, 4, 64, 768], P('batch', None, 'seq')
- grad_tokens: bfloat16 [64, 4, 64, 768], P('batch', None, 'seq')
- grad_ln1_gain: float32 [768], P(('batch', 'seq'))
- grad_ln1_bias: float32 [768], P(('batch', 'seq'))
- grad_w_qkv: float32 [768, 2304], P(('batch', 'seq'))
- grad_q_bias: float32 [768], P(('batch', 'seq'))
- grad_v_bias: float32 [768], P(('batch', 'seq'))
- grad_w_out: float32 [768, 768], P(('batch', 'seq'))
- grad_out_bias: float32 [768], P(('batch', 'seq'))
- grad_ln2_gain: float32 [768], P(('batch', 'seq'))
- grad_ln2_bias: float32 [768], P(('batch', 'seq'))
- grad_w_up: float32 [768, 3072], P(('batch', 'seq'))
- grad_up_bias: float32 [3072], P(('batch', 'seq'))
- grad_w_down: float32 [3072, 768], P(('batch', 'seq'))
- grad_down_bias: float32 [768], P(('batch', 'seq'))
The draws below stay inside these ranges and needn't reach their ends.
Inputs may be any that keep to these rules, and one draw needn't show every extreme that they name: `segment_counts`: slots at or beyond an item's count are absent. Some item holds 4 segments and some item holds one.
All inputs are finite; a program needn't handle non-finite values.
Results may differ from the reference program's by a relative error of at most 0.015.
Values may be sent and summed in bfloat16 or wider, within the bound.
No kernel may reach another device: no remote copies, remote signals or barrier semaphores. Data moves between devices by JAX's collectives and lax.ppermute only.
A program may use at most 128 MiB of HBM per device.

```python
import math
import jax
import jax.numpy as jnp
from jax import lax

D = 768
HEADS = 12
HEAD = 64
FF = 3072
SEGLEN = 64
NSUM = 16
MAXSEG = 4
ITEMS = 64


def draw_segment_counts(key, part):
    key = jax.random.fold_in(key, 7)
    subkeys = jax.random.split(key, 4)
    draw_first = jax.random.randint(subkeys[0], (ITEMS,), 1, MAXSEG + 1)
    draw_second = jax.random.randint(subkeys[1], (ITEMS,), 2, MAXSEG + 1)
    counts = jnp.minimum(draw_first, draw_second)
    fullest = jax.random.randint(subkeys[2], (), 0, ITEMS)
    single_at = (fullest + 1 + jax.random.randint(subkeys[3], (), 0, ITEMS - 1)) % ITEMS
    counts = counts.at[fullest].set(MAXSEG).at[single_at].set(1)
    return counts.astype(jnp.int32)


def level_of(stream_key, extent, cuts, least, high):
    def one(position, shards_of):
        steps = jax.random.uniform(jax.random.fold_in(jax.random.fold_in(stream_key, 6), position), (shards_of,), jnp.float32, least / len(cuts), high / len(cuts))
        return jnp.repeat(jnp.exp(steps), extent[position] // shards_of).reshape((-1,) + (1,) * (len(extent) - position - 1))

    factor_of = one(*cuts[0])
    for cut in cuts[1:]:
        factor_of = factor_of * one(*cut)
    return factor_of


def centred(rng, dims, scale, limit, cuts=(), held_as=jnp.bfloat16):
    level = level_of(rng, dims, cuts, -0.22, 0.18) if cuts else 1.0
    result = jax.random.normal(rng, dims, jnp.float32) * scale * level
    return jnp.minimum(jnp.maximum(result, -limit), limit).astype(held_as)


def setup_inputs(seed: int = 0) -> dict:
    key_of = jax.random.split(jax.random.key(seed), 17)
    tokens = centred(key_of[0], (ITEMS, MAXSEG, SEGLEN, D), 1.0, 6.0, ((0, 64), (2, 2)))
    segment_counts = draw_segment_counts(jax.random.fold_in(key_of[16], 71), 0)
    ln1_gain = jnp.clip(1.0 + 0.1 * jax.random.normal(key_of[2], (D,), jnp.float32), 0.5, 1.5).astype(jnp.bfloat16)
    ln1_bias = centred(key_of[3], (D,), 0.3, 1.75, ((0, 128),))
    w_qkv = centred(key_of[4], (D, 3 * D), D ** -0.5, 0.21875, ((0, 128),))
    q_bias = centred(key_of[5], (D,), 0.5, 3.0, ((0, 128),))
    v_bias = centred(key_of[6], (D,), 0.5, 3.0, ((0, 128),))
    w_out = centred(key_of[7], (D, D), (D // 32) ** -0.5, 1.25, ((0, 128),))
    out_bias = centred(key_of[8], (D,), 0.3, 1.75, ((0, 128),))
    ln2_gain = jnp.clip(1.0 + 0.1 * jax.random.normal(key_of[9], (D,), jnp.float32), 0.5, 1.5).astype(jnp.bfloat16)
    ln2_bias = centred(key_of[10], (D,), 0.3, 1.75, ((0, 128),))
    w_up = centred(key_of[11], (D, FF), D ** -0.5, 0.21875, ((0, 128),))
    up_bias = centred(key_of[12], (FF,), 0.5, 3.0, ((0, 128),))
    w_down = centred(key_of[13], (FF, D), FF ** -0.5, 0.109375, ((0, 128),))
    down_bias = centred(key_of[14], (D,), 0.3, 1.75, ((0, 128),))
    cotangent = centred(key_of[15], (ITEMS, MAXSEG, SEGLEN, D), 1.0, 6.0, ((0, 64), (2, 2)))
    return {"tokens": tokens, "segment_counts": segment_counts, "ln1_gain": ln1_gain, "ln1_bias": ln1_bias, "w_qkv": w_qkv, "q_bias": q_bias, "v_bias": v_bias, "w_out": w_out, "out_bias": out_bias, "ln2_gain": ln2_gain, "ln2_bias": ln2_bias, "w_up": w_up, "up_bias": up_bias, "w_down": w_down, "down_bias": down_bias, "cotangent": cotangent}


@jax.custom_vjp
def low(v):
    return lax.optimization_barrier(v.astype(jnp.bfloat16)).astype(jnp.float32)

@jax.custom_vjp
def low_back(v):
    return v

def low_keep(v):
    return (low(v), None)

def low_pass(kept, grad):
    return (grad,)

def back_keep(v):
    return (v, None)

def back_low(kept, grad):
    return (low(grad),)
low.defvjp(low_keep, low_pass)
low_back.defvjp(back_keep, back_low)
EPSILON = 1e-05
MASKED = -1e+30
HIGHEST = lax.Precision.HIGHEST

def norm_rows(values, gain, shift):
    center = values - lax.optimization_barrier(jnp.mean(values, axis=-1, keepdims=True))
    spread = lax.optimization_barrier(jnp.mean(center * center, axis=-1, keepdims=True))
    return center * lax.rsqrt(spread + EPSILON) * gain + shift

def project(left, right):
    return jnp.dot(left, right, precision=HIGHEST, preferred_element_type=jnp.float32)

def mask_tables():
    query_slot = jnp.arange(MAXSEG * SEGLEN) // SEGLEN
    query_pos = jnp.arange(MAXSEG * SEGLEN) % SEGLEN
    is_summary = query_pos[None, :] >= SEGLEN - NSUM
    same_slot = (query_slot[None, :] == query_slot[:, None]) & (query_pos[None, :] <= query_pos[:, None])
    recent = ((query_slot[None, :] == query_slot[:, None] - 1) | (query_slot[None, :] == query_slot[:, None] - 2)) & is_summary
    older_rows = (query_slot[None, :] <= query_slot[:, None] - 3) & is_summary
    return (same_slot | recent, older_rows)

def block_step(params, consts, block, const_block, present):
    ln1_gain, ln1_bias, w_qkv, q_bias, v_bias, w_out, out_bias, ln2_gain, ln2_bias, w_up, up_bias, w_down, down_bias = params
    groups = block.shape[0]
    token_rows = block.reshape(-1, D)
    const_rows = const_block.reshape(-1, D)
    normed = low(norm_rows(token_rows, ln1_gain, ln1_bias))
    qkv_shift = jnp.concatenate([q_bias, jnp.zeros_like(q_bias), v_bias])
    merged = low(low_back(project(normed, w_qkv) + qkv_shift))
    const_normed = low(norm_rows(const_rows, consts[0], consts[1]))
    const_shift = jnp.concatenate([jnp.zeros_like(consts[4]), consts[4]])
    const_kv = low(low_back(project(const_normed, consts[2][:, D:]) + const_shift))
    item_shape = (groups, MAXSEG * SEGLEN, HEADS, HEAD)
    query = merged[:, :D].reshape(item_shape)
    keys_all = jnp.concatenate([merged[:, D:2 * D].reshape(item_shape), const_kv[:, :D].reshape(item_shape)], axis=1)
    values_all = jnp.concatenate([merged[:, 2 * D:].reshape(item_shape), const_kv[:, D:].reshape(item_shape)], axis=1)
    live_mask, older_mask = mask_tables()
    allowed = jnp.concatenate([live_mask, older_mask], axis=1)
    scores = jnp.einsum('gqhe,gkhe->ghqk', query, keys_all, precision=HIGHEST) * HEAD ** (-0.5)
    scores = low_back(jnp.where(allowed[None, None], scores, MASKED))
    weights = low(jax.nn.softmax(scores, axis=-1))
    mixed = jnp.einsum('ghqk,gkhe->gqhe', weights, values_all, precision=HIGHEST)
    mixed = low(low_back(mixed.reshape(-1, D)))
    attended = low_back(project(mixed, w_out) + out_bias)
    hidden = token_rows + attended
    normed_two = low(norm_rows(hidden, ln2_gain, ln2_bias))
    upward = low_back(project(normed_two, w_up) + up_bias)
    active = low(jax.nn.gelu(upward, approximate=False))
    branch = low_back(project(active, w_down) + down_bias)
    present_rows = jnp.repeat(present, SEGLEN, axis=1).reshape(-1, 1)
    return ((hidden + branch) * present_rows).reshape(block.shape)

def reference(tokens, segment_counts, ln1_gain, ln1_bias, w_qkv, q_bias, v_bias, w_out, out_bias, ln2_gain, ln2_bias, w_up, up_bias, w_down, down_bias, cotangent):
    params = tuple((weight.astype(jnp.float32) for weight in (ln1_gain, ln1_bias, w_qkv, q_bias, v_bias, w_out, out_bias, ln2_gain, ln2_bias, w_up, up_bias, w_down, down_bias)))
    tokens_f = tokens.astype(jnp.float32)
    group = math.gcd(ITEMS, 16)
    nsteps = ITEMS // group
    present = (jnp.arange(MAXSEG)[None, :] < segment_counts[:, None]).astype(jnp.float32)
    const_grouped = tokens_f.reshape(nsteps, group, MAXSEG, SEGLEN, D)
    present_grouped = present.reshape(nsteps, group, MAXSEG)
    stepper = jax.checkpoint(block_step)

    def forward(live_tokens, live_params):

        def scan_body(carry, inputs):
            return (carry, stepper(live_params, params, inputs[0], inputs[1], inputs[2]))
        grouped = live_tokens.reshape(nsteps, group, MAXSEG, SEGLEN, D)
        carry, outputs = lax.scan(scan_body, jnp.zeros((), jnp.float32), (grouped, const_grouped, present_grouped))
        return outputs.reshape(ITEMS, MAXSEG, SEGLEN, D)
    output, pullback = jax.vjp(forward, tokens_f, params)
    grad_input, grads = pullback(cotangent.astype(jnp.float32))
    return (output.astype(jnp.bfloat16), grad_input.astype(jnp.bfloat16), grads[0], grads[1], grads[2], grads[3], grads[4], grads[5], grads[6], grads[7], grads[8], grads[9], grads[10], grads[11], grads[12])
```

```python
import jax
import jax.numpy as jnp
import numpy as np
from jax import lax
from jax.experimental import pallas as pl
from jax.experimental.pallas import tpu as pltpu
from jax.sharding import Mesh
from jax.sharding import PartitionSpec as P

WIDTH = 768
HEAD = 64
NSUM = 16
SLOTS = 4
SEGLEN = 64
HALFSEG = 32
FF = 3072

EPSILON = 1e-05
MASKED = -1e30
SCALE = HEAD ** (-0.5)

AXES = ("x", "yh", "z", "c", "yl")
SIZES = (4, 2, 4, 2, 2)
QUAD_AXES = ("x", "yh", "z")
QUADS = 32
DEVICES = 128
ROWS = 256
OWN = 128
HALF = WIDTH // 2
QKV = 3 * HALF
UP = FF // 2
SMALL = 128
VMEM_LIMIT = 60 * 1024 * 1024

F32 = jnp.float32
BF16 = jnp.bfloat16


def dot_nn(left, right):
    return jnp.dot(left, right, preferred_element_type=F32)


def dot_tn(left, right):
    return lax.dot_general(left, right, (((0,), (0,)), ((), ())), preferred_element_type=F32)


def dot_nt(left, right):
    return lax.dot_general(left, right, (((1,), (1,)), ((), ())), preferred_element_type=F32)


def normalised(values):
    center = values - jnp.mean(values, axis=-1, keepdims=True)
    spread = jnp.mean(center * center, axis=-1, keepdims=True)
    scale = lax.rsqrt(spread + EPSILON)
    return center * scale, scale


def norm_back(grad, unit, scale, gain):
    inner = grad * gain
    mean = jnp.mean(inner, axis=-1, keepdims=True)
    along = jnp.mean(inner * unit, axis=-1, keepdims=True)
    return scale * (inner - mean - unit * along)


def total(values):
    return jnp.sum(values.astype(F32), axis=0, keepdims=True)


def swap_halves(values):
    return jnp.concatenate([values[OWN:], values[:OWN]], axis=0)


def masks(core):
    def place(dim):
        row = lax.broadcasted_iota(jnp.int32, (ROWS, ROWS), dim)
        second = (row >= OWN).astype(jnp.int32)
        inner = row - second * OWN
        half = core + second - 2 * core * second
        slot = inner // HALFSEG
        return slot, half * HALFSEG + inner - slot * HALFSEG

    query_slot, query_pos = place(0)
    key_slot, key_pos = place(1)
    same = (query_slot == key_slot) & (key_pos <= query_pos)
    earlier = (key_slot < query_slot) & (key_pos >= SEGLEN - NSUM)
    return same | earlier, key_slot >= query_slot - 2


def head_lanes(j):
    lane = lax.broadcasted_iota(jnp.int32, (1, 2 * HEAD), 1)
    return jnp.where(lane // HEAD == j, 1.0, 0.0).astype(BF16)


def attend_kernel(core_ref, x_ref, gain_ref, shift_ref, w_ref, b_ref, a_ref, qkv_ref, o_ref, lse_ref):
    unit, _ = normalised(x_ref[...].astype(F32))
    a = (unit * gain_ref[...] + shift_ref[...]).astype(BF16)
    a_ref[...] = a
    qkv_ref[...] = (dot_nn(a, w_ref[...]) + b_ref[...]).astype(BF16)
    admitted, _ = masks(core_ref[0])
    lane = lax.broadcasted_iota(jnp.int32, (ROWS, 128), 1)
    kept = jnp.zeros((ROWS, 128), F32)
    for pair in range(3):
        lanes = pl.ds(128 * pair, 128)
        query = qkv_ref[:, lanes]
        key = qkv_ref[:, pl.ds(HALF + 128 * pair, 128)]
        value = qkv_ref[:, pl.ds(2 * HALF + 128 * pair, 128)]
        out = jnp.zeros((ROWS, 128), F32)
        for j in range(2):
            only = head_lanes(j)
            scores = jnp.where(admitted, dot_nt(query * only, key) * SCALE, MASKED)
            top = jnp.max(scores, axis=-1, keepdims=True)
            grown = jnp.exp(scores - top)
            amount = jnp.sum(grown, axis=-1, keepdims=True)
            kept = jnp.where(lane == 2 * pair + j, top + jnp.log(amount), kept)
            probs = (grown * (1.0 / amount)).astype(BF16)
            out += dot_nn(probs, value * only)
        o_ref[:, lanes] = out.astype(BF16)
    lse_ref[...] = kept


def mlp_kernel(
    core_ref, x_ref, own_o_ref, far_o_ref, own_out_ref, far_out_ref, vec_ref, up_ref, up_b_ref, down_ref, g_ref,
    h_ref, m_own_ref, m_far_ref, grad_a_ref, grad_up_ref, grad_down_ref, grad_up_b_ref, grad_down_b_ref,
):
    core = core_ref[0]
    here = pl.multiple_of(core * HALF, 128)
    there = pl.multiple_of((1 - core) * HALF, 128)
    own_o = own_o_ref[...]
    far_o = swap_halves(far_o_ref[...])
    for out_ref, at in ((own_out_ref, here), (far_out_ref, there)):
        part = dot_nn(own_o, out_ref[pl.ds(here, HALF), :]) + dot_nn(far_o, out_ref[pl.ds(there, HALF), :])
        h_ref[:, pl.ds(at, HALF)] = part
    hidden = x_ref[...].astype(F32) + (h_ref[...] + vec_ref[0:1, :])
    h_ref[...] = hidden
    unit, _ = normalised(hidden)
    a = (unit * vec_ref[1:2, :] + vec_ref[2:3, :]).astype(BF16)
    g = g_ref[...]
    branch = jnp.zeros((ROWS, WIDTH), F32)
    grad_a = jnp.zeros((ROWS, WIDTH), F32)
    step = 512
    for i in range(UP // step):
        cols = pl.ds(i * step, step)
        up = up_ref[:, cols]
        down = down_ref[cols, :]
        u = dot_nn(a, up) + up_b_ref[:, cols]
        phi = 0.5 * (1.0 + lax.erf(u * (0.5**0.5)))
        z = (u * phi).astype(BF16)
        slope = phi + u * (jnp.exp(-0.5 * u * u) * (2.0 * jnp.pi) ** (-0.5))
        branch += dot_nn(z, down)
        gu = (dot_nt(g, down) * slope).astype(BF16)
        grad_down_ref[cols, :] = dot_tn(z, g).astype(BF16)
        grad_up_ref[:, cols] = dot_tn(a, gu).astype(BF16)
        grad_up_b_ref[:, cols] = total(gu)
        grad_a += dot_nt(gu, up)
    m_own_ref[...] = branch[:OWN] + hidden[:OWN] + vec_ref[3:4, :]
    m_far_ref[...] = branch[OWN:]
    grad_a_ref[...] = grad_a
    grad_down_b_ref[...] = total(g[:OWN])


def back_kernel(
    core_ref, h_ref, g_ref, own_grad_ref, far_grad_ref, vec_ref, own_o_ref, far_o_ref, own_out_ref, far_out_ref,
    qkv_ref, lse_ref, a_ref, w_ref,
    grad_w_ref, grad_out_ref, own_x_ref, far_x_ref, gh_ref, vec_out_ref, grad_b_ref,
    gh_low_ref, go_ref, gqkv_ref,
):
    core = core_ref[0]
    here = pl.multiple_of(core * HALF, 128)
    there = pl.multiple_of((1 - core) * HALF, 128)
    grad_a = own_grad_ref[...] + swap_halves(far_grad_ref[...])
    unit, scale = normalised(h_ref[...])
    grad_h = g_ref[...].astype(F32) + norm_back(grad_a, unit, scale, vec_ref[1:2, :])
    gh_ref[...] = grad_h[:OWN]
    low = grad_h.astype(BF16)
    gh_low_ref[...] = low
    vec_out_ref[0:1, :] = total(low[:OWN])
    vec_out_ref[1:2, :] = total(grad_a[:OWN] * unit[:OWN])
    vec_out_ref[2:3, :] = total(grad_a[:OWN])
    low_here = gh_low_ref[:, pl.ds(here, HALF)]
    low_there = gh_low_ref[:, pl.ds(there, HALF)]
    own_o = own_o_ref[...]
    far_o = swap_halves(far_o_ref[...])
    grad_out_ref[pl.ds(here, HALF), :] = dot_tn(own_o, low_here).astype(BF16)
    grad_out_ref[pl.ds(there, HALF), :] = dot_tn(far_o, low_here).astype(BF16)
    rows = pl.ds(here, HALF)
    go_ref[...] = (dot_nt(low_here, own_out_ref[rows, :]) + dot_nt(low_there, far_out_ref[rows, :])).astype(BF16)
    admitted, live = masks(core)
    live = jnp.where(live, 1.0, 0.0)
    lane = lax.broadcasted_iota(jnp.int32, (ROWS, 128), 1)
    for pair in range(3):
        query = qkv_ref[:, pl.ds(128 * pair, 128)]
        key = qkv_ref[:, pl.ds(HALF + 128 * pair, 128)]
        value = qkv_ref[:, pl.ds(2 * HALF + 128 * pair, 128)]
        go = go_ref[:, pl.ds(128 * pair, 128)]
        gq = jnp.zeros((ROWS, 128), F32)
        gk = jnp.zeros((ROWS, 128), F32)
        gv = jnp.zeros((ROWS, 128), F32)
        for j in range(2):
            only = head_lanes(j)
            lse = jnp.sum(jnp.where(lane == 2 * pair + j, lse_ref[...], 0.0), axis=-1, keepdims=True)
            scores = jnp.where(admitted, dot_nt(query * only, key) * SCALE, MASKED)
            probs = jnp.exp(scores - lse)
            grad_p = dot_nt(go * only, value)
            grad_s = probs * (grad_p - jnp.sum(probs * grad_p, axis=-1, keepdims=True))
            gq += dot_nn(grad_s.astype(BF16), key * only)
            gk += dot_tn((grad_s * live).astype(BF16), query * only)
            gv += dot_tn((probs * live).astype(BF16), go * only)
        gqkv_ref[:, pl.ds(128 * pair, 128)] = (gq * SCALE).astype(BF16)
        gqkv_ref[:, pl.ds(HALF + 128 * pair, 128)] = (gk * SCALE).astype(BF16)
        gqkv_ref[:, pl.ds(2 * HALF + 128 * pair, 128)] = gv.astype(BF16)
    gqkv = gqkv_ref[...]
    grad_w_ref[...] = dot_tn(a_ref[...], gqkv).astype(BF16)
    grad_b_ref[...] = total(gqkv)
    grad_x = dot_nt(gqkv, w_ref[...])
    own_x_ref[...] = grad_x[:OWN]
    far_x_ref[...] = grad_x[OWN:]


def tokens_kernel(x_ref, own_ref, far_ref, gh_ref, gain_ref, out_ref, vec_ref):
    grad = own_ref[...] + far_ref[...]
    unit, scale = normalised(x_ref[...].astype(F32))
    out_ref[...] = (gh_ref[...] + norm_back(grad, unit, scale, gain_ref[...])).astype(BF16)
    vec_ref[0:1, :] = total(grad * unit)
    vec_ref[1:2, :] = total(grad)


def call(kernel, core, args, outs, scratch=()):
    specs = [pl.BlockSpec(memory_space=pltpu.VMEM)] * len(args)
    if core is not None:
        args = (core,) + tuple(args)
        specs = [pl.BlockSpec(memory_space=pltpu.SMEM)] + specs
    return pl.pallas_call(
        kernel,
        out_shape=tuple(jax.ShapeDtypeStruct(s, d) for s, d in outs),
        in_specs=specs,
        out_specs=tuple(pl.BlockSpec(memory_space=pltpu.VMEM) for _ in outs),
        scratch_shapes=[pltpu.VMEM(s, d) for s, d in scratch],
        compiler_params=pltpu.CompilerParams(vmem_limit_bytes=VMEM_LIMIT),
    )(*args)


def between_cores(values):
    return lax.ppermute(values, "c", [(0, 1), (1, 0)])


def between_chips(values):
    return lax.ppermute(values, "yl", [(0, 1), (1, 0)])


def swap_items(values):
    return lax.ppermute(values, ("c", "yl"), [(0, 0), (1, 2), (2, 1), (3, 3)])


HALVES = [(64 * c + 2 * k + yl, 4 * k + 2 * c + yl) for k in range(QUADS) for c in range(2) for yl in range(2)]


def halves_out(values):
    return lax.ppermute(values, AXES, HALVES)


def halves_back(values):
    return lax.ppermute(values, AXES, [(b, a) for a, b in HALVES])


def gather(block):
    spread = jnp.broadcast_to(block[None], (QUADS,) + block.shape)
    got = lax.all_to_all(spread, QUAD_AXES, 0, 0, tiled=True)
    return got.reshape(QUADS * block.shape[0], block.shape[1])


def reduce(grads):
    rows = grads.shape[0] // QUADS
    got = lax.all_to_all(grads.reshape(QUADS, rows, grads.shape[1]), QUAD_AXES, 0, 0, tiled=True)
    return jnp.sum(got.astype(F32), axis=0)


def by_place(place, first, second, axis=0):
    return jnp.where(
        place == 0, jnp.concatenate([first, second], axis), jnp.concatenate([second, first], axis)
    )


def shards(
    tokens,
    segment_counts,
    ln1_gain,
    ln1_bias,
    w_qkv,
    q_bias,
    v_bias,
    w_out,
    out_bias,
    ln2_gain,
    ln2_bias,
    w_up,
    up_bias,
    w_down,
    down_bias,
    cotangent,
):
    core = lax.axis_index("c")
    side = lax.axis_index("yl")
    core_arg = core.astype(jnp.int32).reshape(1)
    present = jnp.arange(SLOTS) < segment_counts[0]
    present_rows = jnp.repeat(present, HALFSEG)[:, None]
    cot = jnp.where(present_rows, cotangent.reshape(OWN, WIDTH), 0).astype(BF16)
    mine = swap_items(jnp.concatenate([tokens.reshape(OWN, WIDTH), cot], axis=1))
    item = jnp.concatenate([mine, between_cores(mine)], axis=0)
    x, g = item[:, :WIDTH], item[:, WIDTH:]

    small = jnp.stack([ln1_gain, ln1_bias, q_bias, v_bias, out_bias, ln2_gain, ln2_bias, down_bias], axis=1)
    small = jnp.concatenate([small, up_bias.reshape(6, 4), jnp.zeros((6, SMALL - 12), BF16)], axis=1)

    def half_of(t):
        parts = [w_qkv[:, j * WIDTH + t * HALF : j * WIDTH + (t + 1) * HALF] for j in range(3)]
        parts += [small, w_out[:, t * HALF : (t + 1) * HALF], w_up[:, t * UP : (t + 1) * UP]]
        return jnp.concatenate(parts, axis=1)

    first, second = half_of(0), half_of(1)
    rows = lax.all_to_all(jnp.stack([first, first, second, second]), ("c", "yl"), 0, 0, tiled=True)
    rows = rows.reshape(24, QKV + SMALL + HALF + UP)
    near = halves_out(w_down)
    down_rows = by_place(side, near, between_chips(near))

    attn = gather(rows[:, : QKV + SMALL + HALF])
    w_in = attn[:, :QKV]
    small_all = attn[:, QKV : QKV + SMALL]
    own_out = attn[:, QKV + SMALL :]
    far_out = between_cores(own_out)
    vectors = small_all[:, :12].T.astype(F32)
    at = core * HALF
    query_b = lax.dynamic_slice(vectors[2:3], (0, at), (1, HALF))
    value_b = lax.dynamic_slice(vectors[3:4], (0, at), (1, HALF))
    qkv_b = jnp.concatenate([query_b, jnp.zeros_like(query_b), value_b], axis=1)
    up_b = lax.dynamic_slice(small_all, (at, 8), (HALF, 4)).reshape(1, UP).astype(F32)
    mid_vec = jnp.concatenate([vectors[4:8], jnp.zeros((4, WIDTH), F32)], axis=0)

    a1, qkv, own_o, lse = call(
        attend_kernel,
        core_arg,
        (x, vectors[0:1], vectors[1:2], w_in, qkv_b),
        (((ROWS, WIDTH), BF16), ((ROWS, QKV), BF16), ((ROWS, HALF), BF16), ((ROWS, 128), F32)),
    )
    far_o = between_cores(own_o)
    w_up_all = gather(rows[:, QKV + SMALL + HALF :])
    w_down_all = gather(down_rows)
    hidden, m_own, m_far, grad_a_own, grad_up, grad_down, grad_up_b, grad_down_b = call(
        mlp_kernel,
        core_arg,
        (x, own_o, far_o, own_out, far_out, mid_vec, w_up_all, up_b, w_down_all, g),
        (
            ((ROWS, WIDTH), F32),
            ((OWN, WIDTH), F32),
            ((OWN, WIDTH), F32),
            ((ROWS, WIDTH), F32),
            ((WIDTH, UP), BF16),
            ((UP, WIDTH), BF16),
            ((1, UP), F32),
            ((1, WIDTH), F32),
        ),
    )
    grad_a_far = between_cores(grad_a_own)
    block = swap_items((m_own + between_cores(m_far)).astype(BF16))
    block_out = jnp.where(present_rows, block, 0).reshape(tokens.shape)

    grad_w, grad_out, own_x, far_x, gh, vec_mid, grad_b = call(
        back_kernel,
        core_arg,
        (hidden, g, grad_a_own, grad_a_far, mid_vec, own_o, far_o, own_out, far_out, qkv, lse, a1, w_in),
        (
            ((WIDTH, QKV), BF16),
            ((WIDTH, HALF), BF16),
            ((OWN, WIDTH), F32),
            ((OWN, WIDTH), F32),
            ((OWN, WIDTH), F32),
            ((3, WIDTH), F32),
            ((1, QKV), F32),
        ),
        (((ROWS, WIDTH), BF16), ((ROWS, HALF), BF16), ((ROWS, QKV), BF16)),
    )
    grad_x, vec_first = call(
        tokens_kernel,
        None,
        (x[:OWN], own_x, between_cores(far_x), gh, vectors[0:1]),
        (((OWN, WIDTH), BF16), ((2, WIDTH), F32)),
    )
    grad_tokens = swap_items(grad_x).reshape(tokens.shape)

    def placed(values, length):
        return lax.dynamic_update_slice(jnp.zeros((1, length), F32), values, (0, core * values.shape[1]))

    grad_vec = jnp.concatenate(
        [
            vec_first,
            placed(grad_b[:, :HALF], WIDTH),
            placed(grad_b[:, 2 * HALF :], WIDTH),
            vec_mid,
            grad_down_b,
            placed(grad_up_b, FF).reshape(WIDTH, 4).T,
        ],
        axis=0,
    ).T
    high = grad_vec.astype(BF16)
    low = (grad_vec - high.astype(F32)).astype(BF16)
    grad_small = jnp.concatenate([high, low, jnp.zeros((WIDTH, SMALL - 24), BF16)], axis=1)

    down_sum = reduce(grad_down)
    down_near = jnp.where(side == 0, down_sum[:24], down_sum[24:])
    down_other = jnp.where(side == 0, down_sum[24:], down_sum[:24])
    out_down = halves_back(down_near + between_chips(down_other))
    row_sum = jnp.concatenate(
        [reduce(jnp.concatenate([grad_w, grad_small, grad_out], axis=1)), reduce(grad_up)], axis=1
    )
    got = lax.all_to_all(row_sum.reshape(4, 6, row_sum.shape[1]), ("c", "yl"), 0, 0, tiled=True)
    both = got[0::2] + got[1::2]
    out_qkv = jnp.concatenate(
        [both[t, :, j * HALF : (j + 1) * HALF] for j in range(3) for t in range(2)], axis=1
    )
    vec = both[0, :, QKV : QKV + SMALL] + both[1, :, QKV : QKV + SMALL]
    vec = vec[:, :12] + vec[:, 12:24]
    out_out = jnp.concatenate([both[t, :, QKV + SMALL : QKV + SMALL + HALF] for t in range(2)], axis=1)
    out_up = jnp.concatenate([both[t, :, QKV + SMALL + HALF :] for t in range(2)], axis=1)
    return (
        block_out,
        grad_tokens,
        vec[:, 0],
        vec[:, 1],
        out_qkv,
        vec[:, 2],
        vec[:, 3],
        out_out,
        vec[:, 4],
        vec[:, 5],
        vec[:, 6],
        out_up,
        vec[:, 8:12].reshape(24),
        out_down,
        vec[:, 7],
    )


def solution(mesh):
    torus = Mesh(np.asarray(mesh.devices).reshape(SIZES), AXES)
    items = P(("x", "yh", "z", "c"), None, "yl", None)
    part, rows = P(AXES), P(AXES, None)
    return jax.shard_map(
        shards,
        mesh=torus,
        in_specs=(
            items, P(("x", "yh", "z", "c")), part, part, rows, part, part, rows, part, part, part, rows, part, rows,
            part, items,
        ),
        out_specs=(
            items, items, part, part, rows, part, part, rows, part, part, part, rows, part, rows, part,
        ),
        check_vma=False,
    )
```

```python
import jax
import jax.numpy as jnp
import numpy as np
from jax import lax
from jax.experimental import pallas as pl
from jax.experimental.pallas import tpu as pltpu
from jax.sharding import Mesh
from jax.sharding import PartitionSpec as P

WIDTH = 768
HEAD = 64
NSUM = 16
SLOTS = 4
SEGLEN = 64
HALFSEG = 32
FF = 3072

EPSILON = 1e-05
MASKED = -1e30
SCALE = HEAD ** (-0.5)

AXES = ("x", "yh", "z", "c", "yl")
SIZES = (4, 2, 4, 2, 2)
QUAD_AXES = ("x", "yh", "z")
QUADS = 32
DEVICES = 128
ROWS = 256
OWN = 128
HALF = WIDTH // 2
QKV = 3 * HALF
UP = FF // 2
SMALL = 128
ATTN = QKV + SMALL + HALF
UP_ROWS = WIDTH // 4
DOWN_ROWS = UP // 4
RING_Y = ("yh", "yl")
VMEM_LIMIT = 60 * 1024 * 1024

F32 = jnp.float32
BF16 = jnp.bfloat16


def dot_nn(left, right):
    return jnp.dot(left, right, preferred_element_type=F32)


def dot_tn(left, right):
    return lax.dot_general(left, right, (((0,), (0,)), ((), ())), preferred_element_type=F32)


def dot_nt(left, right):
    return lax.dot_general(left, right, (((1,), (1,)), ((), ())), preferred_element_type=F32)


def normalised(values):
    center = values - jnp.mean(values, axis=-1, keepdims=True)
    spread = jnp.mean(center * center, axis=-1, keepdims=True)
    scale = lax.rsqrt(spread + EPSILON)
    return center * scale, scale


def norm_back(grad, unit, scale, gain):
    inner = grad * gain
    mean = jnp.mean(inner, axis=-1, keepdims=True)
    along = jnp.mean(inner * unit, axis=-1, keepdims=True)
    return scale * (inner - mean - unit * along)


def total(values):
    return jnp.sum(values.astype(F32), axis=0, keepdims=True)


def swap_halves(values):
    return jnp.concatenate([values[OWN:], values[:OWN]], axis=0)


def masks(core):
    def place(dim):
        row = lax.broadcasted_iota(jnp.int32, (ROWS, ROWS), dim)
        second = (row >= OWN).astype(jnp.int32)
        inner = row - second * OWN
        half = core + second - 2 * core * second
        slot = inner // HALFSEG
        return slot, half * HALFSEG + inner - slot * HALFSEG

    query_slot, query_pos = place(0)
    key_slot, key_pos = place(1)
    same = (query_slot == key_slot) & (key_pos <= query_pos)
    earlier = (key_slot < query_slot) & (key_pos >= SEGLEN - NSUM)
    return same | earlier, key_slot >= query_slot - 2


def head_lanes(j):
    lane = lax.broadcasted_iota(jnp.int32, (1, 2 * HEAD), 1)
    return jnp.where(lane // HEAD == j, 1.0, 0.0).astype(BF16)


def attend_kernel(place_ref, x_ref, gain_ref, shift_ref, w_ref, b_ref, a_ref, qkv_ref, o_ref, lse_ref):
    unit, _ = normalised(x_ref[...].astype(F32))
    a = (unit * gain_ref[...] + shift_ref[...]).astype(BF16)
    a_ref[...] = a
    qkv_ref[...] = (dot_nn(a, w_ref[...]) + b_ref[...]).astype(BF16)
    admitted, _ = masks(place_ref[0])
    lane = lax.broadcasted_iota(jnp.int32, (ROWS, 128), 1)
    kept = jnp.zeros((ROWS, 128), F32)
    for pair in range(3):
        lanes = pl.ds(128 * pair, 128)
        query = qkv_ref[:, lanes]
        key = qkv_ref[:, pl.ds(HALF + 128 * pair, 128)]
        value = qkv_ref[:, pl.ds(2 * HALF + 128 * pair, 128)]
        out = jnp.zeros((ROWS, 128), F32)
        for j in range(2):
            only = head_lanes(j)
            scores = jnp.where(admitted, dot_nt(query * only, key) * SCALE, MASKED)
            top = jnp.max(scores, axis=-1, keepdims=True)
            grown = jnp.exp(scores - top)
            amount = jnp.sum(grown, axis=-1, keepdims=True)
            kept = jnp.where(lane == 2 * pair + j, top + jnp.log(amount), kept)
            probs = (grown * (1.0 / amount)).astype(BF16)
            out += dot_nn(probs, value * only)
        o_ref[:, lanes] = out.astype(BF16)
    lse_ref[...] = kept


def mlp_kernel(
    place_ref, x_ref, own_o_ref, far_o_ref, own_out_ref, far_out_ref, vec_ref, up_b_ref, g_ref,
    up_0, up_1, up_2, up_3, down_0, down_1, down_2, down_3,
    h_ref, m_own_ref, m_far_ref, grad_a_ref, grad_up_b_ref, grad_down_b_ref,
    gup_0, gup_1, gup_2, gup_3, gdown_0, gdown_1, gdown_2, gdown_3,
    up_ref, down_ref, grad_up_ref, grad_down_ref,
):
    core, x_at, y_at = place_ref[0], place_ref[1], place_ref[2]
    for j, (up, down) in enumerate(((up_0, down_0), (up_1, down_1), (up_2, down_2), (up_3, down_3))):
        up_ref[pl.ds(pl.multiple_of(lax.rem(x_at + j, 4) * UP_ROWS, 64), UP_ROWS), :] = up[...]
        down_ref[pl.ds(pl.multiple_of(lax.rem(y_at + j, 4) * DOWN_ROWS, 128), DOWN_ROWS), :] = down[...]
    here = pl.multiple_of(core * HALF, 128)
    there = pl.multiple_of((1 - core) * HALF, 128)
    own_o = own_o_ref[...]
    far_o = swap_halves(far_o_ref[...])
    for out_ref, at in ((own_out_ref, here), (far_out_ref, there)):
        part = dot_nn(own_o, out_ref[pl.ds(here, HALF), :]) + dot_nn(far_o, out_ref[pl.ds(there, HALF), :])
        h_ref[:, pl.ds(at, HALF)] = part
    hidden = x_ref[...].astype(F32) + (h_ref[...] + vec_ref[0:1, :])
    h_ref[...] = hidden
    unit, _ = normalised(hidden)
    a = (unit * vec_ref[1:2, :] + vec_ref[2:3, :]).astype(BF16)
    g = g_ref[...]
    branch = jnp.zeros((ROWS, WIDTH), F32)
    grad_a = jnp.zeros((ROWS, WIDTH), F32)
    step = 512
    for i in range(UP // step):
        cols = pl.ds(i * step, step)
        up = up_ref[:, cols]
        down = down_ref[cols, :]
        u = dot_nn(a, up) + up_b_ref[:, cols]
        phi = 0.5 * (1.0 + lax.erf(u * (0.5**0.5)))
        z = (u * phi).astype(BF16)
        slope = phi + u * (jnp.exp(-0.5 * u * u) * (2.0 * jnp.pi) ** (-0.5))
        branch += dot_nn(z, down)
        gu = (dot_nt(g, down) * slope).astype(BF16)
        grad_down_ref[cols, :] = dot_tn(z, g).astype(BF16)
        grad_up_ref[:, cols] = dot_tn(a, gu).astype(BF16)
        grad_up_b_ref[:, cols] = total(gu)
        grad_a += dot_nt(gu, up)
    m_own_ref[...] = branch[:OWN] + hidden[:OWN] + vec_ref[3:4, :]
    m_far_ref[...] = branch[OWN:]
    grad_a_ref[...] = grad_a
    grad_down_b_ref[...] = total(g[:OWN])
    for j, (gup, gdown) in enumerate(((gup_0, gdown_0), (gup_1, gdown_1), (gup_2, gdown_2), (gup_3, gdown_3))):
        gup[...] = grad_up_ref[pl.ds(pl.multiple_of(lax.rem(x_at + j, 4) * UP_ROWS, 64), UP_ROWS), :]
        gdown[...] = grad_down_ref[pl.ds(pl.multiple_of(lax.rem(y_at + j, 4) * DOWN_ROWS, 128), DOWN_ROWS), :]


def back_kernel(
    place_ref, h_ref, g_ref, own_grad_ref, far_grad_ref, vec_ref, own_out_ref, far_out_ref, qkv_ref, lse_ref, w_ref,
    gqkv_ref, gh_low_ref, own_x_ref, far_x_ref, gh_ref, vec_out_ref,
    go_ref,
):
    core = place_ref[0]
    here = pl.multiple_of(core * HALF, 128)
    there = pl.multiple_of((1 - core) * HALF, 128)
    grad_a = own_grad_ref[...] + swap_halves(far_grad_ref[...])
    unit, scale = normalised(h_ref[...])
    grad_h = g_ref[...].astype(F32) + norm_back(grad_a, unit, scale, vec_ref[1:2, :])
    gh_ref[...] = grad_h[:OWN]
    low = grad_h.astype(BF16)
    gh_low_ref[...] = low
    vec_out_ref[0:1, :] = total(low[:OWN])
    vec_out_ref[1:2, :] = total(grad_a[:OWN] * unit[:OWN])
    vec_out_ref[2:3, :] = total(grad_a[:OWN])
    low_here = gh_low_ref[:, pl.ds(here, HALF)]
    low_there = gh_low_ref[:, pl.ds(there, HALF)]
    rows = pl.ds(here, HALF)
    go_ref[...] = (dot_nt(low_here, own_out_ref[rows, :]) + dot_nt(low_there, far_out_ref[rows, :])).astype(BF16)
    admitted, live = masks(core)
    live = jnp.where(live, 1.0, 0.0)
    lane = lax.broadcasted_iota(jnp.int32, (ROWS, 128), 1)
    for pair in range(3):
        query = qkv_ref[:, pl.ds(128 * pair, 128)]
        key = qkv_ref[:, pl.ds(HALF + 128 * pair, 128)]
        value = qkv_ref[:, pl.ds(2 * HALF + 128 * pair, 128)]
        go = go_ref[:, pl.ds(128 * pair, 128)]
        gq = jnp.zeros((ROWS, 128), F32)
        gk = jnp.zeros((ROWS, 128), F32)
        gv = jnp.zeros((ROWS, 128), F32)
        for j in range(2):
            only = head_lanes(j)
            lse = jnp.sum(jnp.where(lane == 2 * pair + j, lse_ref[...], 0.0), axis=-1, keepdims=True)
            scores = jnp.where(admitted, dot_nt(query * only, key) * SCALE, MASKED)
            probs = jnp.exp(scores - lse)
            grad_p = dot_nt(go * only, value)
            grad_s = probs * (grad_p - jnp.sum(probs * grad_p, axis=-1, keepdims=True))
            gq += dot_nn(grad_s.astype(BF16), key * only)
            gk += dot_tn((grad_s * live).astype(BF16), query * only)
            gv += dot_tn((probs * live).astype(BF16), go * only)
        gqkv_ref[:, pl.ds(128 * pair, 128)] = (gq * SCALE).astype(BF16)
        gqkv_ref[:, pl.ds(HALF + 128 * pair, 128)] = (gk * SCALE).astype(BF16)
        gqkv_ref[:, pl.ds(2 * HALF + 128 * pair, 128)] = gv.astype(BF16)
    grad_x = dot_nt(gqkv_ref[...], w_ref[...])
    own_x_ref[...] = grad_x[:OWN]
    far_x_ref[...] = grad_x[OWN:]


def weights_kernel(
    place_ref, x_ref, a_ref, gqkv_ref, own_o_ref, far_o_ref, gh_low_ref, own_x_ref, far_x_ref, gh_ref, gain_ref,
    mid_ref, down_b_ref, up_cols_ref,
    message_ref, out_ref,
    rows_ref,
):
    core = place_ref[0]
    here = pl.multiple_of(core * HALF, 128)
    there = pl.multiple_of((1 - core) * HALF, 128)
    grad = own_x_ref[...] + far_x_ref[...]
    unit, scale = normalised(x_ref[:OWN].astype(F32))
    out_ref[...] = (gh_ref[...] + norm_back(grad, unit, scale, gain_ref[...])).astype(BF16)
    gqkv = gqkv_ref[...]
    sums = total(gqkv)
    rows_ref[...] = jnp.zeros((128, WIDTH), F32)
    rows_ref[0:1, :] = total(grad * unit)
    rows_ref[1:2, :] = total(grad)
    rows_ref[2:3, pl.ds(here, HALF)] = sums[:, :HALF]
    rows_ref[3:4, pl.ds(here, HALF)] = sums[:, 2 * HALF :]
    rows_ref[4:7, :] = mid_ref[...]
    rows_ref[7:8, :] = down_b_ref[...]
    full = rows_ref[0:8, :]
    high = full.astype(BF16).astype(F32)
    rows_ref[0:8, :] = high
    rows_ref[16:24, :] = full - high
    message_ref[:, pl.ds(QKV, SMALL)] = (rows_ref[...].T + up_cols_ref[...]).astype(BF16)
    message_ref[:, pl.ds(0, QKV)] = dot_tn(a_ref[...], gqkv).astype(BF16)
    low_here = gh_low_ref[:, pl.ds(here, HALF)]
    outs = pl.ds(QKV + SMALL, HALF)
    message_ref[pl.ds(here, HALF), outs] = dot_tn(own_o_ref[...], low_here).astype(BF16)
    message_ref[pl.ds(there, HALF), outs] = dot_tn(swap_halves(far_o_ref[...]), low_here).astype(BF16)


def call(kernel, core, args, outs, scratch=()):
    specs = [pl.BlockSpec(memory_space=pltpu.VMEM)] * len(args)
    if core is not None:
        args = (core,) + tuple(args)
        specs = [pl.BlockSpec(memory_space=pltpu.SMEM)] + specs
    return pl.pallas_call(
        kernel,
        out_shape=tuple(jax.ShapeDtypeStruct(s, d) for s, d in outs),
        in_specs=specs,
        out_specs=tuple(pl.BlockSpec(memory_space=pltpu.VMEM) for _ in outs),
        scratch_shapes=[pltpu.VMEM(s, d) for s, d in scratch],
        compiler_params=pltpu.CompilerParams(vmem_limit_bytes=VMEM_LIMIT),
    )(*args)


def between_cores(values):
    return lax.ppermute(values, "c", [(0, 1), (1, 0)])


def between_chips(values):
    return lax.ppermute(values, "yl", [(0, 1), (1, 0)])


def swap_items(values):
    return lax.ppermute(values, ("c", "yl"), [(0, 0), (1, 2), (2, 1), (3, 3)])


HALVES = [
    (64 * c + 16 * (2 * yh + yl) + 4 * z + x, (((x * 2 + yh) * 4 + z) * 2 + c) * 2 + yl)
    for x in range(4)
    for yh in range(2)
    for z in range(4)
    for c in range(2)
    for yl in range(2)
]


def halves_out(values):
    return lax.ppermute(values, AXES, HALVES)


def halves_back(values):
    return lax.ppermute(values, AXES, [(b, a) for a, b in HALVES])


def ring(values, axis, by):
    return lax.ppermute(values, axis, [(i, (i + by) % 4) for i in range(4)])


def ring_gather(block, axis):
    return [block, ring(block, axis, -1), ring(block, axis, 2), ring(block, axis, 1)]


def ring_order(blocks, at):
    return jnp.concatenate([lax.select_n(lax.rem(j - at + 4, 4), *blocks) for j in range(4)], axis=0)


def ring_reduce(blocks, axis):
    got = [ring(blocks[1], axis, 1), ring(blocks[2], axis, 2), ring(blocks[3], axis, -1)]
    return sum((g.astype(F32) for g in got), blocks[0].astype(F32))


def ring_split(values, at):
    rows = values.shape[0] // 4
    return [lax.dynamic_slice_in_dim(values, lax.rem(at + j, 4) * rows, rows, 0) for j in range(4)]


def gather(block):
    spread = jnp.broadcast_to(block[None], (QUADS,) + block.shape)
    got = lax.all_to_all(spread, QUAD_AXES, 0, 0, tiled=True)
    return got.reshape(QUADS * block.shape[0], block.shape[1])


def reduce(grads):
    rows = grads.shape[0] // QUADS
    got = lax.all_to_all(grads.reshape(QUADS, rows, grads.shape[1]), QUAD_AXES, 0, 0, tiled=True)
    return jnp.sum(got.astype(F32), axis=0)


def by_place(place, first, second, axis=0):
    return jnp.where(
        place == 0, jnp.concatenate([first, second], axis), jnp.concatenate([second, first], axis)
    )


def other_half(values, place):
    rows = values.shape[0] // 2
    return (
        lax.dynamic_slice_in_dim(values, (1 - place) * rows, rows, 0),
        lax.dynamic_slice_in_dim(values, place * rows, rows, 0),
    )


def shards(
    tokens,
    segment_counts,
    ln1_gain,
    ln1_bias,
    w_qkv,
    q_bias,
    v_bias,
    w_out,
    out_bias,
    ln2_gain,
    ln2_bias,
    w_up,
    up_bias,
    w_down,
    down_bias,
    cotangent,
):
    core = lax.axis_index("c")
    side = lax.axis_index("yl")
    x_at, z_at, pair_at = lax.axis_index("x"), lax.axis_index("z"), lax.axis_index("yh")
    y_at = lax.axis_index(RING_Y)
    place = jnp.stack([core, x_at, y_at]).astype(jnp.int32)
    present = jnp.arange(SLOTS) < segment_counts[0]
    present_rows = jnp.repeat(present, HALFSEG)[:, None]
    cot = jnp.where(present_rows, cotangent.reshape(OWN, WIDTH), 0).astype(BF16)
    mine = swap_items(jnp.concatenate([tokens.reshape(OWN, WIDTH), cot], axis=1))
    item = jnp.concatenate([mine, between_cores(mine)], axis=0)
    x, g = item[:, :WIDTH], item[:, WIDTH:]

    small = jnp.stack([ln1_gain, ln1_bias, q_bias, v_bias, out_bias, ln2_gain, ln2_bias, down_bias], axis=1)
    small = jnp.concatenate([small, up_bias.reshape(6, 4), jnp.zeros((6, SMALL - 12), BF16)], axis=1)

    def half_of(t):
        parts = [w_qkv[:, j * WIDTH + t * HALF : j * WIDTH + (t + 1) * HALF] for j in range(3)]
        parts += [small, w_out[:, t * HALF : (t + 1) * HALF], w_up[:, t * UP : (t + 1) * UP]]
        return jnp.concatenate(parts, axis=1)

    first, second = half_of(0), half_of(1)
    rows = lax.all_to_all(jnp.stack([first, first, second, second]), ("c", "yl"), 0, 0, tiled=True)
    rows = rows.reshape(24, ATTN + UP)

    attn = gather(rows[:, :ATTN])
    ups = ring_order(ring_gather(rows[:, ATTN:], "z"), z_at)
    ups = by_place(pair_at, ups, lax.ppermute(ups, "yh", [(0, 1), (1, 0)]))
    ups = ring_gather(ups, "x")
    downs = ring_order(ring_gather(halves_out(w_down), "x"), x_at)
    downs = ring_order(ring_gather(downs, "z"), z_at)
    downs = ring_gather(downs, RING_Y)

    w_in = attn[:, :QKV]
    small_all = attn[:, QKV : QKV + SMALL]
    own_out = attn[:, QKV + SMALL :]
    far_out = between_cores(own_out)
    vectors = small_all[:, :12].T.astype(F32)
    at = core * HALF
    query_b = lax.dynamic_slice(vectors[2:3], (0, at), (1, HALF))
    value_b = lax.dynamic_slice(vectors[3:4], (0, at), (1, HALF))
    qkv_b = jnp.concatenate([query_b, jnp.zeros_like(query_b), value_b], axis=1)
    up_b = lax.dynamic_slice(small_all, (at, 8), (HALF, 4)).reshape(1, UP).astype(F32)
    mid_vec = jnp.concatenate([vectors[4:8], jnp.zeros((4, WIDTH), F32)], axis=0)

    a1, qkv, own_o, lse = call(
        attend_kernel,
        place,
        (x, vectors[0:1], vectors[1:2], w_in, qkv_b),
        (((ROWS, WIDTH), BF16), ((ROWS, QKV), BF16), ((ROWS, HALF), BF16), ((ROWS, 128), F32)),
    )
    far_o = between_cores(own_o)
    hidden, m_own, m_far, grad_a_own, grad_up_b, grad_down_b, *grads = call(
        mlp_kernel,
        place,
        (x, own_o, far_o, own_out, far_out, mid_vec, up_b, g, *ups, *downs),
        (
            ((ROWS, WIDTH), F32),
            ((OWN, WIDTH), F32),
            ((OWN, WIDTH), F32),
            ((ROWS, WIDTH), F32),
            ((1, UP), F32),
            ((1, WIDTH), F32),
        )
        + (((UP_ROWS, UP), BF16),) * 4
        + (((DOWN_ROWS, WIDTH), BF16),) * 4,
        (((WIDTH, UP), BF16), ((UP, WIDTH), BF16), ((WIDTH, UP), BF16), ((UP, WIDTH), BF16)),
    )
    grad_a_far = between_cores(grad_a_own)
    block = swap_items((m_own + between_cores(m_far)).astype(BF16))
    block_out = jnp.where(present_rows, block, 0).reshape(tokens.shape)
    up_cols = lax.dynamic_update_slice(jnp.zeros((WIDTH, 4), F32), grad_up_b.reshape(HALF, 4), (at, 0))
    up_high = up_cols.astype(BF16).astype(F32)
    up_cols = jnp.pad(up_high, ((0, 0), (8, SMALL - 12))) + jnp.pad(up_cols - up_high, ((0, 0), (24, SMALL - 28)))

    gqkv, gh_low, own_x, far_x, gh, vec_mid = call(
        back_kernel,
        place,
        (hidden, g, grad_a_own, grad_a_far, mid_vec, own_out, far_out, qkv, lse, w_in),
        (
            ((ROWS, QKV), BF16),
            ((ROWS, WIDTH), BF16),
            ((OWN, WIDTH), F32),
            ((OWN, WIDTH), F32),
            ((OWN, WIDTH), F32),
            ((3, WIDTH), F32),
        ),
        (((ROWS, HALF), BF16),),
    )
    message, grad_x = call(
        weights_kernel,
        place,
        (
            x, a1, gqkv, own_o, far_o, gh_low, own_x, between_cores(far_x), gh, vectors[0:1], vec_mid, grad_down_b,
            up_cols,
        ),
        (((WIDTH, ATTN), BF16), ((OWN, WIDTH), BF16)),
        (((128, WIDTH), F32),),
    )
    grad_tokens = swap_items(grad_x).reshape(tokens.shape)

    up_sum = ring_reduce(grads[:4], "x").astype(BF16)
    far_up, near_up = other_half(up_sum, pair_at)
    up_sum = near_up.astype(F32) + lax.ppermute(far_up, "yh", [(0, 1), (1, 0)]).astype(F32)
    up_sum = ring_reduce(ring_split(up_sum.astype(BF16), z_at), "z")
    up_sum = jnp.swapaxes(up_sum.reshape(2, 2, 6, UP), 0, 1)
    far_up, near_up = other_half(up_sum, side)
    far_up, near_up = other_half(near_up[0] + between_chips(far_up)[0], core)
    out_up = by_place(core, near_up[0], between_cores(far_up)[0], axis=1)

    down_sum = ring_reduce(grads[4:], RING_Y).astype(BF16)
    down_sum = ring_reduce(ring_split(down_sum, z_at), "z").astype(BF16)
    down_sum = ring_reduce(ring_split(down_sum, x_at), "x")
    out_down = halves_back(down_sum)

    got = lax.all_to_all(reduce(message).reshape(4, 6, ATTN), ("c", "yl"), 0, 0, tiled=True)
    both = got[0::2] + got[1::2]
    out_qkv = jnp.concatenate(
        [both[t, :, j * HALF : (j + 1) * HALF] for j in range(3) for t in range(2)], axis=1
    )
    vec = both[0, :, QKV : QKV + SMALL] + both[1, :, QKV : QKV + SMALL]
    vec = vec[:, :12] + vec[:, 16:28]
    out_out = jnp.concatenate([both[t, :, QKV + SMALL :] for t in range(2)], axis=1)
    return (
        block_out,
        grad_tokens,
        vec[:, 0],
        vec[:, 1],
        out_qkv,
        vec[:, 2],
        vec[:, 3],
        out_out,
        vec[:, 4],
        vec[:, 5],
        vec[:, 6],
        out_up,
        vec[:, 8:12].reshape(24),
        out_down,
        vec[:, 7],
    )


def solution(mesh):
    torus = Mesh(np.asarray(mesh.devices).reshape(SIZES), AXES)
    items = P(("x", "yh", "z", "c"), None, "yl", None)
    part, rows = P(AXES), P(AXES, None)
    return jax.shard_map(
        shards,
        mesh=torus,
        in_specs=(
            items, P(("x", "yh", "z", "c")), part, part, rows, part, part, rows, part, part, part, rows, part, rows,
            part, items,
        ),
        out_specs=(
            items, items, part, part, rows, part, part, rows, part, part, part, rows, part, rows, part,
        ),
        check_vma=False,
    )
```

```python
import jax
import jax.numpy as jnp
import numpy as np
from jax import lax
from jax.experimental import pallas as pl
from jax.experimental.pallas import tpu as pltpu
from jax.sharding import Mesh
from jax.sharding import PartitionSpec as P

WIDTH = 768
HEAD = 64
NSUM = 16
SLOTS = 4
SEGLEN = 64
HALFSEG = 32
FF = 3072

EPSILON = 1e-05
MASKED = -1e30
SCALE = HEAD ** (-0.5)

AXES = ("x", "yh", "z", "c", "yl")
SIZES = (4, 2, 4, 2, 2)
QUAD_AXES = ("x", "yh", "z")
QUADS = 32
DEVICES = 128
ROWS = 256
OWN = 128
HALF = WIDTH // 2
QKV = 3 * HALF
UP = FF // 2
SMALL = 128
ATTN = QKV + SMALL + HALF
BLOCK = WIDTH // 4
DOWN_ROWS = UP // 4
RING_Y = ("yh", "yl")
VMEM_LIMIT = 60 * 1024 * 1024

F32 = jnp.float32
BF16 = jnp.bfloat16


def dot_nn(left, right):
    return jnp.dot(left, right, preferred_element_type=F32)


def dot_tn(left, right):
    return lax.dot_general(left, right, (((0,), (0,)), ((), ())), preferred_element_type=F32)


def dot_nt(left, right):
    return lax.dot_general(left, right, (((1,), (1,)), ((), ())), preferred_element_type=F32)


def normalised(values):
    center = values - jnp.mean(values, axis=-1, keepdims=True)
    spread = jnp.mean(center * center, axis=-1, keepdims=True)
    scale = lax.rsqrt(spread + EPSILON)
    return center * scale, scale


def norm_back(grad, unit, scale, gain):
    inner = grad * gain
    mean = jnp.mean(inner, axis=-1, keepdims=True)
    along = jnp.mean(inner * unit, axis=-1, keepdims=True)
    return scale * (inner - mean - unit * along)


def total(values):
    return jnp.sum(values.astype(F32), axis=0, keepdims=True)


def swap_halves(values):
    return jnp.concatenate([values[OWN:], values[:OWN]], axis=0)


def masks(core):
    def place(dim):
        row = lax.broadcasted_iota(jnp.int32, (ROWS, ROWS), dim)
        second = (row >= OWN).astype(jnp.int32)
        inner = row - second * OWN
        half = core + second - 2 * core * second
        slot = inner // HALFSEG
        return slot, half * HALFSEG + inner - slot * HALFSEG

    query_slot, query_pos = place(0)
    key_slot, key_pos = place(1)
    same = (query_slot == key_slot) & (key_pos <= query_pos)
    earlier = (key_slot < query_slot) & (key_pos >= SEGLEN - NSUM)
    return same | earlier, key_slot >= query_slot - 2


def positions(core, at):
    way = 1 - 2 * core
    return at, lax.rem(at + 4 - way, 4), lax.rem(at + 4 + way, 4), lax.rem(at + 2, 4)


def head_lanes(j):
    lane = lax.broadcasted_iota(jnp.int32, (1, 2 * HEAD), 1)
    return jnp.where(lane // HEAD == j, 1.0, 0.0).astype(BF16)


def halves_kernel(place_ref, qkv_ref, small_ref, out_ref, up_ref, near_ref, far_ref):
    core = place_ref[0]
    for ref, side in ((near_ref, core), (far_ref, 1 - core)):
        for j in range(3):
            ref[:, pl.ds(j * HALF, HALF)] = qkv_ref[:, pl.ds(pl.multiple_of(j * WIDTH + side * HALF, 128), HALF)]
        ref[:, pl.ds(QKV, SMALL)] = small_ref[...]
        ref[:, pl.ds(QKV + SMALL, HALF)] = out_ref[:, pl.ds(pl.multiple_of(side * HALF, 128), HALF)]
        ref[:, pl.ds(ATTN, UP)] = up_ref[:, pl.ds(pl.multiple_of(side * UP, 128), UP)]


def attend_kernel(
    place_ref, x_ref, part_0, part_1, part_2, part_3,
    a_ref, qkv_ref, o_ref, lse_ref, w_ref, out_ref, small_ref, vec_ref,
):
    core = place_ref[0]
    for part, at in zip((part_0, part_1, part_2, part_3), positions(core, place_ref[1])):
        rows = pl.ds(pl.multiple_of(at * BLOCK, 64), BLOCK)
        w_ref[rows, :] = part[:, pl.ds(0, QKV)]
        small_ref[rows, :] = part[:, pl.ds(QKV, SMALL)]
        out_ref[rows, :] = part[:, pl.ds(QKV + SMALL, HALF)]
    vec_ref[...] = small_ref[...].astype(F32).T[:16]
    unit, _ = normalised(x_ref[...].astype(F32))
    a = (unit * vec_ref[0:1, :] + vec_ref[1:2, :]).astype(BF16)
    a_ref[...] = a
    here = pl.ds(pl.multiple_of(core * HALF, 128), HALF)
    shift = jnp.concatenate([vec_ref[2:3, here], jnp.zeros((1, HALF), F32), vec_ref[3:4, here]], axis=1)
    qkv_ref[...] = (dot_nn(a, w_ref[...]) + shift).astype(BF16)
    admitted, _ = masks(core)
    lane = lax.broadcasted_iota(jnp.int32, (ROWS, 128), 1)
    kept = jnp.zeros((ROWS, 128), F32)
    for pair in range(3):
        lanes = pl.ds(128 * pair, 128)
        query = qkv_ref[:, lanes]
        key = qkv_ref[:, pl.ds(HALF + 128 * pair, 128)]
        value = qkv_ref[:, pl.ds(2 * HALF + 128 * pair, 128)]
        out = jnp.zeros((ROWS, 128), F32)
        for j in range(2):
            only = head_lanes(j)
            scores = jnp.where(admitted, dot_nt(query * only, key) * SCALE, MASKED)
            top = jnp.max(scores, axis=-1, keepdims=True)
            grown = jnp.exp(scores - top)
            amount = jnp.sum(grown, axis=-1, keepdims=True)
            kept = jnp.where(lane == 2 * pair + j, top + jnp.log(amount), kept)
            probs = (grown * (1.0 / amount)).astype(BF16)
            out += dot_nn(probs, value * only)
        o_ref[:, lanes] = out.astype(BF16)
    lse_ref[...] = kept


def mlp_kernel(
    place_ref, x_ref, own_o_ref, far_o_ref, own_out_ref, far_out_ref, vec_ref, up_b_ref, g_ref, order_ref,
    up_0, up_1, up_2, up_3, down_0, down_1, down_2, down_3,
    h_ref, m_own_ref, m_far_ref, grad_a_ref, grad_up_b_ref, grad_down_b_ref,
    gup_0, gup_1, gup_2, gup_3, gdown_0, gdown_1, gdown_2, gdown_3,
    up_ref, down_ref, grad_up_ref, grad_down_ref,
):
    core = place_ref[0]
    up_at, down_at = positions(core, place_ref[3]), positions(core, place_ref[2])
    for up, at in zip((up_0, up_1, up_2, up_3), up_at):
        up_ref[pl.ds(pl.multiple_of(at * BLOCK, 64), BLOCK), :] = up[...]
    for down, at in zip((down_0, down_1, down_2, down_3), down_at):
        down_ref[pl.ds(pl.multiple_of(at * DOWN_ROWS, 128), DOWN_ROWS), :] = down[...]
    here = pl.multiple_of(core * HALF, 128)
    there = pl.multiple_of((1 - core) * HALF, 128)
    own_o = own_o_ref[...]
    far_o = swap_halves(far_o_ref[...])
    for out_ref, at in ((own_out_ref, here), (far_out_ref, there)):
        part = dot_nn(own_o, out_ref[pl.ds(here, HALF), :]) + dot_nn(far_o, out_ref[pl.ds(there, HALF), :])
        h_ref[:, pl.ds(at, HALF)] = part
    hidden = x_ref[...].astype(F32) + (h_ref[...] + vec_ref[4:5, :])
    h_ref[...] = hidden
    unit, _ = normalised(hidden)
    a = (unit * vec_ref[5:6, :] + vec_ref[6:7, :]).astype(BF16)
    a = dot_nn(a, order_ref[...]).astype(BF16)
    g = g_ref[...]
    branch = jnp.zeros((ROWS, WIDTH), F32)
    grad_a = jnp.zeros((ROWS, WIDTH), F32)
    step = 512
    for i in range(UP // step):
        cols = pl.ds(i * step, step)
        up = up_ref[:, cols]
        down = down_ref[cols, :]
        u = dot_nn(a, up) + up_b_ref[:, cols]
        phi = 0.5 * (1.0 + lax.erf(u * (0.5**0.5)))
        z = (u * phi).astype(BF16)
        slope = phi + u * (jnp.exp(-0.5 * u * u) * (2.0 * jnp.pi) ** (-0.5))
        branch += dot_nn(z, down)
        gu = (dot_nt(g, down) * slope).astype(BF16)
        grad_down_ref[cols, :] = dot_tn(z, g).astype(BF16)
        grad_up_ref[:, cols] = dot_tn(a, gu).astype(BF16)
        grad_up_b_ref[:, cols] = total(gu)
        grad_a += dot_nt(gu, up)
    m_own_ref[...] = branch[:OWN] + hidden[:OWN] + vec_ref[7:8, :]
    m_far_ref[...] = branch[OWN:]
    high = grad_a.astype(BF16)
    low = (grad_a - high.astype(F32)).astype(BF16)
    grad_a_ref[...] = dot_nt(high, order_ref[...]) + dot_nt(low, order_ref[...])
    grad_down_b_ref[...] = total(g[:OWN])
    for gup, at in zip((gup_0, gup_1, gup_2, gup_3), up_at):
        gup[...] = grad_up_ref[pl.ds(pl.multiple_of(at * BLOCK, 64), BLOCK), :]
    for gdown, at in zip((gdown_0, gdown_1, gdown_2, gdown_3), down_at):
        gdown[...] = grad_down_ref[pl.ds(pl.multiple_of(at * DOWN_ROWS, 128), DOWN_ROWS), :]


def back_kernel(
    place_ref, h_ref, g_ref, own_grad_ref, far_grad_ref, vec_ref, own_out_ref, far_out_ref, qkv_ref, lse_ref, w_ref,
    gqkv_ref, gh_low_ref, own_x_ref, far_x_ref, gh_ref, vec_out_ref,
    go_ref,
):
    core = place_ref[0]
    here = pl.multiple_of(core * HALF, 128)
    there = pl.multiple_of((1 - core) * HALF, 128)
    grad_a = own_grad_ref[...] + swap_halves(far_grad_ref[...])
    unit, scale = normalised(h_ref[...])
    grad_h = g_ref[...].astype(F32) + norm_back(grad_a, unit, scale, vec_ref[5:6, :])
    gh_ref[...] = grad_h[:OWN]
    low = grad_h.astype(BF16)
    gh_low_ref[...] = low
    vec_out_ref[0:1, :] = total(low[:OWN])
    vec_out_ref[1:2, :] = total(grad_a[:OWN] * unit[:OWN])
    vec_out_ref[2:3, :] = total(grad_a[:OWN])
    low_here = gh_low_ref[:, pl.ds(here, HALF)]
    low_there = gh_low_ref[:, pl.ds(there, HALF)]
    rows = pl.ds(here, HALF)
    go_ref[...] = (dot_nt(low_here, own_out_ref[rows, :]) + dot_nt(low_there, far_out_ref[rows, :])).astype(BF16)
    admitted, live = masks(core)
    live = jnp.where(live, 1.0, 0.0)
    lane = lax.broadcasted_iota(jnp.int32, (ROWS, 128), 1)
    for pair in range(3):
        query = qkv_ref[:, pl.ds(128 * pair, 128)]
        key = qkv_ref[:, pl.ds(HALF + 128 * pair, 128)]
        value = qkv_ref[:, pl.ds(2 * HALF + 128 * pair, 128)]
        go = go_ref[:, pl.ds(128 * pair, 128)]
        gq = jnp.zeros((ROWS, 128), F32)
        gk = jnp.zeros((ROWS, 128), F32)
        gv = jnp.zeros((ROWS, 128), F32)
        for j in range(2):
            only = head_lanes(j)
            lse = jnp.sum(jnp.where(lane == 2 * pair + j, lse_ref[...], 0.0), axis=-1, keepdims=True)
            scores = jnp.where(admitted, dot_nt(query * only, key) * SCALE, MASKED)
            probs = jnp.exp(scores - lse)
            grad_p = dot_nt(go * only, value)
            grad_s = probs * (grad_p - jnp.sum(probs * grad_p, axis=-1, keepdims=True))
            gq += dot_nn(grad_s.astype(BF16), key * only)
            gk += dot_tn((grad_s * live).astype(BF16), query * only)
            gv += dot_tn((probs * live).astype(BF16), go * only)
        gqkv_ref[:, pl.ds(128 * pair, 128)] = (gq * SCALE).astype(BF16)
        gqkv_ref[:, pl.ds(HALF + 128 * pair, 128)] = (gk * SCALE).astype(BF16)
        gqkv_ref[:, pl.ds(2 * HALF + 128 * pair, 128)] = gv.astype(BF16)
    grad_x = dot_nt(gqkv_ref[...], w_ref[...])
    own_x_ref[...] = grad_x[:OWN]
    far_x_ref[...] = grad_x[OWN:]


def weights_kernel(
    place_ref, x_ref, a_ref, gqkv_ref, own_o_ref, far_o_ref, gh_low_ref, own_x_ref, far_x_ref, gh_ref, vec_ref,
    mid_ref, down_b_ref, up_cols_ref,
    message_ref, out_ref,
    rows_ref,
):
    core = place_ref[0]
    here = pl.multiple_of(core * HALF, 128)
    there = pl.multiple_of((1 - core) * HALF, 128)
    grad = own_x_ref[...] + far_x_ref[...]
    unit, scale = normalised(x_ref[:OWN].astype(F32))
    out_ref[...] = (gh_ref[...] + norm_back(grad, unit, scale, vec_ref[0:1, :])).astype(BF16)
    gqkv = gqkv_ref[...]
    sums = total(gqkv)
    rows_ref[...] = jnp.zeros((128, WIDTH), F32)
    rows_ref[0:1, :] = total(grad * unit)
    rows_ref[1:2, :] = total(grad)
    rows_ref[2:3, pl.ds(here, HALF)] = sums[:, :HALF]
    rows_ref[3:4, pl.ds(here, HALF)] = sums[:, 2 * HALF :]
    rows_ref[4:7, :] = mid_ref[...]
    rows_ref[7:8, :] = down_b_ref[...]
    full = rows_ref[0:8, :]
    high = full.astype(BF16).astype(F32)
    rows_ref[0:8, :] = high
    rows_ref[16:24, :] = full - high
    message_ref[:, pl.ds(QKV, SMALL)] = (rows_ref[...].T + up_cols_ref[...]).astype(BF16)
    message_ref[:, pl.ds(0, QKV)] = dot_tn(a_ref[...], gqkv).astype(BF16)
    low_here = gh_low_ref[:, pl.ds(here, HALF)]
    outs = pl.ds(QKV + SMALL, HALF)
    message_ref[pl.ds(here, HALF), outs] = dot_tn(own_o_ref[...], low_here).astype(BF16)
    message_ref[pl.ds(there, HALF), outs] = dot_tn(swap_halves(far_o_ref[...]), low_here).astype(BF16)


def call(kernel, core, args, outs, scratch=()):
    specs = [pl.BlockSpec(memory_space=pltpu.VMEM)] * len(args)
    if core is not None:
        args = (core,) + tuple(args)
        specs = [pl.BlockSpec(memory_space=pltpu.SMEM)] + specs
    return pl.pallas_call(
        kernel,
        out_shape=tuple(jax.ShapeDtypeStruct(s, d) for s, d in outs),
        in_specs=specs,
        out_specs=tuple(pl.BlockSpec(memory_space=pltpu.VMEM) for _ in outs),
        scratch_shapes=[pltpu.VMEM(s, d) for s, d in scratch],
        compiler_params=pltpu.CompilerParams(vmem_limit_bytes=VMEM_LIMIT),
    )(*args)


def between_cores(values):
    return lax.ppermute(values, "c", [(0, 1), (1, 0)])


def between_chips(values):
    return lax.ppermute(values, "yl", [(0, 1), (1, 0)])


def swap_items(values):
    return lax.ppermute(values, ("c", "yl"), [(0, 0), (1, 2), (2, 1), (3, 3)])


HALVES = [
    (64 * c + 16 * (2 * yh + yl) + 4 * z + x, (((x * 2 + yh) * 4 + z) * 2 + c) * 2 + yl)
    for x in range(4)
    for yh in range(2)
    for z in range(4)
    for c in range(2)
    for yl in range(2)
]


def up_order():
    order = np.zeros((WIDTH, WIDTH), np.float32)
    for x, yh, z, i in np.ndindex(4, 2, 4, 24):
        order[((x * 2 + yh) * 4 + z) * 24 + i, z * BLOCK + x * 48 + yh * 24 + i] = 1.0
    return order


UP_ORDER = up_order()


def halves_out(values):
    return lax.ppermute(values, AXES, HALVES)


def halves_back(values):
    return lax.ppermute(values, AXES, [(b, a) for a, b in HALVES])


def ring(values, axis, by):
    return lax.ppermute(values, axis, [(i, (i + by) % 4) for i in range(4)])


def ring_gather(block, axis):
    return [block, ring(block, axis, -1), ring(block, axis, 2), ring(block, axis, 1)]


def ring_order(blocks, at):
    return [lax.select_n(lax.rem(j - at + 4, 4), *blocks) for j in range(4)]


def ring_reduce(blocks, axis):
    got = [ring(blocks[1], axis, 1), ring(blocks[2], axis, 2), ring(blocks[3], axis, -1)]
    return sum((g.astype(F32) for g in got), blocks[0].astype(F32))


def ring_split(values, at):
    rows = values.shape[0] // 4
    return [lax.dynamic_slice_in_dim(values, lax.rem(at + j, 4) * rows, rows, 0) for j in range(4)]


def along(axis, by):
    pairs = []
    for x, yh, z, c, yl in np.ndindex(*SIZES):
        at = {"x": x, "y": 2 * yh + yl, "z": z}
        at[axis] = (at[axis] + (by if c == 0 else -by)) % 4
        to = (at["x"], at["y"] // 2, at["z"], c, at["y"] % 2)
        pairs.append((int(np.ravel_multi_index((x, yh, z, c, yl), SIZES)), int(np.ravel_multi_index(to, SIZES))))
    return pairs


def send(values, axis, by):
    return lax.ppermute(values, AXES, along(axis, by))


def relay_gather(block, axis):
    behind = send(block, axis, 1)
    return [block, behind, send(block, axis, -1), send(behind, axis, 1)]


def relay_start(blocks, axis):
    return send(blocks[3], axis, 1), send(blocks[1], axis, -1)


def relay_end(blocks, got, axis):
    ahead = (blocks[2].astype(F32) + got[0].astype(F32)).astype(BF16)
    return blocks[0].astype(F32) + got[1].astype(F32) + send(ahead, axis, 1).astype(F32)


def gather(block):
    spread = jnp.broadcast_to(block[None], (QUADS,) + block.shape)
    got = lax.all_to_all(spread, QUAD_AXES, 0, 0, tiled=True)
    return got.reshape(QUADS * block.shape[0], block.shape[1])


def reduce(grads):
    rows = grads.shape[0] // QUADS
    got = lax.all_to_all(grads.reshape(QUADS, rows, grads.shape[1]), QUAD_AXES, 0, 0, tiled=True)
    return jnp.sum(got.astype(F32), axis=0)


def by_place(place, first, second, axis=0):
    return jnp.where(
        place == 0, jnp.concatenate([first, second], axis), jnp.concatenate([second, first], axis)
    )


def other_half(values, place):
    rows = values.shape[0] // 2
    return (
        lax.dynamic_slice_in_dim(values, (1 - place) * rows, rows, 0),
        lax.dynamic_slice_in_dim(values, place * rows, rows, 0),
    )


def shards(
    tokens,
    segment_counts,
    ln1_gain,
    ln1_bias,
    w_qkv,
    q_bias,
    v_bias,
    w_out,
    out_bias,
    ln2_gain,
    ln2_bias,
    w_up,
    up_bias,
    w_down,
    down_bias,
    cotangent,
):
    core = lax.axis_index("c")
    x_at, z_at = lax.axis_index("x"), lax.axis_index("z")
    y_at = lax.axis_index(RING_Y)
    place = jnp.stack([core, x_at, y_at, z_at]).astype(jnp.int32)
    present = jnp.arange(SLOTS) < segment_counts[0]
    present_rows = jnp.repeat(present, HALFSEG)[:, None]
    cot = jnp.where(present_rows, cotangent.reshape(OWN, WIDTH), 0).astype(BF16)

    small = jnp.stack([ln1_gain, ln1_bias, q_bias, v_bias, out_bias, ln2_gain, ln2_bias, down_bias], axis=1)
    small = jnp.concatenate([small, up_bias.reshape(6, 4), jnp.zeros((6, SMALL - 12), BF16)], axis=1)
    near, far = call(
        halves_kernel, place, (w_qkv, small, w_out, w_up), (((6, ATTN + UP), BF16), ((6, ATTN + UP), BF16))
    )
    rows = by_place(core, near, between_cores(far))
    downs = halves_out(w_down)
    mine = swap_items(jnp.concatenate([tokens.reshape(OWN, WIDTH), cot], axis=1))

    rows = ring_gather(rows, RING_Y)
    downs = ring_gather(downs, "x")
    rows = jnp.stack(ring_order(rows, y_at)).reshape(2, 2, 2, 6, ATTN + UP)
    rows = jnp.swapaxes(rows, 1, 2).reshape(2, 24, ATTN + UP)
    attn, ups = rows[:, :, :ATTN], rows[:, :, ATTN:].reshape(48, UP)
    downs = jnp.concatenate(ring_order(downs, x_at), axis=0)

    attn = ring_gather(attn, "z")
    ups = ring_gather(ups, "x")
    downs = ring_gather(downs, "z")
    item = jnp.concatenate([mine, between_cores(mine)], axis=0)
    x, g = item[:, :WIDTH], item[:, WIDTH:]
    attn = jnp.concatenate(ring_order(attn, z_at), axis=1).reshape(BLOCK, ATTN)
    ups = jnp.concatenate(ring_order(ups, x_at), axis=0)
    downs = jnp.concatenate(ring_order(downs, z_at), axis=0)

    attn = relay_gather(attn, "x")
    ups = relay_gather(ups, "z")
    downs = relay_gather(downs, "y")

    a1, qkv, own_o, lse, w_in, own_out, small_all, vectors = call(
        attend_kernel,
        place,
        (x, *attn),
        (
            ((ROWS, WIDTH), BF16),
            ((ROWS, QKV), BF16),
            ((ROWS, HALF), BF16),
            ((ROWS, 128), F32),
            ((WIDTH, QKV), BF16),
            ((WIDTH, HALF), BF16),
            ((WIDTH, SMALL), BF16),
            ((16, WIDTH), F32),
        ),
    )
    far_o, far_out = between_cores(own_o), between_cores(own_out)
    at = core * HALF
    up_b = lax.dynamic_slice(small_all, (at, 8), (HALF, 4)).reshape(1, UP).astype(F32)
    hidden, m_own, m_far, grad_a_own, grad_up_b, grad_down_b, *grads = call(
        mlp_kernel,
        place,
        (x, own_o, far_o, own_out, far_out, vectors, up_b, g, jnp.asarray(UP_ORDER, BF16), *ups, *downs),
        (
            ((ROWS, WIDTH), F32),
            ((OWN, WIDTH), F32),
            ((OWN, WIDTH), F32),
            ((ROWS, WIDTH), F32),
            ((1, UP), F32),
            ((1, WIDTH), F32),
        )
        + (((BLOCK, UP), BF16),) * 4
        + (((DOWN_ROWS, WIDTH), BF16),) * 4,
        (((WIDTH, UP), BF16), ((UP, WIDTH), BF16), ((WIDTH, UP), BF16), ((UP, WIDTH), BF16)),
    )
    grad_a_far = between_cores(grad_a_own)
    grad_a_far, *grads = lax.optimization_barrier((grad_a_far, *grads))
    grad_ups, grad_downs = grads[:4], grads[4:]
    got_ups = relay_start(grad_ups, "z")
    got_downs = relay_start(grad_downs, "y")
    block = swap_items((m_own + between_cores(m_far)).astype(BF16))
    block_out = jnp.where(present_rows, block, 0).reshape(tokens.shape)
    up_cols = lax.dynamic_update_slice(jnp.zeros((WIDTH, 4), F32), grad_up_b.reshape(HALF, 4), (at, 0))
    up_high = up_cols.astype(BF16).astype(F32)
    up_cols = jnp.pad(up_high, ((0, 0), (8, SMALL - 12))) + jnp.pad(up_cols - up_high, ((0, 0), (24, SMALL - 28)))

    gqkv, gh_low, own_x, far_x, gh, vec_mid = call(
        back_kernel,
        place,
        (hidden, g, grad_a_own, grad_a_far, vectors, own_out, far_out, qkv, lse, w_in),
        (
            ((ROWS, QKV), BF16),
            ((ROWS, WIDTH), BF16),
            ((OWN, WIDTH), F32),
            ((OWN, WIDTH), F32),
            ((OWN, WIDTH), F32),
            ((3, WIDTH), F32),
        ),
        (((ROWS, HALF), BF16),),
    )
    message, grad_x = call(
        weights_kernel,
        place,
        (
            x, a1, gqkv, own_o, far_o, gh_low, own_x, between_cores(far_x), gh, vectors, vec_mid, grad_down_b, up_cols,
        ),
        (((WIDTH, ATTN), BF16), ((OWN, WIDTH), BF16)),
        (((128, WIDTH), F32),),
    )
    grad_tokens = swap_items(grad_x).reshape(tokens.shape)
    attn_sum = reduce(message)

    up_sum = relay_end(grad_ups, got_ups, "z").astype(BF16)
    up_sum = ring_reduce(ring_split(up_sum, x_at), "x").astype(BF16)
    up_sum = jnp.swapaxes(up_sum.reshape(2, 2, 2, 6, UP), 1, 2).reshape(4, 12, UP)
    up_sum = ring_reduce([u[0] for u in ring_split(up_sum, y_at)], RING_Y)
    far_up, near_up = other_half(up_sum.reshape(2, 6, UP), core)
    out_up = by_place(core, near_up[0], between_cores(far_up[0]), axis=1)

    down_sum = relay_end(grad_downs, got_downs, "y").astype(BF16)
    down_sum = ring_reduce(ring_split(down_sum, z_at), "z").astype(BF16)
    down_sum = ring_reduce(ring_split(down_sum, x_at), "x")
    out_down = halves_back(down_sum)

    got = lax.all_to_all(attn_sum.reshape(4, 6, ATTN), ("c", "yl"), 0, 0, tiled=True)
    both = got[0::2] + got[1::2]
    out_qkv = jnp.concatenate(
        [both[t, :, j * HALF : (j + 1) * HALF] for j in range(3) for t in range(2)], axis=1
    )
    vec = both[0, :, QKV : QKV + SMALL] + both[1, :, QKV : QKV + SMALL]
    vec = vec[:, :12] + vec[:, 16:28]
    out_out = jnp.concatenate([both[t, :, QKV + SMALL :] for t in range(2)], axis=1)
    return (
        block_out,
        grad_tokens,
        vec[:, 0],
        vec[:, 1],
        out_qkv,
        vec[:, 2],
        vec[:, 3],
        out_out,
        vec[:, 4],
        vec[:, 5],
        vec[:, 6],
        out_up,
        vec[:, 8:12].reshape(24),
        out_down,
        vec[:, 7],
    )


def solution(mesh):
    torus = Mesh(np.asarray(mesh.devices).reshape(SIZES), AXES)
    items = P(("x", "yh", "z", "c"), None, "yl", None)
    part, rows = P(AXES), P(AXES, None)
    return jax.shard_map(
        shards,
        mesh=torus,
        in_specs=(
            items, P(("x", "yh", "z", "c")), part, part, rows, part, part, rows, part, part, part, rows, part, rows,
            part, items,
        ),
        out_specs=(
            items, items, part, part, rows, part, part, rows, part, part, part, rows, part, rows, part,
        ),
        check_vma=False,
    )
```

```python
import jax
import jax.numpy as jnp
import numpy as np
from jax import lax
from jax.experimental import pallas as pl
from jax.experimental.pallas import tpu as pltpu
from jax.sharding import Mesh
from jax.sharding import PartitionSpec as P

WIDTH = 768
HEAD = 64
NSUM = 16
SLOTS = 4
SEGLEN = 64
HALFSEG = 32
FF = 3072

EPSILON = 1e-05
MASKED = -1e30
SCALE = HEAD ** (-0.5)

AXES = ("x", "yh", "z", "c", "yl")
SIZES = (4, 2, 4, 2, 2)
QUAD_AXES = ("x", "yh", "z")
QUADS = 32
DEVICES = 128
ROWS = 256
OWN = 128
HALF = WIDTH // 2
QKV = 3 * HALF
UP = FF // 2
SMALL = 128
ATTN = QKV + SMALL + HALF
BLOCK = WIDTH // 4
DOWN_ROWS = UP // 4
RING_Y = ("yh", "yl")
EIGHT = ("yh", "c", "yl")
VMEM_LIMIT = 60 * 1024 * 1024

F32 = jnp.float32
BF16 = jnp.bfloat16


def dot_nn(left, right):
    return jnp.dot(left, right, preferred_element_type=F32)


def dot_tn(left, right):
    return lax.dot_general(left, right, (((0,), (0,)), ((), ())), preferred_element_type=F32)


def dot_nt(left, right):
    return lax.dot_general(left, right, (((1,), (1,)), ((), ())), preferred_element_type=F32)


def normalised(values):
    center = values - jnp.mean(values, axis=-1, keepdims=True)
    spread = jnp.mean(center * center, axis=-1, keepdims=True)
    scale = lax.rsqrt(spread + EPSILON)
    return center * scale, scale


def norm_back(grad, unit, scale, gain):
    inner = grad * gain
    mean = jnp.mean(inner, axis=-1, keepdims=True)
    along = jnp.mean(inner * unit, axis=-1, keepdims=True)
    return scale * (inner - mean - unit * along)


def total(values):
    return jnp.sum(values.astype(F32), axis=0, keepdims=True)


def swap_halves(values):
    return jnp.concatenate([values[OWN:], values[:OWN]], axis=0)


def masks(core):
    def place(dim):
        row = lax.broadcasted_iota(jnp.int32, (ROWS, ROWS), dim)
        second = (row >= OWN).astype(jnp.int32)
        inner = row - second * OWN
        half = core + second - 2 * core * second
        slot = inner // HALFSEG
        return slot, half * HALFSEG + inner - slot * HALFSEG

    query_slot, query_pos = place(0)
    key_slot, key_pos = place(1)
    same = (query_slot == key_slot) & (key_pos <= query_pos)
    earlier = (key_slot < query_slot) & (key_pos >= SEGLEN - NSUM)
    return same | earlier, key_slot >= query_slot - 2


def positions(core, at):
    way = 1 - 2 * core
    return at, lax.rem(at + 4 - way, 4), lax.rem(at + 4 + way, 4), lax.rem(at + 2, 4)


def head_lanes(j):
    lane = lax.broadcasted_iota(jnp.int32, (1, 2 * HEAD), 1)
    return jnp.where(lane // HEAD == j, 1.0, 0.0).astype(BF16)


def up_runs(t):
    for yh, yl, z, x in np.ndindex(2, 2, 4, 4):
        yield 96 * ((x * 2 + yh) * 4 + z) + 48 * t + 24 * yl, 24 * (((yh * 2 + yl) * 4 + z) * 4 + x)


def halves_kernel(qkv_ref, out_ref, up_ref, *refs):
    *vec_refs, up_b_ref, parts_ref, rows_ref, wide_ref, half_ref = refs
    rows_ref[...] = jnp.zeros((16, 128), F32)
    for v, ref in enumerate(vec_refs):
        rows_ref[v : v + 1, 0:6] = ref[...].astype(F32).reshape(1, 6)
    rows_ref[8:9, 0:24] = up_b_ref[...].astype(F32).reshape(1, 24)
    row = lax.broadcasted_iota(jnp.int32, (8, 128), 0)
    lane = lax.broadcasted_iota(jnp.int32, (8, 128), 1)
    src = lax.broadcasted_iota(jnp.int32, (128, 128), 0)
    col = lax.broadcasted_iota(jnp.int32, (128, 128), 1)
    one = jnp.where(row == lane, 1.0, 0.0).astype(BF16)
    vecs = jnp.concatenate([rows_ref[0:8, :].astype(BF16), jnp.zeros((120, 128), BF16)], axis=0)
    up_b = jnp.where(lane // 4 == row, jnp.broadcast_to(rows_ref[8:9, :], (8, 128)), 0.0).astype(BF16)
    put = jnp.where((src < 24) & (8 + lax.rem(src, 4) == col), 1.0, 0.0).astype(BF16)
    small = (dot_nt(one, vecs) + dot_nn(up_b, put)).astype(BF16)
    wide_ref[...] = up_ref[...].astype(F32)
    for t in range(2):
        for src, to in up_runs(t):
            half_ref[:, to : to + 24] = wide_ref[:, src : src + 24]
        up = half_ref[...].astype(BF16)
        for at in (2 * t, 2 * t + 1, 2 * t + 4, 2 * t + 5):
            for j in range(3):
                parts_ref[at, :, j * HALF : (j + 1) * HALF] = qkv_ref[:, j * WIDTH + t * HALF : j * WIDTH + (t + 1) * HALF]
            parts_ref[at, :, QKV : QKV + SMALL] = small[:6]
            parts_ref[at, :, QKV + SMALL : ATTN] = out_ref[:, t * HALF : (t + 1) * HALF]
            parts_ref[at, :, ATTN:] = up


def outputs_kernel(
    got_ref, down_ref, tokens_ref,
    qkv_ref, out_ref, up_ref, out_down_ref, out_tokens_ref, *refs,
):
    *vec_refs, up_b_ref, rows_ref = refs
    out_down_ref[...] = down_ref[...]
    out_tokens_ref[...] = tokens_ref[...]
    small = jnp.zeros((6, SMALL), F32)
    for t in range(2):
        rows = [got_ref[at].astype(F32) for at in (2 * t, 2 * t + 1, 2 * t + 4, 2 * t + 5)]
        rows = (rows[0] + rows[1]) + (rows[2] + rows[3])
        for j in range(3):
            qkv_ref[:, j * WIDTH + t * HALF : j * WIDTH + (t + 1) * HALF] = rows[:, j * HALF : (j + 1) * HALF]
        small += rows[:, QKV : QKV + SMALL]
        out_ref[:, t * HALF : (t + 1) * HALF] = rows[:, QKV + SMALL : ATTN]
        for to, src in up_runs(t):
            up_ref[:, to : to + 24] = rows[:, ATTN + src : ATTN + src + 24]
    small = small[:, 0:12] + small[:, 16:28]
    rows_ref[...] = jnp.zeros((128, 128), F32)
    rows_ref[0:6, 0:12] = small
    flipped = rows_ref[...].T
    for v, ref in enumerate(vec_refs):
        ref[...] = flipped[v : v + 1, 0:6].reshape(6)
    up_b_ref[...] = jnp.concatenate([small[j : j + 1, 8:12] for j in range(6)], axis=1).reshape(24)


def attend_kernel(
    place_ref, x_ref, part_0, part_1, part_2, part_3,
    a_ref, qkv_ref, o_ref, lse_ref, w_ref, out_ref, small_ref, vec_ref,
):
    core = place_ref[0]
    for part, at in zip((part_0, part_1, part_2, part_3), positions(core, place_ref[1])):
        rows = pl.ds(pl.multiple_of(at * BLOCK, 64), BLOCK)
        w_ref[rows, :] = part[:, pl.ds(0, QKV)]
        small_ref[rows, :] = part[:, pl.ds(QKV, SMALL)]
        out_ref[rows, :] = part[:, pl.ds(QKV + SMALL, HALF)]
    vec_ref[...] = small_ref[...].astype(F32).T[:16]
    unit, _ = normalised(x_ref[...].astype(F32))
    a = (unit * vec_ref[0:1, :] + vec_ref[1:2, :]).astype(BF16)
    a_ref[...] = a
    here = pl.ds(pl.multiple_of(core * HALF, 128), HALF)
    shift = jnp.concatenate([vec_ref[2:3, here], jnp.zeros((1, HALF), F32), vec_ref[3:4, here]], axis=1)
    qkv_ref[...] = (dot_nn(a, w_ref[...]) + shift).astype(BF16)
    admitted, _ = masks(core)
    lane = lax.broadcasted_iota(jnp.int32, (ROWS, 128), 1)
    kept = jnp.zeros((ROWS, 128), F32)
    for pair in range(3):
        lanes = pl.ds(128 * pair, 128)
        query = qkv_ref[:, lanes]
        key = qkv_ref[:, pl.ds(HALF + 128 * pair, 128)]
        value = qkv_ref[:, pl.ds(2 * HALF + 128 * pair, 128)]
        out = jnp.zeros((ROWS, 128), F32)
        for j in range(2):
            only = head_lanes(j)
            scores = jnp.where(admitted, dot_nt(query * only, key) * SCALE, MASKED)
            top = jnp.max(scores, axis=-1, keepdims=True)
            grown = jnp.exp(scores - top)
            amount = jnp.sum(grown, axis=-1, keepdims=True)
            kept = jnp.where(lane == 2 * pair + j, top + jnp.log(amount), kept)
            probs = (grown * (1.0 / amount)).astype(BF16)
            out += dot_nn(probs, value * only)
        o_ref[:, lanes] = out.astype(BF16)
    lse_ref[...] = kept


def mlp_kernel(
    place_ref, x_ref, own_o_ref, far_o_ref, own_out_ref, far_out_ref, vec_ref, up_b_ref, g_ref, order_ref,
    up_0, up_1, up_2, up_3, down_0, down_1, down_2, down_3,
    h_ref, m_own_ref, m_far_ref, grad_a_ref, grad_up_b_ref, grad_down_b_ref,
    part_0, part_1, part_2, part_3,
    up_ref, down_ref, grad_up_ref, grad_down_ref,
):
    core = place_ref[0]
    up_at, down_at = positions(core, place_ref[3]), positions(core, place_ref[2])
    for up, at in zip((up_0, up_1, up_2, up_3), up_at):
        up_ref[pl.ds(pl.multiple_of(at * BLOCK, 64), BLOCK), :] = up[...]
    for down, at in zip((down_0, down_1, down_2, down_3), down_at):
        down_ref[pl.ds(pl.multiple_of(at * DOWN_ROWS, 128), DOWN_ROWS), :] = down[...]
    here = pl.multiple_of(core * HALF, 128)
    there = pl.multiple_of((1 - core) * HALF, 128)
    own_o = own_o_ref[...]
    far_o = swap_halves(far_o_ref[...])
    for out_ref, at in ((own_out_ref, here), (far_out_ref, there)):
        part = dot_nn(own_o, out_ref[pl.ds(here, HALF), :]) + dot_nn(far_o, out_ref[pl.ds(there, HALF), :])
        h_ref[:, pl.ds(at, HALF)] = part
    hidden = x_ref[...].astype(F32) + (h_ref[...] + vec_ref[4:5, :])
    h_ref[...] = hidden
    unit, _ = normalised(hidden)
    a = (unit * vec_ref[5:6, :] + vec_ref[6:7, :]).astype(BF16)
    a = dot_nn(a, order_ref[...]).astype(BF16)
    g = g_ref[...]
    branch = jnp.zeros((ROWS, WIDTH), F32)
    grad_a = jnp.zeros((ROWS, WIDTH), F32)
    step = 512
    for i in range(UP // step):
        cols = pl.ds(i * step, step)
        up = up_ref[:, cols]
        down = down_ref[cols, :]
        u = dot_nn(a, up) + up_b_ref[:, cols]
        phi = 0.5 * (1.0 + lax.erf(u * (0.5**0.5)))
        z = (u * phi).astype(BF16)
        slope = phi + u * (jnp.exp(-0.5 * u * u) * (2.0 * jnp.pi) ** (-0.5))
        branch += dot_nn(z, down)
        gu = (dot_nt(g, down) * slope).astype(BF16)
        grad_down_ref[cols, :] = dot_tn(z, g).astype(BF16)
        grad_up_ref[:, cols] = dot_tn(a, gu).astype(BF16)
        grad_up_b_ref[:, cols] = total(gu)
        grad_a += dot_nt(gu, up)
    m_own_ref[...] = branch[:OWN] + hidden[:OWN] + vec_ref[7:8, :]
    m_far_ref[...] = branch[OWN:]
    high = grad_a.astype(BF16)
    low = (grad_a - high.astype(F32)).astype(BF16)
    grad_a_ref[...] = dot_nt(high, order_ref[...]) + dot_nt(low, order_ref[...])
    grad_down_b_ref[...] = total(g[:OWN])
    for part, at in zip((part_0, part_1, part_2, part_3), up_at):
        rows = pl.ds(pl.multiple_of(at * BLOCK, 64), BLOCK)
        part[0:BLOCK, :] = grad_up_ref[rows, pl.ds(0, WIDTH)]
        part[BLOCK : 2 * BLOCK, :] = grad_up_ref[rows, pl.ds(WIDTH, WIDTH)]
        for y in range(4):
            part[2 * BLOCK + 96 * y : 2 * BLOCK + 96 * (y + 1), :] = grad_down_ref[
                pl.ds(pl.multiple_of(DOWN_ROWS * y + 96 * at, 32), 96), :
            ]


def back_kernel(
    place_ref, x_ref, h_ref, g_ref, own_grad_ref, far_grad_ref, vec_ref, own_o_ref, far_o_ref, own_out_ref, far_out_ref,
    qkv_ref, lse_ref, a_ref, w_ref, down_b_ref, up_cols_ref,
    part_0, part_1, part_2, part_3, own_x_ref, far_x_ref, gh_ref,
    gh_low_ref, go_ref, gqkv_ref, rows_ref, message_ref,
):
    core = place_ref[0]
    here = pl.multiple_of(core * HALF, 128)
    there = pl.multiple_of((1 - core) * HALF, 128)
    rows_ref[...] = jnp.zeros((128, WIDTH), F32)
    grad_a = own_grad_ref[...] + swap_halves(far_grad_ref[...])
    unit, scale = normalised(h_ref[...])
    grad_h = g_ref[...].astype(F32) + norm_back(grad_a, unit, scale, vec_ref[5:6, :])
    gh_ref[...] = grad_h[:OWN]
    low = grad_h.astype(BF16)
    gh_low_ref[...] = low
    rows_ref[4:5, :] = total(low[:OWN])
    rows_ref[5:6, :] = total(grad_a[:OWN] * unit[:OWN])
    rows_ref[6:7, :] = total(grad_a[:OWN])
    rows_ref[7:8, :] = down_b_ref[...]
    low_here = gh_low_ref[:, pl.ds(here, HALF)]
    low_there = gh_low_ref[:, pl.ds(there, HALF)]
    rows = pl.ds(here, HALF)
    go_ref[...] = (dot_nt(low_here, own_out_ref[rows, :]) + dot_nt(low_there, far_out_ref[rows, :])).astype(BF16)
    outs = pl.ds(QKV + SMALL, HALF)
    message_ref[pl.ds(here, HALF), outs] = dot_tn(own_o_ref[...], low_here).astype(BF16)
    message_ref[pl.ds(there, HALF), outs] = dot_tn(swap_halves(far_o_ref[...]), low_here).astype(BF16)
    admitted, live = masks(core)
    live = jnp.where(live, 1.0, 0.0)
    lane = lax.broadcasted_iota(jnp.int32, (ROWS, 128), 1)
    for pair in range(3):
        query = qkv_ref[:, pl.ds(128 * pair, 128)]
        key = qkv_ref[:, pl.ds(HALF + 128 * pair, 128)]
        value = qkv_ref[:, pl.ds(2 * HALF + 128 * pair, 128)]
        go = go_ref[:, pl.ds(128 * pair, 128)]
        gq = jnp.zeros((ROWS, 128), F32)
        gk = jnp.zeros((ROWS, 128), F32)
        gv = jnp.zeros((ROWS, 128), F32)
        for j in range(2):
            only = head_lanes(j)
            lse = jnp.sum(jnp.where(lane == 2 * pair + j, lse_ref[...], 0.0), axis=-1, keepdims=True)
            scores = jnp.where(admitted, dot_nt(query * only, key) * SCALE, MASKED)
            probs = jnp.exp(scores - lse)
            grad_p = dot_nt(go * only, value)
            grad_s = probs * (grad_p - jnp.sum(probs * grad_p, axis=-1, keepdims=True))
            gq += dot_nn(grad_s.astype(BF16), key * only)
            gk += dot_tn((grad_s * live).astype(BF16), query * only)
            gv += dot_tn((probs * live).astype(BF16), go * only)
        gqkv_ref[:, pl.ds(128 * pair, 128)] = (gq * SCALE).astype(BF16)
        gqkv_ref[:, pl.ds(HALF + 128 * pair, 128)] = (gk * SCALE).astype(BF16)
        gqkv_ref[:, pl.ds(2 * HALF + 128 * pair, 128)] = gv.astype(BF16)
    gqkv = gqkv_ref[...]
    message_ref[:, pl.ds(0, QKV)] = dot_tn(a_ref[...], gqkv).astype(BF16)
    grad_x = dot_nt(gqkv, w_ref[...])
    own_x_ref[...] = grad_x[:OWN]
    far_x_ref[...] = grad_x[OWN:]
    unit, _ = normalised(x_ref[...].astype(F32))
    sums = total(gqkv)
    rows_ref[0:1, :] = total(grad_x * unit)
    rows_ref[1:2, :] = total(grad_x)
    rows_ref[2:3, pl.ds(here, HALF)] = sums[:, :HALF]
    rows_ref[3:4, pl.ds(here, HALF)] = sums[:, 2 * HALF :]
    full = rows_ref[0:8, :]
    high = full.astype(BF16).astype(F32)
    rows_ref[0:8, :] = high
    rows_ref[16:24, :] = full - high
    message_ref[:, pl.ds(QKV, SMALL)] = (rows_ref[...].T + up_cols_ref[...]).astype(BF16)
    for part, at in zip((part_0, part_1, part_2, part_3), positions(core, place_ref[1])):
        part[...] = message_ref[pl.ds(pl.multiple_of(at * BLOCK, 64), BLOCK), :]


def tokens_kernel(place_ref, x_ref, own_x_ref, far_x_ref, gh_ref, vec_ref, out_ref):
    unit, scale = normalised(x_ref[0:OWN, :].astype(F32))
    grad = own_x_ref[...] + far_x_ref[...]
    out_ref[...] = (gh_ref[...] + norm_back(grad, unit, scale, vec_ref[0:1, :])).astype(BF16)


def call(kernel, place, args, outs, scratch=()):
    specs = [pl.BlockSpec(memory_space=pltpu.VMEM)] * len(args)
    if place is not None:
        args = (place,) + tuple(args)
        specs = [pl.BlockSpec(memory_space=pltpu.SMEM)] + specs
    return pl.pallas_call(
        kernel,
        out_shape=tuple(jax.ShapeDtypeStruct(s, d) for s, d in outs),
        in_specs=specs,
        out_specs=tuple(pl.BlockSpec(memory_space=pltpu.VMEM) for _ in outs),
        scratch_shapes=[pltpu.VMEM(s, d) for s, d in scratch],
        compiler_params=pltpu.CompilerParams(vmem_limit_bytes=VMEM_LIMIT),
        cost_estimate=pl.CostEstimate(flops=1, bytes_accessed=1, transcendentals=0),
    )(*args)


def between_cores(values):
    return lax.ppermute(values, "c", [(0, 1), (1, 0)])


def between_chips(values):
    return lax.ppermute(values, "yl", [(0, 1), (1, 0)])


def swap_items(values):
    return lax.ppermute(values, ("c", "yl"), [(0, 0), (1, 2), (2, 1), (3, 3)])


def up_order():
    u = lax.optimization_barrier(jnp.arange(WIDTH, dtype=jnp.int32))
    z, x, yh, i = u // BLOCK, u % BLOCK // 48, u % 48 // 24, u % 24
    n = ((x * 2 + yh) * 4 + z) * 24 + i
    return (n[None, :] == lax.broadcasted_iota(jnp.int32, (WIDTH, WIDTH), 0)).astype(BF16)


def ring(values, axis, by):
    return lax.ppermute(values, axis, [(i, (i + by) % 4) for i in range(4)])


def ring_gather(block, axis):
    return [block, ring(block, axis, -1), ring(block, axis, 2), ring(block, axis, 1)]


def ring_order(blocks, at):
    return [lax.select_n(lax.rem(j - at + 4, 4), *blocks) for j in range(4)]


def ring_reduce(blocks, axis):
    got = [ring(blocks[1], axis, 1), ring(blocks[2], axis, 2), ring(blocks[3], axis, -1)]
    return sum((g.astype(F32) for g in got), blocks[0].astype(F32))


def ring_split(values, at, axis=0):
    size = values.shape[axis] // 4
    return [lax.dynamic_slice_in_dim(values, lax.rem(at + j, 4) * size, size, axis) for j in range(4)]


def along(axis, by):
    pairs = []
    for x, yh, z, c, yl in np.ndindex(*SIZES):
        at = {"x": x, "y": 2 * yh + yl, "z": z}
        at[axis] = (at[axis] + (by if c == 0 else -by)) % 4
        to = (at["x"], at["y"] // 2, at["z"], c, at["y"] % 2)
        pairs.append((int(np.ravel_multi_index((x, yh, z, c, yl), SIZES)), int(np.ravel_multi_index(to, SIZES))))
    return pairs


def send(values, axis, by):
    return lax.ppermute(values, AXES, along(axis, by))


def relay_gather(block, axis):
    behind = send(block, axis, 1)
    return [block, behind, send(block, axis, -1), send(behind, axis, 1)]


def relay_start(blocks, axis):
    return send(blocks[3], axis, 1), send(blocks[1], axis, -1)


def relay_end(blocks, got, axis):
    ahead = (blocks[2].astype(F32) + got[0].astype(F32)).astype(BF16)
    return blocks[0].astype(F32) + got[1].astype(F32) + send(ahead, axis, 1).astype(F32)


def by_place(place, first, second, axis=0):
    return jnp.where(
        place == 0, jnp.concatenate([first, second], axis), jnp.concatenate([second, first], axis)
    )


def other_half(values, place):
    rows = values.shape[0] // 2
    return (
        lax.dynamic_slice_in_dim(values, (1 - place) * rows, rows, 0),
        lax.dynamic_slice_in_dim(values, place * rows, rows, 0),
    )


def shards(
    tokens,
    segment_counts,
    ln1_gain,
    ln1_bias,
    w_qkv,
    q_bias,
    v_bias,
    w_out,
    out_bias,
    ln2_gain,
    ln2_bias,
    w_up,
    up_bias,
    w_down,
    down_bias,
    cotangent,
):
    core = lax.axis_index("c")
    x_at, z_at = lax.axis_index("x"), lax.axis_index("z")
    y_at = lax.axis_index(RING_Y)
    place = jnp.stack([core, x_at, y_at, z_at]).astype(jnp.int32)
    present = jnp.arange(SLOTS) < segment_counts[0]
    present_rows = jnp.repeat(present, HALFSEG)[:, None]
    cot = jnp.where(present_rows, cotangent.reshape(OWN, WIDTH), 0).astype(BF16)

    mine = swap_items(jnp.concatenate([tokens.reshape(OWN, WIDTH), cot], axis=1))
    downs = ring_gather(w_down, "x")
    (parts,) = call(
        halves_kernel,
        None,
        (
            w_qkv, w_out, w_up, ln1_gain, ln1_bias, q_bias, v_bias, out_bias, ln2_gain, ln2_bias, down_bias, up_bias,
        ),
        (((8, 6, ATTN + UP), BF16),),
        (((16, 128), F32), ((6, FF), F32), ((6, UP), F32)),
    )
    rows = lax.all_to_all(parts, EIGHT, 0, 0, tiled=True).reshape(2, 24, ATTN + UP)
    attn, ups = rows[:, :, :ATTN], rows[:, :, ATTN:].reshape(48, UP)
    downs = jnp.concatenate(ring_order(downs, x_at), axis=0)

    attn = ring_gather(attn, "z")
    ups = ring_gather(ups, "x")
    *attn, downs = lax.optimization_barrier((*attn, downs))
    downs = ring_gather(downs, "z")
    item = jnp.concatenate([mine, between_cores(mine)], axis=0)
    x, g = item[:, :WIDTH], item[:, WIDTH:]
    attn = jnp.concatenate(ring_order(attn, z_at), axis=1).reshape(BLOCK, ATTN)
    ups = jnp.concatenate(ring_order(ups, x_at), axis=0)
    downs = jnp.concatenate(ring_order(downs, z_at), axis=0)

    attn = relay_gather(attn, "x")
    ups = relay_gather(ups, "z")
    downs = relay_gather(downs, "y")

    a1, qkv, own_o, lse, w_in, own_out, small_all, vectors = call(
        attend_kernel,
        place,
        (x, *attn),
        (
            ((ROWS, WIDTH), BF16),
            ((ROWS, QKV), BF16),
            ((ROWS, HALF), BF16),
            ((ROWS, 128), F32),
            ((WIDTH, QKV), BF16),
            ((WIDTH, HALF), BF16),
            ((WIDTH, SMALL), BF16),
            ((16, WIDTH), F32),
        ),
    )
    far_o, far_out = between_cores(own_o), between_cores(own_out)
    up_b = small_all[:, 8:12].reshape(4, 2, 4, 2, 2, 24)
    up_b = lax.dynamic_index_in_dim(up_b, core, 3, keepdims=False)
    up_b = up_b.transpose(1, 3, 2, 0, 4).reshape(1, UP).astype(F32)
    hidden, m_own, m_far, grad_a_own, grad_up_b, grad_down_b, *grads = call(
        mlp_kernel,
        place,
        (x, own_o, far_o, own_out, far_out, vectors, up_b, g, up_order(), *ups, *downs),
        (
            ((ROWS, WIDTH), F32),
            ((OWN, WIDTH), F32),
            ((OWN, WIDTH), F32),
            ((ROWS, WIDTH), F32),
            ((1, UP), F32),
            ((1, WIDTH), F32),
        )
        + (((2 * BLOCK + DOWN_ROWS, WIDTH), BF16),) * 4,
        (((WIDTH, UP), BF16), ((UP, WIDTH), BF16), ((WIDTH, UP), BF16), ((UP, WIDTH), BF16)),
    )
    grad_a_far = between_cores(grad_a_own)
    grad_a_far, *grads = lax.optimization_barrier((grad_a_far, *grads))
    got = relay_start(grads, "z")
    block = swap_items((m_own + between_cores(m_far)).astype(BF16))
    block_out = jnp.where(present_rows, block, 0).reshape(tokens.shape)
    up_cols = grad_up_b.reshape(2, 2, 4, 4, 24).transpose(3, 0, 2, 1, 4)[:, :, :, None]
    up_cols = jnp.where((jnp.arange(2) == core)[:, None, None], up_cols, 0.0).reshape(WIDTH, 4)
    up_high = up_cols.astype(BF16).astype(F32)
    up_cols = jnp.pad(up_high, ((0, 0), (8, SMALL - 12))) + jnp.pad(up_cols - up_high, ((0, 0), (24, SMALL - 28)))

    *grad_attn, own_x, far_x, gh = call(
        back_kernel,
        place,
        (
            x, hidden, g, grad_a_own, grad_a_far, vectors, own_o, far_o, own_out, far_out, qkv, lse, a1, w_in,
            grad_down_b, up_cols,
        ),
        (((BLOCK, ATTN), BF16),) * 4 + (((OWN, WIDTH), F32),) * 3,
        (
            ((ROWS, WIDTH), BF16),
            ((ROWS, HALF), BF16),
            ((ROWS, QKV), BF16),
            ((128, WIDTH), F32),
            ((WIDTH, ATTN), BF16),
        ),
    )
    (grad_x,) = call(
        tokens_kernel, place, (x, own_x, between_cores(far_x), gh, vectors), (((OWN, WIDTH), BF16),)
    )
    grad_x = swap_items(grad_x)

    attn_sum = relay_end(grad_attn, relay_start(grad_attn, "x"), "x").astype(BF16).reshape(2, 4, 24, ATTN)
    attn_sum = ring_reduce([a[:, 0] for a in ring_split(attn_sum, z_at, 1)], "z")
    mlp_sum = relay_end(grads, got, "z").astype(BF16)
    up_parts = ring_split(mlp_sum[: 2 * BLOCK].reshape(2, 4, 48, WIDTH), x_at, 1)
    down_parts = ring_split(mlp_sum[2 * BLOCK :].reshape(4, 4, 24, WIDTH), x_at, 1)
    mlp_sum = ring_reduce(
        [jnp.concatenate([u.reshape(96, WIDTH), d.reshape(96, WIDTH)]) for u, d in zip(up_parts, down_parts)], "x"
    )
    up_sum = jnp.concatenate([mlp_sum[:48], mlp_sum[48:96]], axis=1).reshape(2, 24, UP)
    down_sum = ring_reduce(ring_split(mlp_sum[96:].astype(BF16), y_at), RING_Y)
    sums = jnp.concatenate([attn_sum.astype(BF16), up_sum.astype(BF16)], axis=2)
    got = lax.all_to_all(sums.reshape(8, 6, ATTN + UP), EIGHT, 0, 0, tiled=True)
    out_qkv, out_out, out_up, out_down, grad_tokens, *vecs, out_up_b = call(
        outputs_kernel,
        None,
        (got, down_sum, grad_x),
        (
            ((6, 3 * WIDTH), F32),
            ((6, WIDTH), F32),
            ((6, FF), F32),
            ((24, WIDTH), F32),
            ((OWN, WIDTH), BF16),
        )
        + (((6,), F32),) * 8
        + (((24,), F32),),
        (((128, 128), F32),),
    )
    gain_1, bias_1, bias_q, bias_v, bias_out, gain_2, bias_2, bias_down = vecs
    return (
        block_out,
        grad_tokens.reshape(tokens.shape),
        gain_1,
        bias_1,
        out_qkv,
        bias_q,
        bias_v,
        out_out,
        bias_out,
        gain_2,
        bias_2,
        out_up,
        out_up_b,
        out_down,
        bias_down,
    )


def solution(mesh):
    torus = Mesh(np.asarray(mesh.devices).reshape(SIZES), AXES)
    items = P(("x", "yh", "z", "c"), None, "yl", None)
    part, rows = P(AXES), P(AXES, None)
    return jax.shard_map(
        shards,
        mesh=torus,
        in_specs=(
            items, P(("x", "yh", "z", "c")), part, part, rows, part, part, rows, part, part, part, rows, part, rows,
            part, items,
        ),
        out_specs=(
            items, items, part, part, rows, part, part, rows, part, part, part, rows, part, rows, part,
        ),
        check_vma=False,
    )
```

```python
import jax
import jax.numpy as jnp
import numpy as np
from jax import lax
from jax.experimental import pallas as pl
from jax.experimental.pallas import tpu as pltpu
from jax.sharding import Mesh
from jax.sharding import PartitionSpec as P

WIDTH = 768
HEAD = 64
NSUM = 16
SLOTS = 4
SEGLEN = 64
HALFSEG = 32
FF = 3072

EPSILON = 1e-05
MASKED = -1e30
SCALE = HEAD ** (-0.5)

AXES = ("x", "yh", "z", "c", "yl")
SIZES = (4, 2, 4, 2, 2)
QUAD_AXES = ("x", "yh", "z")
QUADS = 32
DEVICES = 128
ROWS = 256
OWN = 128
HALF = WIDTH // 2
QKV = 3 * HALF
UP = FF // 2
SMALL = 128
ATTN = QKV + SMALL + HALF
BLOCK = WIDTH // 4
DOWN_ROWS = UP // 4
RING_Y = ("yh", "yl")
EIGHT = ("yh", "c", "yl")
VMEM_LIMIT = 60 * 1024 * 1024

F32 = jnp.float32
BF16 = jnp.bfloat16


def dot_nn(left, right):
    return jnp.dot(left, right, preferred_element_type=F32)


def dot_tn(left, right):
    return lax.dot_general(left, right, (((0,), (0,)), ((), ())), preferred_element_type=F32)


def dot_nt(left, right):
    return lax.dot_general(left, right, (((1,), (1,)), ((), ())), preferred_element_type=F32)


def normalised(values):
    center = values - jnp.mean(values, axis=-1, keepdims=True)
    spread = jnp.mean(center * center, axis=-1, keepdims=True)
    scale = lax.rsqrt(spread + EPSILON)
    return center * scale, scale


def norm_back(grad, unit, scale, gain):
    inner = grad * gain
    mean = jnp.mean(inner, axis=-1, keepdims=True)
    along = jnp.mean(inner * unit, axis=-1, keepdims=True)
    return scale * (inner - mean - unit * along)


def total(values):
    return jnp.sum(values.astype(F32), axis=0, keepdims=True)


def swap_halves(values):
    return jnp.concatenate([values[OWN:], values[:OWN]], axis=0)


def masks(core):
    def place(dim):
        row = lax.broadcasted_iota(jnp.int32, (ROWS, ROWS), dim)
        second = (row >= OWN).astype(jnp.int32)
        inner = row - second * OWN
        half = core + second - 2 * core * second
        slot = inner // HALFSEG
        return slot, half * HALFSEG + inner - slot * HALFSEG

    query_slot, query_pos = place(0)
    key_slot, key_pos = place(1)
    same = (query_slot == key_slot) & (key_pos <= query_pos)
    earlier = (key_slot < query_slot) & (key_pos >= SEGLEN - NSUM)
    return same | earlier, key_slot >= query_slot - 2


def positions(core, at):
    way = 1 - 2 * core
    return at, lax.rem(at + 4 - way, 4), lax.rem(at + 4 + way, 4), lax.rem(at + 2, 4)


def head_lanes(j):
    lane = lax.broadcasted_iota(jnp.int32, (1, 2 * HEAD), 1)
    return jnp.where(lane // HEAD == j, 1.0, 0.0).astype(BF16)


def up_runs(t):
    for yh, yl, z, x in np.ndindex(2, 2, 4, 4):
        yield 96 * ((x * 2 + yh) * 4 + z) + 48 * t + 24 * yl, 24 * (((yh * 2 + yl) * 4 + z) * 4 + x)


def halves_kernel(qkv_ref, out_ref, up_ref, *refs):
    *vec_refs, up_b_ref, parts_ref, rows_ref, wide_ref, half_ref = refs
    rows_ref[...] = jnp.zeros((16, 128), F32)
    for v, ref in enumerate(vec_refs):
        rows_ref[v : v + 1, 0:6] = ref[...].astype(F32).reshape(1, 6)
    rows_ref[8:9, 0:24] = up_b_ref[...].astype(F32).reshape(1, 24)
    row = lax.broadcasted_iota(jnp.int32, (8, 128), 0)
    lane = lax.broadcasted_iota(jnp.int32, (8, 128), 1)
    src = lax.broadcasted_iota(jnp.int32, (128, 128), 0)
    col = lax.broadcasted_iota(jnp.int32, (128, 128), 1)
    one = jnp.where(row == lane, 1.0, 0.0).astype(BF16)
    vecs = jnp.concatenate([rows_ref[0:8, :].astype(BF16), jnp.zeros((120, 128), BF16)], axis=0)
    up_b = jnp.where(lane // 4 == row, jnp.broadcast_to(rows_ref[8:9, :], (8, 128)), 0.0).astype(BF16)
    put = jnp.where((src < 24) & (8 + lax.rem(src, 4) == col), 1.0, 0.0).astype(BF16)
    small = (dot_nt(one, vecs) + dot_nn(up_b, put)).astype(BF16)
    wide_ref[...] = up_ref[...].astype(F32)
    for t in range(2):
        for src, to in up_runs(t):
            half_ref[:, to : to + 24] = wide_ref[:, src : src + 24]
        up = half_ref[...].astype(BF16)
        for at in (2 * t, 2 * t + 1, 2 * t + 4, 2 * t + 5):
            for j in range(3):
                parts_ref[at, :, j * HALF : (j + 1) * HALF] = qkv_ref[:, j * WIDTH + t * HALF : j * WIDTH + (t + 1) * HALF]
            parts_ref[at, :, QKV : QKV + SMALL] = small[:6]
            parts_ref[at, :, QKV + SMALL : ATTN] = out_ref[:, t * HALF : (t + 1) * HALF]
            parts_ref[at, :, ATTN:] = up


def outputs_kernel(
    got_ref, down_ref, tokens_ref,
    qkv_ref, out_ref, up_ref, out_down_ref, out_tokens_ref, *refs,
):
    *vec_refs, up_b_ref, rows_ref = refs
    out_down_ref[...] = down_ref[...]
    out_tokens_ref[...] = tokens_ref[...]
    small = jnp.zeros((6, SMALL), F32)
    for t in range(2):
        rows = [got_ref[at].astype(F32) for at in (2 * t, 2 * t + 1, 2 * t + 4, 2 * t + 5)]
        rows = (rows[0] + rows[1]) + (rows[2] + rows[3])
        for j in range(3):
            qkv_ref[:, j * WIDTH + t * HALF : j * WIDTH + (t + 1) * HALF] = rows[:, j * HALF : (j + 1) * HALF]
        small += rows[:, QKV : QKV + SMALL]
        out_ref[:, t * HALF : (t + 1) * HALF] = rows[:, QKV + SMALL : ATTN]
        for to, src in up_runs(t):
            up_ref[:, to : to + 24] = rows[:, ATTN + src : ATTN + src + 24]
    small = small[:, 0:12] + small[:, 16:28]
    rows_ref[...] = jnp.zeros((128, 128), F32)
    rows_ref[0:6, 0:12] = small
    flipped = rows_ref[...].T
    for v, ref in enumerate(vec_refs):
        ref[...] = flipped[v : v + 1, 0:6].reshape(6)
    up_b_ref[...] = jnp.concatenate([small[j : j + 1, 8:12] for j in range(6)], axis=1).reshape(24)


def attend_kernel(
    place_ref, x_ref, part_0, part_1, part_2, part_3,
    a_ref, qkv_ref, o_ref, lse_ref, w_ref, out_ref, small_ref, vec_ref,
):
    core = place_ref[0]
    for part, at in zip((part_0, part_1, part_2, part_3), positions(core, place_ref[1])):
        rows = pl.ds(pl.multiple_of(at * BLOCK, 64), BLOCK)
        w_ref[rows, :] = part[:, pl.ds(0, QKV)]
        small_ref[rows, :] = part[:, pl.ds(QKV, SMALL)]
        out_ref[rows, :] = part[:, pl.ds(QKV + SMALL, HALF)]
    vec_ref[...] = small_ref[...].astype(F32).T[:16]
    unit, _ = normalised(x_ref[...].astype(F32))
    a = (unit * vec_ref[0:1, :] + vec_ref[1:2, :]).astype(BF16)
    a_ref[...] = a
    here = pl.ds(pl.multiple_of(core * HALF, 128), HALF)
    shift = jnp.concatenate([vec_ref[2:3, here], jnp.zeros((1, HALF), F32), vec_ref[3:4, here]], axis=1)
    qkv_ref[...] = (dot_nn(a, w_ref[...]) + shift).astype(BF16)
    admitted, _ = masks(core)
    lane = lax.broadcasted_iota(jnp.int32, (ROWS, 128), 1)
    kept = jnp.zeros((ROWS, 128), F32)
    for pair in range(3):
        lanes = pl.ds(128 * pair, 128)
        query = qkv_ref[:, lanes]
        key = qkv_ref[:, pl.ds(HALF + 128 * pair, 128)]
        value = qkv_ref[:, pl.ds(2 * HALF + 128 * pair, 128)]
        out = jnp.zeros((ROWS, 128), F32)
        for j in range(2):
            only = head_lanes(j)
            scores = jnp.where(admitted, dot_nt(query * only, key) * SCALE, MASKED)
            top = jnp.max(scores, axis=-1, keepdims=True)
            grown = jnp.exp(scores - top)
            amount = jnp.sum(grown, axis=-1, keepdims=True)
            kept = jnp.where(lane == 2 * pair + j, top + jnp.log(amount), kept)
            probs = (grown * (1.0 / amount)).astype(BF16)
            out += dot_nn(probs, value * only)
        o_ref[:, lanes] = out.astype(BF16)
    lse_ref[...] = kept


def mlp_kernel(
    place_ref, x_ref, own_o_ref, far_o_ref, own_out_ref, far_out_ref, vec_ref, up_b_ref, g_ref, order_ref,
    up_0, up_1, up_2, up_3, down_0, down_1, down_2, down_3,
    h_ref, m_own_ref, m_far_ref, grad_a_ref, grad_up_b_ref, grad_down_b_ref,
    gup_0, gup_1, gup_2, gup_3, gdown_0, gdown_1, gdown_2, gdown_3,
    up_ref, down_ref, grad_up_ref, grad_down_ref,
):
    core = place_ref[0]
    up_at, down_at = positions(core, place_ref[3]), positions(core, place_ref[2])
    for up, at in zip((up_0, up_1, up_2, up_3), up_at):
        up_ref[pl.ds(pl.multiple_of(at * BLOCK, 64), BLOCK), :] = up[...]
    for down, at in zip((down_0, down_1, down_2, down_3), down_at):
        down_ref[pl.ds(pl.multiple_of(at * DOWN_ROWS, 128), DOWN_ROWS), :] = down[...]
    here = pl.multiple_of(core * HALF, 128)
    there = pl.multiple_of((1 - core) * HALF, 128)
    own_o = own_o_ref[...]
    far_o = swap_halves(far_o_ref[...])
    for out_ref, at in ((own_out_ref, here), (far_out_ref, there)):
        part = dot_nn(own_o, out_ref[pl.ds(here, HALF), :]) + dot_nn(far_o, out_ref[pl.ds(there, HALF), :])
        h_ref[:, pl.ds(at, HALF)] = part
    hidden = x_ref[...].astype(F32) + (h_ref[...] + vec_ref[4:5, :])
    h_ref[...] = hidden
    unit, _ = normalised(hidden)
    a = (unit * vec_ref[5:6, :] + vec_ref[6:7, :]).astype(BF16)
    a = dot_nn(a, order_ref[...]).astype(BF16)
    g = g_ref[...]
    branch = jnp.zeros((ROWS, WIDTH), F32)
    grad_a = jnp.zeros((ROWS, WIDTH), F32)
    step = 512
    for i in range(UP // step):
        cols = pl.ds(i * step, step)
        up = up_ref[:, cols]
        down = down_ref[cols, :]
        u = dot_nn(a, up) + up_b_ref[:, cols]
        phi = 0.5 * (1.0 + lax.erf(u * (0.5**0.5)))
        z = (u * phi).astype(BF16)
        slope = phi + u * (jnp.exp(-0.5 * u * u) * (2.0 * jnp.pi) ** (-0.5))
        branch += dot_nn(z, down)
        gu = (dot_nt(g, down) * slope).astype(BF16)
        grad_down_ref[cols, :] = dot_tn(z, g).astype(BF16)
        grad_up_ref[:, cols] = dot_tn(a, gu).astype(BF16)
        grad_up_b_ref[:, cols] = total(gu)
        grad_a += dot_nt(gu, up)
    m_own_ref[...] = branch[:OWN] + hidden[:OWN] + vec_ref[7:8, :]
    m_far_ref[...] = branch[OWN:]
    high = grad_a.astype(BF16)
    low = (grad_a - high.astype(F32)).astype(BF16)
    grad_a_ref[...] = dot_nt(high, order_ref[...]) + dot_nt(low, order_ref[...])
    grad_down_b_ref[...] = total(g[:OWN])
    for gup, at in zip((gup_0, gup_1, gup_2, gup_3), up_at):
        gup[...] = grad_up_ref[pl.ds(pl.multiple_of(at * BLOCK, 64), BLOCK), :]
    for gdown, at in zip((gdown_0, gdown_1, gdown_2, gdown_3), down_at):
        gdown[...] = grad_down_ref[pl.ds(pl.multiple_of(at * DOWN_ROWS, 128), DOWN_ROWS), :]


def back_kernel(
    place_ref, x_ref, h_ref, g_ref, own_grad_ref, far_grad_ref, vec_ref, own_o_ref, far_o_ref, own_out_ref, far_out_ref,
    qkv_ref, lse_ref, a_ref, w_ref, down_b_ref, up_cols_ref,
    part_0, part_1, part_2, part_3, own_x_ref, far_x_ref, gh_ref,
    gh_low_ref, go_ref, gqkv_ref, rows_ref, message_ref,
):
    core = place_ref[0]
    here = pl.multiple_of(core * HALF, 128)
    there = pl.multiple_of((1 - core) * HALF, 128)
    rows_ref[...] = jnp.zeros((128, WIDTH), F32)
    grad_a = own_grad_ref[...] + swap_halves(far_grad_ref[...])
    unit, scale = normalised(h_ref[...])
    grad_h = g_ref[...].astype(F32) + norm_back(grad_a, unit, scale, vec_ref[5:6, :])
    gh_ref[...] = grad_h[:OWN]
    low = grad_h.astype(BF16)
    gh_low_ref[...] = low
    rows_ref[4:5, :] = total(low[:OWN])
    rows_ref[5:6, :] = total(grad_a[:OWN] * unit[:OWN])
    rows_ref[6:7, :] = total(grad_a[:OWN])
    rows_ref[7:8, :] = down_b_ref[...]
    low_here = gh_low_ref[:, pl.ds(here, HALF)]
    low_there = gh_low_ref[:, pl.ds(there, HALF)]
    rows = pl.ds(here, HALF)
    go_ref[...] = (dot_nt(low_here, own_out_ref[rows, :]) + dot_nt(low_there, far_out_ref[rows, :])).astype(BF16)
    outs = pl.ds(QKV + SMALL, HALF)
    message_ref[pl.ds(here, HALF), outs] = dot_tn(own_o_ref[...], low_here).astype(BF16)
    message_ref[pl.ds(there, HALF), outs] = dot_tn(swap_halves(far_o_ref[...]), low_here).astype(BF16)
    admitted, live = masks(core)
    live = jnp.where(live, 1.0, 0.0)
    lane = lax.broadcasted_iota(jnp.int32, (ROWS, 128), 1)
    for pair in range(3):
        query = qkv_ref[:, pl.ds(128 * pair, 128)]
        key = qkv_ref[:, pl.ds(HALF + 128 * pair, 128)]
        value = qkv_ref[:, pl.ds(2 * HALF + 128 * pair, 128)]
        go = go_ref[:, pl.ds(128 * pair, 128)]
        gq = jnp.zeros((ROWS, 128), F32)
        gk = jnp.zeros((ROWS, 128), F32)
        gv = jnp.zeros((ROWS, 128), F32)
        for j in range(2):
            only = head_lanes(j)
            lse = jnp.sum(jnp.where(lane == 2 * pair + j, lse_ref[...], 0.0), axis=-1, keepdims=True)
            scores = jnp.where(admitted, dot_nt(query * only, key) * SCALE, MASKED)
            probs = jnp.exp(scores - lse)
            grad_p = dot_nt(go * only, value)
            grad_s = probs * (grad_p - jnp.sum(probs * grad_p, axis=-1, keepdims=True))
            gq += dot_nn(grad_s.astype(BF16), key * only)
            gk += dot_tn((grad_s * live).astype(BF16), query * only)
            gv += dot_tn((probs * live).astype(BF16), go * only)
        gqkv_ref[:, pl.ds(128 * pair, 128)] = (gq * SCALE).astype(BF16)
        gqkv_ref[:, pl.ds(HALF + 128 * pair, 128)] = (gk * SCALE).astype(BF16)
        gqkv_ref[:, pl.ds(2 * HALF + 128 * pair, 128)] = gv.astype(BF16)
    gqkv = gqkv_ref[...]
    message_ref[:, pl.ds(0, QKV)] = dot_tn(a_ref[...], gqkv).astype(BF16)
    grad_x = dot_nt(gqkv, w_ref[...])
    own_x_ref[...] = grad_x[:OWN]
    far_x_ref[...] = grad_x[OWN:]
    unit, _ = normalised(x_ref[...].astype(F32))
    sums = total(gqkv)
    rows_ref[0:1, :] = total(grad_x * unit)
    rows_ref[1:2, :] = total(grad_x)
    rows_ref[2:3, pl.ds(here, HALF)] = sums[:, :HALF]
    rows_ref[3:4, pl.ds(here, HALF)] = sums[:, 2 * HALF :]
    full = rows_ref[0:8, :]
    high = full.astype(BF16).astype(F32)
    rows_ref[0:8, :] = high
    rows_ref[16:24, :] = full - high
    message_ref[:, pl.ds(QKV, SMALL)] = (rows_ref[...].T + up_cols_ref[...]).astype(BF16)
    for part, at in zip((part_0, part_1, part_2, part_3), positions(core, place_ref[1])):
        part[...] = message_ref[pl.ds(pl.multiple_of(at * BLOCK, 64), BLOCK), :]


def tokens_kernel(place_ref, x_ref, own_x_ref, far_x_ref, gh_ref, vec_ref, out_ref):
    unit, scale = normalised(x_ref[0:OWN, :].astype(F32))
    grad = own_x_ref[...] + far_x_ref[...]
    out_ref[...] = (gh_ref[...] + norm_back(grad, unit, scale, vec_ref[0:1, :])).astype(BF16)


def call(kernel, place, args, outs, scratch=(), limit=VMEM_LIMIT):
    specs = [pl.BlockSpec(memory_space=pltpu.VMEM)] * len(args)
    if place is not None:
        args = (place,) + tuple(args)
        specs = [pl.BlockSpec(memory_space=pltpu.SMEM)] + specs
    return pl.pallas_call(
        kernel,
        out_shape=tuple(jax.ShapeDtypeStruct(s, d) for s, d in outs),
        in_specs=specs,
        out_specs=tuple(pl.BlockSpec(memory_space=pltpu.VMEM) for _ in outs),
        scratch_shapes=[pltpu.VMEM(s, d) for s, d in scratch],
        compiler_params=pltpu.CompilerParams(vmem_limit_bytes=limit),
        cost_estimate=pl.CostEstimate(flops=1, bytes_accessed=1, transcendentals=0),
    )(*args)


def between_cores(values):
    return lax.ppermute(values, "c", [(0, 1), (1, 0)])


def between_chips(values):
    return lax.ppermute(values, "yl", [(0, 1), (1, 0)])


def swap_items(values):
    return lax.ppermute(values, ("c", "yl"), [(0, 0), (1, 2), (2, 1), (3, 3)])


def up_order():
    u = lax.optimization_barrier(jnp.arange(WIDTH, dtype=jnp.int32))
    z, x, yh, i = u // BLOCK, u % BLOCK // 48, u % 48 // 24, u % 24
    n = ((x * 2 + yh) * 4 + z) * 24 + i
    return (n[None, :] == lax.broadcasted_iota(jnp.int32, (WIDTH, WIDTH), 0)).astype(BF16)


def ring(values, axis, by):
    return lax.ppermute(values, axis, [(i, (i + by) % 4) for i in range(4)])


def ring_gather(block, axis):
    return [block, ring(block, axis, -1), ring(block, axis, 2), ring(block, axis, 1)]


def ring_order(blocks, at):
    return [lax.select_n(lax.rem(j - at + 4, 4), *blocks) for j in range(4)]


def ring_sent(blocks, axis):
    return [ring(blocks[1], axis, 1), ring(blocks[2], axis, 2), ring(blocks[3], axis, -1)]


def ring_total(blocks, got):
    return sum((g.astype(F32) for g in got), blocks[0].astype(F32))


def ring_reduce(blocks, axis):
    return ring_total(blocks, ring_sent(blocks, axis))


def ring_split(values, at, axis=0):
    size = values.shape[axis] // 4
    return [lax.dynamic_slice_in_dim(values, lax.rem(at + j, 4) * size, size, axis) for j in range(4)]


def along(axis, by):
    pairs = []
    for x, yh, z, c, yl in np.ndindex(*SIZES):
        at = {"x": x, "y": 2 * yh + yl, "z": z}
        at[axis] = (at[axis] + (by if c == 0 else -by)) % 4
        to = (at["x"], at["y"] // 2, at["z"], c, at["y"] % 2)
        pairs.append((int(np.ravel_multi_index((x, yh, z, c, yl), SIZES)), int(np.ravel_multi_index(to, SIZES))))
    return pairs


def send(values, axis, by):
    return lax.ppermute(values, AXES, along(axis, by))


def relay_gather(block, axis):
    behind = send(block, axis, 1)
    return [block, behind, send(block, axis, -1), send(behind, axis, 1)]


def relay_start(blocks, axis):
    return send(blocks[3], axis, 1), send(blocks[1], axis, -1)


def relay_ahead(blocks, got):
    return (blocks[2].astype(F32) + got[0].astype(F32)).astype(BF16)


def relay_end(blocks, got, far):
    return blocks[0].astype(F32) + got[1].astype(F32) + far.astype(F32)


def after(values, *others):
    tied = lax.optimization_barrier((*values, *others))
    return list(tied[: len(values)])


def by_place(place, first, second, axis=0):
    return jnp.where(
        place == 0, jnp.concatenate([first, second], axis), jnp.concatenate([second, first], axis)
    )


def other_half(values, place):
    rows = values.shape[0] // 2
    return (
        lax.dynamic_slice_in_dim(values, (1 - place) * rows, rows, 0),
        lax.dynamic_slice_in_dim(values, place * rows, rows, 0),
    )


def shards(
    tokens,
    segment_counts,
    ln1_gain,
    ln1_bias,
    w_qkv,
    q_bias,
    v_bias,
    w_out,
    out_bias,
    ln2_gain,
    ln2_bias,
    w_up,
    up_bias,
    w_down,
    down_bias,
    cotangent,
):
    core = lax.axis_index("c")
    x_at, z_at = lax.axis_index("x"), lax.axis_index("z")
    y_at = lax.axis_index(RING_Y)
    place = jnp.stack([core, x_at, y_at, z_at]).astype(jnp.int32)
    present = jnp.arange(SLOTS) < segment_counts[0]
    present_rows = jnp.repeat(present, HALFSEG)[:, None]
    cot = jnp.where(present_rows, cotangent.reshape(OWN, WIDTH), 0).astype(BF16)

    mine = swap_items(jnp.concatenate([tokens.reshape(OWN, WIDTH), cot], axis=1))
    (parts,) = call(
        halves_kernel,
        None,
        (
            w_qkv, w_out, w_up, ln1_gain, ln1_bias, q_bias, v_bias, out_bias, ln2_gain, ln2_bias, down_bias, up_bias,
        ),
        (((8, 6, ATTN + UP), BF16),),
        (((16, 128), F32), ((6, FF), F32), ((6, UP), F32)),
    )
    downs = ring_gather(after([w_down], parts)[0], "x")
    rows = lax.all_to_all(parts, EIGHT, 0, 0, tiled=True).reshape(2, 24, ATTN + UP)
    attn, ups = rows[:, :, :ATTN], rows[:, :, ATTN:].reshape(48, UP)
    downs = jnp.concatenate(ring_order(downs, x_at), axis=0)

    attn = ring_gather(attn, "z")
    ups = ring_gather(ups, "x")
    *attn, downs = lax.optimization_barrier((*attn, downs))
    downs = ring_gather(downs, "z")
    item = jnp.concatenate([mine, between_cores(mine)], axis=0)
    x, g = item[:, :WIDTH], item[:, WIDTH:]
    attn = jnp.concatenate(ring_order(attn, z_at), axis=1).reshape(BLOCK, ATTN)
    ups = jnp.concatenate(ring_order(ups, x_at), axis=0)
    downs = jnp.concatenate(ring_order(downs, z_at), axis=0)

    attn = relay_gather(attn, "x")
    ups = relay_gather(ups, "z")
    downs = relay_gather(downs, "y")

    order = up_order()
    (x,) = after([x], order)
    a1, qkv, own_o, lse, w_in, own_out, small_all, vectors = call(
        attend_kernel,
        place,
        (x, *attn),
        (
            ((ROWS, WIDTH), BF16),
            ((ROWS, QKV), BF16),
            ((ROWS, HALF), BF16),
            ((ROWS, 128), F32),
            ((WIDTH, QKV), BF16),
            ((WIDTH, HALF), BF16),
            ((WIDTH, SMALL), BF16),
            ((16, WIDTH), F32),
        ),
    )
    far_o, far_out = between_cores(own_o), between_cores(own_out)
    up_b = small_all[:, 8:12].reshape(4, 2, 4, 2, 2, 24)
    up_b = lax.dynamic_index_in_dim(up_b, core, 3, keepdims=False)
    up_b = up_b.transpose(1, 3, 2, 0, 4).reshape(1, UP).astype(F32)
    hidden, m_own, m_far, grad_a_own, grad_up_b, grad_down_b, *grads = call(
        mlp_kernel,
        place,
        (x, own_o, far_o, own_out, far_out, vectors, up_b, g, order, *ups, *downs),
        (
            ((ROWS, WIDTH), F32),
            ((OWN, WIDTH), F32),
            ((OWN, WIDTH), F32),
            ((ROWS, WIDTH), F32),
            ((1, UP), F32),
            ((1, WIDTH), F32),
        )
        + (((BLOCK, UP), BF16),) * 4
        + (((DOWN_ROWS, WIDTH), BF16),) * 4,
        (((WIDTH, UP), BF16), ((UP, WIDTH), BF16), ((WIDTH, UP), BF16), ((UP, WIDTH), BF16)),
    )
    grad_a_far = between_cores(grad_a_own)
    grad_a_far, *grads = lax.optimization_barrier((grad_a_far, *grads))
    grad_ups, grad_downs = grads[:4], grads[4:]
    got_ups, got_downs = relay_start(grad_ups, "z"), relay_start(grad_downs, "y")
    block = (m_own + between_cores(m_far)).astype(BF16)
    up_cols = grad_up_b.reshape(2, 2, 4, 4, 24).transpose(3, 0, 2, 1, 4)[:, :, :, None]
    up_cols = jnp.where((jnp.arange(2) == core)[:, None, None], up_cols, 0.0).reshape(WIDTH, 4)
    up_high = up_cols.astype(BF16).astype(F32)
    up_cols = jnp.pad(up_high, ((0, 0), (8, SMALL - 12))) + jnp.pad(up_cols - up_high, ((0, 0), (24, SMALL - 28)))

    *grad_attn, own_x, far_x, gh = call(
        back_kernel,
        place,
        (
            x, hidden, g, grad_a_own, grad_a_far, vectors, own_o, far_o, own_out, far_out, qkv, lse, a1, w_in,
            grad_down_b, up_cols,
        ),
        (((BLOCK, ATTN), BF16),) * 4 + (((OWN, WIDTH), F32),) * 3,
        (
            ((ROWS, WIDTH), BF16),
            ((ROWS, HALF), BF16),
            ((ROWS, QKV), BF16),
            ((128, WIDTH), F32),
            ((WIDTH, ATTN), BF16),
        ),
    )
    ups_ahead, downs_ahead = relay_ahead(grad_ups, got_ups), relay_ahead(grad_downs, got_downs)
    (far_x,) = after([between_cores(far_x)], ups_ahead, downs_ahead)
    (grad_x,) = call(tokens_kernel, place, (x, own_x, far_x, gh, vectors), (((OWN, WIDTH), BF16),))

    got_attn = relay_start(grad_attn, "x")
    got_attn = after(got_attn, grad_x, block)
    attn_ahead = relay_ahead(grad_attn, got_attn)
    far_ups, far_downs = after([send(ups_ahead, "z", 1), send(downs_ahead, "y", 1)], attn_ahead)
    up_sum = relay_end(grad_ups, got_ups, far_ups).astype(BF16)
    down_sum = relay_end(grad_downs, got_downs, far_downs).astype(BF16)
    (far_attn,) = after([send(attn_ahead, "x", 1)], up_sum, down_sum)
    up_parts = ring_split(up_sum, x_at)
    down_parts = ring_split(down_sum.reshape(4, 4, 24, WIDTH), x_at, 1)
    mlp_sum = ring_reduce(
        [
            jnp.concatenate([u[:, :WIDTH], u[:, WIDTH:], d.reshape(96, WIDTH)])
            for u, d in zip(up_parts, down_parts)
        ],
        "x",
    )
    attn_sum = relay_end(grad_attn, got_attn, far_attn).astype(BF16).reshape(2, 4, 24, ATTN)
    results = swap_items(after([jnp.concatenate([block, grad_x], axis=1)], attn_sum)[0])
    attn_sum = ring_reduce([a[:, 0] for a in ring_split(attn_sum, z_at, 1)], "z")
    block_out = jnp.where(present_rows, results[:, :WIDTH], 0).reshape(tokens.shape)
    up_sum = jnp.concatenate([mlp_sum[:48], mlp_sum[48:96]], axis=1).reshape(2, 24, UP)
    sums = jnp.concatenate([attn_sum.astype(BF16), up_sum.astype(BF16)], axis=2)
    sums = sums.reshape(8, 6, ATTN + UP)
    got = lax.all_to_all(sums, EIGHT, 0, 0, tiled=True)
    down_parts = ring_split(mlp_sum[96:].astype(BF16), z_at)
    down_sum = ring_total(down_parts, after(ring_sent(down_parts, "z"), got))
    out_qkv, out_out, out_up, out_down, grad_tokens, *vecs, out_up_b = call(
        outputs_kernel,
        None,
        (got, down_sum, results[:, WIDTH:]),
        (
            ((6, 3 * WIDTH), F32),
            ((6, WIDTH), F32),
            ((6, FF), F32),
            ((24, WIDTH), F32),
            ((OWN, WIDTH), BF16),
        )
        + (((6,), F32),) * 8
        + (((24,), F32),),
        (((128, 128), F32),),
        8 * 1024 * 1024,
    )
    gain_1, bias_1, bias_q, bias_v, bias_out, gain_2, bias_2, bias_down = vecs
    return (
        block_out,
        grad_tokens.reshape(tokens.shape),
        gain_1,
        bias_1,
        out_qkv,
        bias_q,
        bias_v,
        out_out,
        bias_out,
        gain_2,
        bias_2,
        out_up,
        out_up_b,
        out_down,
        bias_down,
    )


def solution(mesh):
    torus = Mesh(np.asarray(mesh.devices).reshape(SIZES), AXES)
    items = P(("x", "yh", "z", "c"), None, "yl", None)
    part, rows = P(AXES), P(AXES, None)
    return jax.shard_map(
        shards,
        mesh=torus,
        in_specs=(
            items, P(("x", "yh", "z", "c")), part, part, rows, part, part, rows, part, part, part, rows, part, rows,
            part, items,
        ),
        out_specs=(
            items, items, part, part, rows, part, part, rows, part, part, part, rows, part, rows, part,
        ),
        check_vma=False,
    )
```

```python
import jax
import jax.numpy as jnp
import numpy as np
from jax import lax
from jax.experimental import pallas as pl
from jax.experimental.pallas import tpu as pltpu
from jax.sharding import Mesh
from jax.sharding import PartitionSpec as P

WIDTH = 768
HEAD = 64
NSUM = 16
SLOTS = 4
SEGLEN = 64
HALFSEG = 32
FF = 3072

EPSILON = 1e-05
MASKED = -1e30
SCALE = HEAD ** (-0.5)

AXES = ("x", "yh", "z", "c", "yl")
SIZES = (4, 2, 4, 2, 2)
QUAD_AXES = ("x", "yh", "z")
QUADS = 32
DEVICES = 128
ROWS = 256
OWN = 128
HALF = WIDTH // 2
QKV = 3 * HALF
UP = FF // 2
SMALL = 128
ATTN = QKV + SMALL + HALF
BLOCK = WIDTH // 4
DOWN_ROWS = UP // 4
RING_Y = ("yh", "yl")
EIGHT = ("yh", "c", "yl")
VMEM_LIMIT = 60 * 1024 * 1024

F32 = jnp.float32
BF16 = jnp.bfloat16


def dot_nn(left, right):
    return jnp.dot(left, right, preferred_element_type=F32)


def dot_tn(left, right):
    return lax.dot_general(left, right, (((0,), (0,)), ((), ())), preferred_element_type=F32)


def dot_nt(left, right):
    return lax.dot_general(left, right, (((1,), (1,)), ((), ())), preferred_element_type=F32)


def normalised(values):
    center = values - jnp.mean(values, axis=-1, keepdims=True)
    spread = jnp.mean(center * center, axis=-1, keepdims=True)
    scale = lax.rsqrt(spread + EPSILON)
    return center * scale, scale


def norm_back(grad, unit, scale, gain):
    inner = grad * gain
    mean = jnp.mean(inner, axis=-1, keepdims=True)
    along = jnp.mean(inner * unit, axis=-1, keepdims=True)
    return scale * (inner - mean - unit * along)


def total(values):
    return jnp.sum(values.astype(F32), axis=0, keepdims=True)


def swap_halves(values):
    return jnp.concatenate([values[OWN:], values[:OWN]], axis=0)


def masks(core):
    def place(dim):
        row = lax.broadcasted_iota(jnp.int32, (ROWS, ROWS), dim)
        second = (row >= OWN).astype(jnp.int32)
        inner = row - second * OWN
        half = core + second - 2 * core * second
        slot = inner // HALFSEG
        return slot, half * HALFSEG + inner - slot * HALFSEG

    query_slot, query_pos = place(0)
    key_slot, key_pos = place(1)
    same = (query_slot == key_slot) & (key_pos <= query_pos)
    earlier = (key_slot < query_slot) & (key_pos >= SEGLEN - NSUM)
    return same | earlier, key_slot >= query_slot - 2


def bring(copies, sems):
    started = [pltpu.make_async_copy(src, dst, sems.at[i]) for i, (src, dst) in enumerate(copies)]
    for copy in started:
        copy.start()
    return [copy.wait for copy in started]


def finish(waits):
    for wait in waits:
        wait()


def row_block(at, size):
    return pl.ds(pl.multiple_of(at * size, 64), size)


def positions(core, at):
    way = 1 - 2 * core
    return at, lax.rem(at + 4 - way, 4), lax.rem(at + 4 + way, 4), lax.rem(at + 2, 4)


def head_lanes(j):
    lane = lax.broadcasted_iota(jnp.int32, (1, 2 * HEAD), 1)
    return jnp.where(lane // HEAD == j, 1.0, 0.0).astype(BF16)


def up_runs(t):
    for yh, yl, x, z in np.ndindex(2, 2, 4, 4):
        yield 96 * ((x * 2 + yh) * 4 + z) + 48 * t + 24 * yl, 24 * (((yh * 2 + yl) * 4 + x) * 4 + z)


def halves_kernel(qkv_ref, out_ref, up_ref, *refs):
    *vec_refs, up_b_ref, parts_ref, rows_ref, wide_ref, half_ref = refs
    rows_ref[...] = jnp.zeros((16, 128), F32)
    for v, ref in enumerate(vec_refs):
        rows_ref[v : v + 1, 0:6] = ref[...].astype(F32).reshape(1, 6)
    rows_ref[8:9, 0:24] = up_b_ref[...].astype(F32).reshape(1, 24)
    row = lax.broadcasted_iota(jnp.int32, (8, 128), 0)
    lane = lax.broadcasted_iota(jnp.int32, (8, 128), 1)
    src = lax.broadcasted_iota(jnp.int32, (128, 128), 0)
    col = lax.broadcasted_iota(jnp.int32, (128, 128), 1)
    one = jnp.where(row == lane, 1.0, 0.0).astype(BF16)
    vecs = jnp.concatenate([rows_ref[0:8, :].astype(BF16), jnp.zeros((120, 128), BF16)], axis=0)
    up_b = jnp.where(lane // 4 == row, jnp.broadcast_to(rows_ref[8:9, :], (8, 128)), 0.0).astype(BF16)
    put = jnp.where((src < 24) & (8 + lax.rem(src, 4) == col), 1.0, 0.0).astype(BF16)
    small = (dot_nt(one, vecs) + dot_nn(up_b, put)).astype(BF16)
    wide_ref[...] = up_ref[...].astype(F32)
    for t in range(2):
        for src, to in up_runs(t):
            half_ref[:, to : to + 24] = wide_ref[:, src : src + 24]
        up = half_ref[...].astype(BF16)
        for at in (2 * t, 2 * t + 1, 2 * t + 4, 2 * t + 5):
            for j in range(3):
                parts_ref[at, :, j * HALF : (j + 1) * HALF] = qkv_ref[:, j * WIDTH + t * HALF : j * WIDTH + (t + 1) * HALF]
            parts_ref[at, :, QKV : QKV + SMALL] = small[:6]
            parts_ref[at, :, QKV + SMALL : ATTN] = out_ref[:, t * HALF : (t + 1) * HALF]
            parts_ref[at, :, ATTN:] = up


def outputs_kernel(
    got_ref, down_ref, tokens_ref,
    qkv_ref, out_ref, up_ref, out_down_ref, out_tokens_ref, *refs,
):
    *vec_refs, up_b_ref, rows_ref = refs
    out_down_ref[...] = down_ref[...]
    out_tokens_ref[...] = tokens_ref[...]
    small = jnp.zeros((6, SMALL), F32)
    for t in range(2):
        rows = [got_ref[at].astype(F32) for at in (2 * t, 2 * t + 1, 2 * t + 4, 2 * t + 5)]
        rows = (rows[0] + rows[1]) + (rows[2] + rows[3])
        for j in range(3):
            qkv_ref[:, j * WIDTH + t * HALF : j * WIDTH + (t + 1) * HALF] = rows[:, j * HALF : (j + 1) * HALF]
        small += rows[:, QKV : QKV + SMALL]
        out_ref[:, t * HALF : (t + 1) * HALF] = rows[:, QKV + SMALL : ATTN]
        for to, src in up_runs(t):
            up_ref[:, to : to + 24] = rows[:, ATTN + src : ATTN + src + 24]
    small = small[:, 0:12] + small[:, 16:28]
    rows_ref[...] = jnp.zeros((128, 128), F32)
    rows_ref[0:6, 0:12] = small
    flipped = rows_ref[...].T
    for v, ref in enumerate(vec_refs):
        ref[...] = flipped[v : v + 1, 0:6].reshape(6)
    up_b_ref[...] = jnp.concatenate([small[j : j + 1, 8:12] for j in range(6)], axis=1).reshape(24)


def attend_kernel(
    place_ref, x_ref, part_0, part_1, part_2, part_3,
    a_ref, qkv_ref, o_ref, lse_ref, w_ref, out_ref, small_ref, vec_ref,
):
    core = place_ref[0]
    for part, at in zip((part_0, part_1, part_2, part_3), positions(core, place_ref[1])):
        rows = pl.ds(pl.multiple_of(at * BLOCK, 64), BLOCK)
        w_ref[rows, :] = part[:, pl.ds(0, QKV)]
        small_ref[rows, :] = part[:, pl.ds(QKV, SMALL)]
        out_ref[rows, :] = part[:, pl.ds(QKV + SMALL, HALF)]
    vec_ref[...] = small_ref[...].astype(F32).T[:16]
    unit, _ = normalised(x_ref[...].astype(F32))
    a = (unit * vec_ref[0:1, :] + vec_ref[1:2, :]).astype(BF16)
    a_ref[...] = a
    here = pl.ds(pl.multiple_of(core * HALF, 128), HALF)
    shift = jnp.concatenate([vec_ref[2:3, here], jnp.zeros((1, HALF), F32), vec_ref[3:4, here]], axis=1)
    qkv_ref[...] = (dot_nn(a, w_ref[...]) + shift).astype(BF16)
    admitted, _ = masks(core)
    lane = lax.broadcasted_iota(jnp.int32, (ROWS, 128), 1)
    kept = jnp.zeros((ROWS, 128), F32)
    for pair in range(3):
        lanes = pl.ds(128 * pair, 128)
        query = qkv_ref[:, lanes]
        key = qkv_ref[:, pl.ds(HALF + 128 * pair, 128)]
        value = qkv_ref[:, pl.ds(2 * HALF + 128 * pair, 128)]
        out = jnp.zeros((ROWS, 128), F32)
        for j in range(2):
            only = head_lanes(j)
            scores = jnp.where(admitted, dot_nt(query * only, key) * SCALE, MASKED)
            top = jnp.max(scores, axis=-1, keepdims=True)
            grown = jnp.exp(scores - top)
            amount = jnp.sum(grown, axis=-1, keepdims=True)
            kept = jnp.where(lane == 2 * pair + j, top + jnp.log(amount), kept)
            probs = (grown * (1.0 / amount)).astype(BF16)
            out += dot_nn(probs, value * only)
        o_ref[:, lanes] = out.astype(BF16)
    lse_ref[...] = kept


def whole_copies(core, own_o, far_o, own_out, far_out, o_ref, out_ref):
    here = pl.ds(pl.multiple_of(core * HALF, 128), HALF)
    there = pl.ds(pl.multiple_of((1 - core) * HALF, 128), HALF)
    return [
        (own_o, o_ref.at[:, here]),
        (far_o.at[pl.ds(0, OWN)], o_ref.at[pl.ds(OWN, OWN), there]),
        (far_o.at[pl.ds(OWN, OWN)], o_ref.at[pl.ds(0, OWN), there]),
        (own_out, out_ref.at[:, here]),
        (far_out, out_ref.at[:, there]),
    ]


def mlp_kernel(
    place_ref, vec_ref, up_b_ref, x_hbm, own_o, far_o, own_out, far_out, g_hbm, order_hbm,
    up_0, up_1, up_2, up_3, down_0, down_1, down_2, down_3,
    h_ref, m_own_ref, m_far_ref, grad_a_ref, grad_up_b_ref, grad_down_b_ref,
    gup_0, gup_1, gup_2, gup_3, gdown_0, gdown_1, gdown_2, gdown_3,
    o_ref, out_ref, x_ref, g_ref, order_ref, up_ref, down_ref, grad_up_ref, grad_down_ref, sems, out_sems,
):
    core = place_ref[0]
    ups = list(zip((up_0, up_1, up_2, up_3), (gup_0, gup_1, gup_2, gup_3), positions(core, place_ref[3])))
    downs = list(zip((down_0, down_1, down_2, down_3), (gdown_0, gdown_1, gdown_2, gdown_3)))
    units = [pl.ds(pl.multiple_of(at * DOWN_ROWS, 128), DOWN_ROWS) for at in positions(core, place_ref[2])]
    pieces = [pl.ds(0, DOWN_ROWS), pl.ds(DOWN_ROWS, DOWN_ROWS)]
    copies = whole_copies(core, own_o, far_o, own_out, far_out, o_ref, out_ref)
    copies += [(x_hbm, x_ref), (order_hbm, order_ref)]
    for half in range(2):
        for e in range(2):
            unit = units[2 * half + e]
            copies += [(up.at[:, unit], up_ref.at[half, row_block(at, BLOCK), pieces[e]]) for up, _, at in ups]
        if half == 0:
            copies += [(g_hbm, g_ref)]
        copies += [(downs[2 * half + e][0], down_ref.at[half, pieces[e]]) for e in range(2)]
    waits = bring(copies, sems)
    finish(waits[:6])
    hidden = x_ref[...].astype(F32) + (dot_nn(o_ref[...], out_ref[...]) + vec_ref[4:5, :])
    h_ref[...] = hidden
    unit, _ = normalised(hidden)
    a = (unit * vec_ref[5:6, :] + vec_ref[6:7, :]).astype(BF16)
    finish(waits[6:7])
    a = dot_nn(a, order_ref[...]).astype(BF16)
    branch = jnp.zeros((ROWS, WIDTH), F32)
    grad_a = jnp.zeros((ROWS, WIDTH), F32)
    out_waits = []
    for half in range(2):
        finish(waits[7:18] if half == 0 else waits[18:])
        g = g_ref[...]
        up = up_ref[half]
        down = down_ref[half]
        first, second = units[2 * half], units[2 * half + 1]
        u = dot_nn(a, up) + jnp.concatenate([up_b_ref[:, first], up_b_ref[:, second]], axis=1)
        phi = 0.5 * (1.0 + lax.erf(u * (0.5**0.5)))
        z = (u * phi).astype(BF16)
        slope = phi + u * (jnp.exp(-0.5 * u * u) * (2.0 * jnp.pi) ** (-0.5))
        branch += dot_nn(z, down)
        gu = (dot_nt(g, down) * slope).astype(BF16)
        grad_down_ref[half] = dot_tn(z, g).astype(BF16)
        grad_up_ref[half] = dot_tn(a, gu).astype(BF16)
        copies = []
        for e in range(2):
            unit = units[2 * half + e]
            copies += [(grad_up_ref.at[half, row_block(at, BLOCK), pieces[e]], gup.at[:, unit]) for _, gup, at in ups]
            copies += [(grad_down_ref.at[half, pieces[e]], downs[2 * half + e][1])]
        out_waits += bring(copies, out_sems.at[pl.ds(10 * half, 10)])
        sums = total(gu)
        grad_up_b_ref[:, first] = sums[:, :DOWN_ROWS]
        grad_up_b_ref[:, second] = sums[:, DOWN_ROWS:]
        grad_a += dot_nt(gu, up)
    high = grad_a.astype(BF16)
    low = (grad_a - high.astype(F32)).astype(BF16)
    grad_a_ref[...] = dot_nt(high, order_ref[...]) + dot_nt(low, order_ref[...])
    m_own_ref[...] = branch[:OWN] + h_ref[0:OWN, :] + vec_ref[7:8, :]
    m_far_ref[...] = branch[OWN:]
    grad_down_b_ref[...] = total(g_ref[0:OWN, :])
    finish(out_waits)


def back_kernel(
    place_ref, x_ref, h_ref, g_ref, own_grad_ref, far_grad_ref, vec_ref, own_o_ref, far_o_ref, own_out_ref, far_out_ref,
    qkv_ref, lse_ref, a_ref, w_ref, down_b_ref, up_cols_ref,
    part_0, part_1, part_2, part_3, own_x_ref, far_x_ref, gh_ref,
    gh_low_ref, go_ref, gqkv_ref, rows_ref, message_ref,
):
    core = place_ref[0]
    here = pl.multiple_of(core * HALF, 128)
    there = pl.multiple_of((1 - core) * HALF, 128)
    rows_ref[...] = jnp.zeros((128, WIDTH), F32)
    grad_a = own_grad_ref[...] + swap_halves(far_grad_ref[...])
    unit, scale = normalised(h_ref[...])
    grad_h = g_ref[...].astype(F32) + norm_back(grad_a, unit, scale, vec_ref[5:6, :])
    gh_ref[...] = grad_h[:OWN]
    low = grad_h.astype(BF16)
    gh_low_ref[...] = low
    rows_ref[4:5, :] = total(low[:OWN])
    rows_ref[5:6, :] = total(grad_a[:OWN] * unit[:OWN])
    rows_ref[6:7, :] = total(grad_a[:OWN])
    rows_ref[7:8, :] = down_b_ref[...]
    low_here = gh_low_ref[:, pl.ds(here, HALF)]
    low_there = gh_low_ref[:, pl.ds(there, HALF)]
    rows = pl.ds(here, HALF)
    go_ref[...] = (dot_nt(low_here, own_out_ref[rows, :]) + dot_nt(low_there, far_out_ref[rows, :])).astype(BF16)
    outs = pl.ds(QKV + SMALL, HALF)
    message_ref[pl.ds(here, HALF), outs] = dot_tn(own_o_ref[...], low_here).astype(BF16)
    message_ref[pl.ds(there, HALF), outs] = dot_tn(swap_halves(far_o_ref[...]), low_here).astype(BF16)
    admitted, live = masks(core)
    live = jnp.where(live, 1.0, 0.0)
    lane = lax.broadcasted_iota(jnp.int32, (ROWS, 128), 1)
    for pair in range(3):
        query = qkv_ref[:, pl.ds(128 * pair, 128)]
        key = qkv_ref[:, pl.ds(HALF + 128 * pair, 128)]
        value = qkv_ref[:, pl.ds(2 * HALF + 128 * pair, 128)]
        go = go_ref[:, pl.ds(128 * pair, 128)]
        gq = jnp.zeros((ROWS, 128), F32)
        gk = jnp.zeros((ROWS, 128), F32)
        gv = jnp.zeros((ROWS, 128), F32)
        for j in range(2):
            only = head_lanes(j)
            lse = jnp.sum(jnp.where(lane == 2 * pair + j, lse_ref[...], 0.0), axis=-1, keepdims=True)
            scores = jnp.where(admitted, dot_nt(query * only, key) * SCALE, MASKED)
            probs = jnp.exp(scores - lse)
            grad_p = dot_nt(go * only, value)
            grad_s = probs * (grad_p - jnp.sum(probs * grad_p, axis=-1, keepdims=True))
            gq += dot_nn(grad_s.astype(BF16), key * only)
            gk += dot_tn((grad_s * live).astype(BF16), query * only)
            gv += dot_tn((probs * live).astype(BF16), go * only)
        gqkv_ref[:, pl.ds(128 * pair, 128)] = (gq * SCALE).astype(BF16)
        gqkv_ref[:, pl.ds(HALF + 128 * pair, 128)] = (gk * SCALE).astype(BF16)
        gqkv_ref[:, pl.ds(2 * HALF + 128 * pair, 128)] = gv.astype(BF16)
    gqkv = gqkv_ref[...]
    message_ref[:, pl.ds(0, QKV)] = dot_tn(a_ref[...], gqkv).astype(BF16)
    grad_x = dot_nt(gqkv, w_ref[...])
    own_x_ref[...] = grad_x[:OWN]
    far_x_ref[...] = grad_x[OWN:]
    unit, _ = normalised(x_ref[...].astype(F32))
    sums = total(gqkv)
    rows_ref[0:1, :] = total(grad_x * unit)
    rows_ref[1:2, :] = total(grad_x)
    rows_ref[2:3, pl.ds(here, HALF)] = sums[:, :HALF]
    rows_ref[3:4, pl.ds(here, HALF)] = sums[:, 2 * HALF :]
    full = rows_ref[0:8, :]
    high = full.astype(BF16).astype(F32)
    rows_ref[0:8, :] = high
    rows_ref[16:24, :] = full - high
    message_ref[:, pl.ds(QKV, SMALL)] = (rows_ref[...].T + up_cols_ref[...]).astype(BF16)
    for part, at in zip((part_0, part_1, part_2, part_3), positions(core, place_ref[1])):
        part[...] = message_ref[pl.ds(pl.multiple_of(at * BLOCK, 64), BLOCK), :]


def tokens_kernel(place_ref, x_ref, own_x_ref, far_x_ref, gh_ref, vec_ref, out_ref):
    unit, scale = normalised(x_ref[0:OWN, :].astype(F32))
    grad = own_x_ref[...] + far_x_ref[...]
    out_ref[...] = (gh_ref[...] + norm_back(grad, unit, scale, vec_ref[0:1, :])).astype(BF16)


VMEM, ANY = pltpu.VMEM, pl.ANY


def call(kernel, place, args, outs, scratch=(), sems=(), in_any=None, out_any=(), limit=VMEM_LIMIT):
    specs = [pl.BlockSpec(memory_space=ANY if in_any is not None and i >= in_any else VMEM) for i in range(len(args))]
    if place is not None:
        args = (place,) + tuple(args)
        specs = [pl.BlockSpec(memory_space=pltpu.SMEM)] + specs
    return pl.pallas_call(
        kernel,
        out_shape=tuple(jax.ShapeDtypeStruct(s, d) for s, d in outs),
        in_specs=specs,
        out_specs=tuple(pl.BlockSpec(memory_space=ANY if i in out_any else VMEM) for i in range(len(outs))),
        scratch_shapes=[VMEM(s, d) for s, d in scratch] + [pltpu.SemaphoreType.DMA((n,)) for n in sems],
        compiler_params=pltpu.CompilerParams(vmem_limit_bytes=limit),
        cost_estimate=pl.CostEstimate(flops=1, bytes_accessed=1, transcendentals=0),
    )(*args)


def between_cores(values):
    return lax.ppermute(values, "c", [(0, 1), (1, 0)])


def between_chips(values):
    return lax.ppermute(values, "yl", [(0, 1), (1, 0)])


def swap_items(values):
    return lax.ppermute(values, ("c", "yl"), [(0, 0), (1, 2), (2, 1), (3, 3)])


def up_order():
    u = lax.optimization_barrier(jnp.arange(WIDTH, dtype=jnp.int32))
    z, x, yh, i = u // BLOCK, u % BLOCK // 48, u % 48 // 24, u % 24
    n = ((x * 2 + yh) * 4 + z) * 24 + i
    return (n[None, :] == lax.broadcasted_iota(jnp.int32, (WIDTH, WIDTH), 0)).astype(BF16)


def ring(values, axis, by):
    return lax.ppermute(values, axis, [(i, (i + by) % 4) for i in range(4)])


def ring_gather(block, axis):
    return [block, ring(block, axis, -1), ring(block, axis, 2), ring(block, axis, 1)]


def ring_order(blocks, at):
    return [lax.select_n(lax.rem(j - at + 4, 4), *blocks) for j in range(4)]


def ring_sent(blocks, axis):
    return [ring(blocks[1], axis, 1), ring(blocks[2], axis, 2), ring(blocks[3], axis, -1)]


def ring_total(blocks, got):
    return sum((g.astype(F32) for g in got), blocks[0].astype(F32))


def ring_reduce(blocks, axis):
    return ring_total(blocks, ring_sent(blocks, axis))


def ring_split(values, at, axis=0):
    size = values.shape[axis] // 4
    return [lax.dynamic_slice_in_dim(values, lax.rem(at + j, 4) * size, size, axis) for j in range(4)]


def along(axis, by):
    pairs = []
    for x, yh, z, c, yl in np.ndindex(*SIZES):
        at = {"x": x, "y": 2 * yh + yl, "z": z}
        at[axis] = (at[axis] + (by if c == 0 else -by)) % 4
        to = (at["x"], at["y"] // 2, at["z"], c, at["y"] % 2)
        pairs.append((int(np.ravel_multi_index((x, yh, z, c, yl), SIZES)), int(np.ravel_multi_index(to, SIZES))))
    return pairs


def send(values, axis, by):
    return lax.ppermute(values, AXES, along(axis, by))


def relay_gather(block, axis):
    behind = send(block, axis, 1)
    return [block, behind, send(block, axis, -1), send(behind, axis, 1)]


def relay_start(blocks, axis):
    return send(blocks[3], axis, 1), send(blocks[1], axis, -1)


def relay_ahead(blocks, got):
    return (blocks[2].astype(F32) + got[0].astype(F32)).astype(BF16)


def relay_end(blocks, got, far):
    return blocks[0].astype(F32) + got[1].astype(F32) + far.astype(F32)


def after(values, *others):
    tied = lax.optimization_barrier((*values, *others))
    return list(tied[: len(values)])


def by_place(place, first, second, axis=0):
    return jnp.where(
        place == 0, jnp.concatenate([first, second], axis), jnp.concatenate([second, first], axis)
    )


def other_half(values, place):
    rows = values.shape[0] // 2
    return (
        lax.dynamic_slice_in_dim(values, (1 - place) * rows, rows, 0),
        lax.dynamic_slice_in_dim(values, place * rows, rows, 0),
    )


def shards(
    tokens,
    segment_counts,
    ln1_gain,
    ln1_bias,
    w_qkv,
    q_bias,
    v_bias,
    w_out,
    out_bias,
    ln2_gain,
    ln2_bias,
    w_up,
    up_bias,
    w_down,
    down_bias,
    cotangent,
):
    core = lax.axis_index("c")
    x_at, z_at = lax.axis_index("x"), lax.axis_index("z")
    y_at = lax.axis_index(RING_Y)
    place = jnp.stack([core, x_at, y_at, z_at]).astype(jnp.int32)
    present = jnp.arange(SLOTS) < segment_counts[0]
    present_rows = jnp.repeat(present, HALFSEG)[:, None]
    cot = jnp.where(present_rows, cotangent.reshape(OWN, WIDTH), 0).astype(BF16)

    mine = swap_items(jnp.concatenate([tokens.reshape(OWN, WIDTH), cot], axis=1))
    (parts,) = call(
        halves_kernel,
        None,
        (
            w_qkv, w_out, w_up, ln1_gain, ln1_bias, q_bias, v_bias, out_bias, ln2_gain, ln2_bias, down_bias, up_bias,
        ),
        (((8, 6, ATTN + UP), BF16),),
        (((16, 128), F32), ((6, FF), F32), ((6, UP), F32)),
    )
    rows = lax.all_to_all(parts, EIGHT, 0, 0, tiled=True)
    rows = rows.reshape(2, 24, ATTN + UP)
    attn, ups = rows[:, :, :ATTN], rows[:, :, ATTN:].reshape(48, UP)

    attn = ring_gather(attn, "z")
    ups = ring_gather(ups, "x")
    (downs,) = after([w_down], *attn)
    downs = lax.all_to_all(jnp.broadcast_to(downs[None], (16, 24, WIDTH)), ("x", "z"), 0, 0, tiled=True)
    item = jnp.concatenate([mine, between_cores(mine)], axis=0)
    x, g = item[:, :WIDTH], item[:, WIDTH:]
    attn = jnp.concatenate(ring_order(attn, z_at), axis=1).reshape(BLOCK, ATTN)
    ups = jnp.concatenate(ring_order(ups, x_at), axis=0)

    attn = relay_gather(attn, "x")
    ups = relay_gather(ups, "z")
    (downs,) = after([downs.reshape(DOWN_ROWS, WIDTH)], attn[1])
    downs = relay_gather(downs, "y")

    order = up_order()
    (x,) = after([x], order)
    a1, qkv, own_o, lse, w_in, own_out, small_all, vectors = call(
        attend_kernel,
        place,
        (x, *attn),
        (
            ((ROWS, WIDTH), BF16),
            ((ROWS, QKV), BF16),
            ((ROWS, HALF), BF16),
            ((ROWS, 128), F32),
            ((WIDTH, QKV), BF16),
            ((WIDTH, HALF), BF16),
            ((WIDTH, SMALL), BF16),
            ((16, WIDTH), F32),
        ),
    )
    far_o, far_out = between_cores(own_o), between_cores(own_out)
    up_b = small_all[:, 8:12].reshape(4, 2, 4, 2, 2, 24)
    up_b = lax.dynamic_index_in_dim(up_b, core, 3, keepdims=False)
    up_b = up_b.transpose(1, 3, 0, 2, 4).reshape(1, UP).astype(F32)
    hidden, m_own, m_far, grad_a_own, grad_up_b, grad_down_b, *grads = call(
        mlp_kernel,
        place,
        (vectors, up_b, x, own_o, far_o, own_out, far_out, g, order, *ups, *downs),
        (
            ((ROWS, WIDTH), F32),
            ((OWN, WIDTH), F32),
            ((OWN, WIDTH), F32),
            ((ROWS, WIDTH), F32),
            ((1, UP), F32),
            ((1, WIDTH), F32),
        )
        + (((BLOCK, UP), BF16),) * 4
        + (((DOWN_ROWS, WIDTH), BF16),) * 4,
        (
            ((ROWS, WIDTH), BF16),
            ((WIDTH, WIDTH), BF16),
            ((ROWS, WIDTH), BF16),
            ((ROWS, WIDTH), BF16),
            ((WIDTH, WIDTH), BF16),
        )
        + (((2, WIDTH, WIDTH), BF16),) * 4,
        (28, 20),
        in_any=2,
        out_any=range(6, 14),
    )
    grad_a_far = between_cores(grad_a_own)
    grad_a_far, *grads = lax.optimization_barrier((grad_a_far, *grads))
    grad_ups, grad_downs = grads[:4], grads[4:]
    got_ups, got_downs = relay_start(grad_ups, "z"), relay_start(grad_downs, "y")
    block = (m_own + between_cores(m_far)).astype(BF16)
    up_cols = grad_up_b.reshape(2, 2, 4, 4, 24).transpose(2, 0, 3, 1, 4)[:, :, :, None]
    up_cols = jnp.where((jnp.arange(2) == core)[:, None, None], up_cols, 0.0).reshape(WIDTH, 4)
    up_high = up_cols.astype(BF16).astype(F32)
    up_cols = jnp.pad(up_high, ((0, 0), (8, SMALL - 12))) + jnp.pad(up_cols - up_high, ((0, 0), (24, SMALL - 28)))

    *grad_attn, own_x, far_x, gh = call(
        back_kernel,
        place,
        (
            x, hidden, g, grad_a_own, grad_a_far, vectors, own_o, far_o, own_out, far_out, qkv, lse, a1, w_in,
            grad_down_b, up_cols,
        ),
        (((BLOCK, ATTN), BF16),) * 4 + (((OWN, WIDTH), F32),) * 3,
        (
            ((ROWS, WIDTH), BF16),
            ((ROWS, HALF), BF16),
            ((ROWS, QKV), BF16),
            ((128, WIDTH), F32),
            ((WIDTH, ATTN), BF16),
        ),
    )
    ups_ahead, downs_ahead = relay_ahead(grad_ups, got_ups), relay_ahead(grad_downs, got_downs)
    (far_x,) = after([between_cores(far_x)], ups_ahead, downs_ahead)
    (grad_x,) = call(tokens_kernel, place, (x, own_x, far_x, gh, vectors), (((OWN, WIDTH), BF16),))

    got_attn = relay_start(grad_attn, "x")
    got_attn = after(got_attn, grad_x, block)
    attn_ahead = relay_ahead(grad_attn, got_attn)
    far_ups, far_downs = after([send(ups_ahead, "z", 1), send(downs_ahead, "y", 1)], attn_ahead)
    up_sum = relay_end(grad_ups, got_ups, far_ups).astype(BF16)
    down_sum = relay_end(grad_downs, got_downs, far_downs).astype(BF16)
    (far_attn,) = after([send(attn_ahead, "x", 1)], up_sum, down_sum)
    up_parts = ring_split(up_sum, x_at)
    down_parts = ring_split(down_sum, x_at)
    mlp_sum = ring_reduce(
        [
            jnp.concatenate([u[:, :WIDTH], u[:, WIDTH:], d])
            for u, d in zip(up_parts, down_parts)
        ],
        "x",
    )
    attn_sum = relay_end(grad_attn, got_attn, far_attn).astype(BF16).reshape(2, 4, 24, ATTN)
    results = swap_items(after([jnp.concatenate([block, grad_x], axis=1)], attn_sum)[0])
    attn_sum = ring_reduce([a[:, 0] for a in ring_split(attn_sum, z_at, 1)], "z")
    block_out = jnp.where(present_rows, results[:, :WIDTH], 0).reshape(tokens.shape)
    up_sum = jnp.concatenate([mlp_sum[:48], mlp_sum[48:96]], axis=1).reshape(2, 24, UP)
    sums = jnp.concatenate([attn_sum.astype(BF16), up_sum.astype(BF16)], axis=2)
    sums = sums.reshape(8, 6, ATTN + UP)
    got = lax.all_to_all(sums, EIGHT, 0, 0, tiled=True)
    down_parts = ring_split(mlp_sum[96:].astype(BF16), z_at)
    down_sum = ring_total(down_parts, after(ring_sent(down_parts, "z"), got))
    out_qkv, out_out, out_up, out_down, grad_tokens, *vecs, out_up_b = call(
        outputs_kernel,
        None,
        (got, down_sum, results[:, WIDTH:]),
        (
            ((6, 3 * WIDTH), F32),
            ((6, WIDTH), F32),
            ((6, FF), F32),
            ((24, WIDTH), F32),
            ((OWN, WIDTH), BF16),
        )
        + (((6,), F32),) * 8
        + (((24,), F32),),
        (((128, 128), F32),),
        limit=8 * 1024 * 1024,
    )
    gain_1, bias_1, bias_q, bias_v, bias_out, gain_2, bias_2, bias_down = vecs
    return (
        block_out,
        grad_tokens.reshape(tokens.shape),
        gain_1,
        bias_1,
        out_qkv,
        bias_q,
        bias_v,
        out_out,
        bias_out,
        gain_2,
        bias_2,
        out_up,
        out_up_b,
        out_down,
        bias_down,
    )


def solution(mesh):
    torus = Mesh(np.asarray(mesh.devices).reshape(SIZES), AXES)
    items = P(("x", "yh", "z", "c"), None, "yl", None)
    part, rows = P(AXES), P(AXES, None)
    return jax.shard_map(
        shards,
        mesh=torus,
        in_specs=(
            items, P(("x", "yh", "z", "c")), part, part, rows, part, part, rows, part, part, part, rows, part, rows,
            part, items,
        ),
        out_specs=(
            items, items, part, part, rows, part, part, rows, part, part, part, rows, part, rows, part,
        ),
        check_vma=False,
    )
```

```python
import jax
import jax.numpy as jnp
import numpy as np
from jax import lax
from jax.experimental import pallas as pl
from jax.experimental.pallas import tpu as pltpu
from jax.sharding import Mesh
from jax.sharding import PartitionSpec as P

WIDTH = 768
HEAD = 64
NSUM = 16
SLOTS = 4
SEGLEN = 64
HALFSEG = 32
FF = 3072

EPSILON = 1e-05
MASKED = -1e30
SCALE = HEAD ** (-0.5)

AXES = ("x", "yh", "z", "c", "yl")
SIZES = (4, 2, 4, 2, 2)
QUAD_AXES = ("x", "yh", "z")
QUADS = 32
DEVICES = 128
ROWS = 256
OWN = 128
HALF = WIDTH // 2
QKV = 3 * HALF
UP = FF // 2
SMALL = 128
ATTN = QKV + SMALL + HALF
BLOCK = WIDTH // 4
DOWN_ROWS = UP // 4
RING_Y = ("yh", "yl")
EIGHT = ("yh", "c", "yl")
VMEM_LIMIT = 60 * 1024 * 1024

F32 = jnp.float32
BF16 = jnp.bfloat16


def dot_nn(left, right):
    return jnp.dot(left, right, preferred_element_type=F32)


def dot_tn(left, right):
    return lax.dot_general(left, right, (((0,), (0,)), ((), ())), preferred_element_type=F32)


def dot_nt(left, right):
    return lax.dot_general(left, right, (((1,), (1,)), ((), ())), preferred_element_type=F32)


def normalised(values):
    center = values - jnp.mean(values, axis=-1, keepdims=True)
    spread = jnp.mean(center * center, axis=-1, keepdims=True)
    scale = lax.rsqrt(spread + EPSILON)
    return center * scale, scale


def norm_back(grad, unit, scale, gain):
    inner = grad * gain
    mean = jnp.mean(inner, axis=-1, keepdims=True)
    along = jnp.mean(inner * unit, axis=-1, keepdims=True)
    return scale * (inner - mean - unit * along)


def total(values):
    return jnp.sum(values.astype(F32), axis=0, keepdims=True)


def swap_halves(values):
    return jnp.concatenate([values[OWN:], values[:OWN]], axis=0)


def masks(core):
    def place(dim):
        row = lax.broadcasted_iota(jnp.int32, (ROWS, ROWS), dim)
        second = (row >= OWN).astype(jnp.int32)
        inner = row - second * OWN
        half = core + second - 2 * core * second
        slot = inner // HALFSEG
        return slot, half * HALFSEG + inner - slot * HALFSEG

    query_slot, query_pos = place(0)
    key_slot, key_pos = place(1)
    same = (query_slot == key_slot) & (key_pos <= query_pos)
    earlier = (key_slot < query_slot) & (key_pos >= SEGLEN - NSUM)
    return same | earlier, key_slot >= query_slot - 2


def bring(copies, sems):
    started = [pltpu.make_async_copy(src, dst, sems.at[i]) for i, (src, dst) in enumerate(copies)]
    for copy in started:
        copy.start()
    return [copy.wait for copy in started]


def finish(waits):
    for wait in waits:
        wait()


def row_block(at, size):
    return pl.ds(pl.multiple_of(at * size, 64), size)


def positions(core, at):
    way = 1 - 2 * core
    return at, lax.rem(at + 4 - way, 4), lax.rem(at + 4 + way, 4), lax.rem(at + 2, 4)


def head_lanes(j):
    lane = lax.broadcasted_iota(jnp.int32, (1, 2 * HEAD), 1)
    return jnp.where(lane // HEAD == j, 1.0, 0.0).astype(BF16)


def up_runs(t):
    for yh, yl, x, z in np.ndindex(2, 2, 4, 4):
        yield 96 * ((x * 2 + yh) * 4 + z) + 48 * t + 24 * yl, 24 * (((yh * 2 + yl) * 4 + x) * 4 + z)


def halves_kernel(qkv_ref, out_ref, up_ref, *refs):
    *vec_refs, up_b_ref, parts_ref, rows_ref, wide_ref, half_ref = refs
    rows_ref[...] = jnp.zeros((16, 128), F32)
    for v, ref in enumerate(vec_refs):
        rows_ref[v : v + 1, 0:6] = ref[...].astype(F32).reshape(1, 6)
    rows_ref[8:9, 0:24] = up_b_ref[...].astype(F32).reshape(1, 24)
    row = lax.broadcasted_iota(jnp.int32, (8, 128), 0)
    lane = lax.broadcasted_iota(jnp.int32, (8, 128), 1)
    src = lax.broadcasted_iota(jnp.int32, (128, 128), 0)
    col = lax.broadcasted_iota(jnp.int32, (128, 128), 1)
    one = jnp.where(row == lane, 1.0, 0.0).astype(BF16)
    vecs = jnp.concatenate([rows_ref[0:8, :].astype(BF16), jnp.zeros((120, 128), BF16)], axis=0)
    up_b = jnp.where(lane // 4 == row, jnp.broadcast_to(rows_ref[8:9, :], (8, 128)), 0.0).astype(BF16)
    put = jnp.where((src < 24) & (8 + lax.rem(src, 4) == col), 1.0, 0.0).astype(BF16)
    small = (dot_nt(one, vecs) + dot_nn(up_b, put)).astype(BF16)
    wide_ref[...] = up_ref[...].astype(F32)
    for t in range(2):
        for src, to in up_runs(t):
            half_ref[:, to : to + 24] = wide_ref[:, src : src + 24]
        up = half_ref[...].astype(BF16)
        for at in (2 * t, 2 * t + 1, 2 * t + 4, 2 * t + 5):
            for j in range(3):
                parts_ref[at, :, j * HALF : (j + 1) * HALF] = qkv_ref[:, j * WIDTH + t * HALF : j * WIDTH + (t + 1) * HALF]
            parts_ref[at, :, QKV : QKV + SMALL] = small[:6]
            parts_ref[at, :, QKV + SMALL : ATTN] = out_ref[:, t * HALF : (t + 1) * HALF]
            parts_ref[at, :, ATTN:] = up


def outputs_kernel(
    got_ref, down_ref, tokens_ref,
    qkv_ref, out_ref, up_ref, out_down_ref, out_tokens_ref, *refs,
):
    *vec_refs, up_b_ref, rows_ref = refs
    out_down_ref[...] = down_ref[...]
    out_tokens_ref[...] = tokens_ref[...]
    small = jnp.zeros((6, SMALL), F32)
    for t in range(2):
        rows = [got_ref[at].astype(F32) for at in (2 * t, 2 * t + 1, 2 * t + 4, 2 * t + 5)]
        rows = (rows[0] + rows[1]) + (rows[2] + rows[3])
        for j in range(3):
            qkv_ref[:, j * WIDTH + t * HALF : j * WIDTH + (t + 1) * HALF] = rows[:, j * HALF : (j + 1) * HALF]
        small += rows[:, QKV : QKV + SMALL]
        out_ref[:, t * HALF : (t + 1) * HALF] = rows[:, QKV + SMALL : ATTN]
        for to, src in up_runs(t):
            up_ref[:, to : to + 24] = rows[:, ATTN + src : ATTN + src + 24]
    small = small[:, 0:12] + small[:, 16:28]
    rows_ref[...] = jnp.zeros((128, 128), F32)
    rows_ref[0:6, 0:12] = small
    flipped = rows_ref[...].T
    for v, ref in enumerate(vec_refs):
        ref[...] = flipped[v : v + 1, 0:6].reshape(6)
    up_b_ref[...] = jnp.concatenate([small[j : j + 1, 8:12] for j in range(6)], axis=1).reshape(24)


def attend_kernel(
    place_ref, x_ref, part_0, part_1, part_2, part_3,
    a_ref, qkv_ref, o_ref, lse_ref, w_ref, out_ref, small_ref, vec_ref,
):
    core = place_ref[0]
    for part, at in zip((part_0, part_1, part_2, part_3), positions(core, place_ref[1])):
        rows = pl.ds(pl.multiple_of(at * BLOCK, 64), BLOCK)
        w_ref[rows, :] = part[:, pl.ds(0, QKV)]
        small_ref[rows, :] = part[:, pl.ds(QKV, SMALL)]
        out_ref[rows, :] = part[:, pl.ds(QKV + SMALL, HALF)]
    vec_ref[...] = small_ref[...].astype(F32).T[:16]
    unit, _ = normalised(x_ref[...].astype(F32))
    a = (unit * vec_ref[0:1, :] + vec_ref[1:2, :]).astype(BF16)
    a_ref[...] = a
    here = pl.ds(pl.multiple_of(core * HALF, 128), HALF)
    shift = jnp.concatenate([vec_ref[2:3, here], jnp.zeros((1, HALF), F32), vec_ref[3:4, here]], axis=1)
    qkv_ref[...] = (dot_nn(a, w_ref[...]) + shift).astype(BF16)
    admitted, _ = masks(core)
    lane = lax.broadcasted_iota(jnp.int32, (ROWS, 128), 1)
    kept = jnp.zeros((ROWS, 128), F32)
    for pair in range(3):
        lanes = pl.ds(128 * pair, 128)
        query = qkv_ref[:, lanes]
        key = qkv_ref[:, pl.ds(HALF + 128 * pair, 128)]
        value = qkv_ref[:, pl.ds(2 * HALF + 128 * pair, 128)]
        out = jnp.zeros((ROWS, 128), F32)
        for j in range(2):
            only = head_lanes(j)
            scores = jnp.where(admitted, dot_nt(query * only, key) * SCALE, MASKED)
            top = jnp.max(scores, axis=-1, keepdims=True)
            grown = jnp.exp(scores - top)
            amount = jnp.sum(grown, axis=-1, keepdims=True)
            kept = jnp.where(lane == 2 * pair + j, top + jnp.log(amount), kept)
            probs = (grown * (1.0 / amount)).astype(BF16)
            out += dot_nn(probs, value * only)
        o_ref[:, lanes] = out.astype(BF16)
    lse_ref[...] = kept


def whole_copies(core, own_o, far_o, own_out, far_out, o_ref, out_ref):
    here = pl.ds(pl.multiple_of(core * HALF, 128), HALF)
    there = pl.ds(pl.multiple_of((1 - core) * HALF, 128), HALF)
    return [
        (own_o, o_ref.at[:, here]),
        (far_o.at[pl.ds(0, OWN)], o_ref.at[pl.ds(OWN, OWN), there]),
        (far_o.at[pl.ds(OWN, OWN)], o_ref.at[pl.ds(0, OWN), there]),
        (own_out, out_ref.at[:, here]),
        (far_out, out_ref.at[:, there]),
    ]


def mlp_kernel(
    place_ref, vec_ref, up_b_ref, x_hbm, own_o, far_o, own_out, far_out, g_hbm, order_hbm,
    up_0, up_1, up_2, up_3, down_0, down_1, down_2, down_3,
    h_ref, m_own_ref, m_far_ref, grad_a_ref, grad_up_b_ref, grad_down_b_ref,
    gup_0, gup_1, gup_2, gup_3, gdown_0, gdown_1, gdown_2, gdown_3,
    o_ref, out_ref, x_ref, g_ref, order_ref, up_ref, down_ref, grad_up_ref, grad_down_ref, sems, out_sems,
):
    core = place_ref[0]
    ups = list(zip((up_0, up_1, up_2, up_3), (gup_0, gup_1, gup_2, gup_3), positions(core, place_ref[3])))
    downs = list(zip((down_0, down_1, down_2, down_3), (gdown_0, gdown_1, gdown_2, gdown_3)))
    units = [pl.ds(pl.multiple_of(at * DOWN_ROWS, 128), DOWN_ROWS) for at in positions(core, place_ref[2])]
    pieces = [pl.ds(0, DOWN_ROWS), pl.ds(DOWN_ROWS, DOWN_ROWS)]
    copies = whole_copies(core, own_o, far_o, own_out, far_out, o_ref, out_ref)
    copies += [(x_hbm, x_ref), (order_hbm, order_ref)]
    for half in range(2):
        for e in range(2):
            unit = units[2 * half + e]
            copies += [(up.at[:, unit], up_ref.at[half, row_block(at, BLOCK), pieces[e]]) for up, _, at in ups]
        if half == 0:
            copies += [(g_hbm, g_ref)]
        copies += [(downs[2 * half + e][0], down_ref.at[half, pieces[e]]) for e in range(2)]
    waits = bring(copies, sems)
    finish(waits[:6])
    hidden = x_ref[...].astype(F32) + (dot_nn(o_ref[...], out_ref[...]) + vec_ref[4:5, :])
    h_ref[...] = hidden
    unit, _ = normalised(hidden)
    a = (unit * vec_ref[5:6, :] + vec_ref[6:7, :]).astype(BF16)
    finish(waits[6:7])
    a = dot_nn(a, order_ref[...]).astype(BF16)
    branch = jnp.zeros((ROWS, WIDTH), F32)
    grad_a = jnp.zeros((ROWS, WIDTH), F32)
    out_waits = []
    for half in range(2):
        finish(waits[7:18] if half == 0 else waits[18:])
        g = g_ref[...]
        up = up_ref[half]
        down = down_ref[half]
        first, second = units[2 * half], units[2 * half + 1]
        u = dot_nn(a, up) + jnp.concatenate([up_b_ref[:, first], up_b_ref[:, second]], axis=1)
        phi = 0.5 * (1.0 + lax.erf(u * (0.5**0.5)))
        z = (u * phi).astype(BF16)
        slope = phi + u * (jnp.exp(-0.5 * u * u) * (2.0 * jnp.pi) ** (-0.5))
        branch += dot_nn(z, down)
        gu = (dot_nt(g, down) * slope).astype(BF16)
        grad_down_ref[half] = dot_tn(z, g).astype(BF16)
        grad_up_ref[half] = dot_tn(a, gu).astype(BF16)
        copies = []
        for e in range(2):
            unit = units[2 * half + e]
            copies += [(grad_up_ref.at[half, row_block(at, BLOCK), pieces[e]], gup.at[:, unit]) for _, gup, at in ups]
            copies += [(grad_down_ref.at[half, pieces[e]], downs[2 * half + e][1])]
        out_waits += bring(copies, out_sems.at[pl.ds(10 * half, 10)])
        sums = total(gu)
        grad_up_b_ref[:, first] = sums[:, :DOWN_ROWS]
        grad_up_b_ref[:, second] = sums[:, DOWN_ROWS:]
        grad_a += dot_nt(gu, up)
    high = grad_a.astype(BF16)
    low = (grad_a - high.astype(F32)).astype(BF16)
    grad_a_ref[...] = dot_nt(high, order_ref[...]) + dot_nt(low, order_ref[...])
    m_own_ref[...] = branch[:OWN] + h_ref[0:OWN, :] + vec_ref[7:8, :]
    m_far_ref[...] = branch[OWN:]
    grad_down_b_ref[...] = total(g_ref[0:OWN, :])
    finish(out_waits)


def back_kernel(
    place_ref, x_ref, h_ref, g_ref, own_grad_ref, far_grad_ref, vec_ref, own_o_ref, far_o_ref, own_out_ref, far_out_ref,
    qkv_ref, lse_ref, a_ref, w_ref, down_b_ref, up_cols_ref,
    part_0, part_1, part_2, part_3, own_x_ref, far_x_ref, gh_ref,
    gh_low_ref, go_ref, gqkv_ref, rows_ref, message_ref,
):
    core = place_ref[0]
    here = pl.multiple_of(core * HALF, 128)
    there = pl.multiple_of((1 - core) * HALF, 128)
    rows_ref[...] = jnp.zeros((128, WIDTH), F32)
    grad_a = own_grad_ref[...] + swap_halves(far_grad_ref[...])
    unit, scale = normalised(h_ref[...])
    grad_h = g_ref[...].astype(F32) + norm_back(grad_a, unit, scale, vec_ref[5:6, :])
    gh_ref[...] = grad_h[:OWN]
    low = grad_h.astype(BF16)
    gh_low_ref[...] = low
    rows_ref[4:5, :] = total(low[:OWN])
    rows_ref[5:6, :] = total(grad_a[:OWN] * unit[:OWN])
    rows_ref[6:7, :] = total(grad_a[:OWN])
    rows_ref[7:8, :] = down_b_ref[...]
    low_here = gh_low_ref[:, pl.ds(here, HALF)]
    low_there = gh_low_ref[:, pl.ds(there, HALF)]
    rows = pl.ds(here, HALF)
    go_ref[...] = (dot_nt(low_here, own_out_ref[rows, :]) + dot_nt(low_there, far_out_ref[rows, :])).astype(BF16)
    outs = pl.ds(QKV + SMALL, HALF)
    message_ref[pl.ds(here, HALF), outs] = dot_tn(own_o_ref[...], low_here).astype(BF16)
    message_ref[pl.ds(there, HALF), outs] = dot_tn(swap_halves(far_o_ref[...]), low_here).astype(BF16)
    admitted, live = masks(core)
    live = jnp.where(live, 1.0, 0.0)
    lane = lax.broadcasted_iota(jnp.int32, (ROWS, 128), 1)
    for pair in range(3):
        query = qkv_ref[:, pl.ds(128 * pair, 128)]
        key = qkv_ref[:, pl.ds(HALF + 128 * pair, 128)]
        value = qkv_ref[:, pl.ds(2 * HALF + 128 * pair, 128)]
        go = go_ref[:, pl.ds(128 * pair, 128)]
        gq = jnp.zeros((ROWS, 128), F32)
        gk = jnp.zeros((ROWS, 128), F32)
        gv = jnp.zeros((ROWS, 128), F32)
        for j in range(2):
            only = head_lanes(j)
            lse = jnp.sum(jnp.where(lane == 2 * pair + j, lse_ref[...], 0.0), axis=-1, keepdims=True)
            scores = jnp.where(admitted, dot_nt(query * only, key) * SCALE, MASKED)
            probs = jnp.exp(scores - lse)
            grad_p = dot_nt(go * only, value)
            grad_s = probs * (grad_p - jnp.sum(probs * grad_p, axis=-1, keepdims=True))
            gq += dot_nn(grad_s.astype(BF16), key * only)
            gk += dot_tn((grad_s * live).astype(BF16), query * only)
            gv += dot_tn((probs * live).astype(BF16), go * only)
        gqkv_ref[:, pl.ds(128 * pair, 128)] = (gq * SCALE).astype(BF16)
        gqkv_ref[:, pl.ds(HALF + 128 * pair, 128)] = (gk * SCALE).astype(BF16)
        gqkv_ref[:, pl.ds(2 * HALF + 128 * pair, 128)] = gv.astype(BF16)
    gqkv = gqkv_ref[...]
    message_ref[:, pl.ds(0, QKV)] = dot_tn(a_ref[...], gqkv).astype(BF16)
    grad_x = dot_nt(gqkv, w_ref[...])
    own_x_ref[...] = grad_x[:OWN]
    far_x_ref[...] = grad_x[OWN:]
    unit, _ = normalised(x_ref[...].astype(F32))
    sums = total(gqkv)
    rows_ref[0:1, :] = total(grad_x * unit)
    rows_ref[1:2, :] = total(grad_x)
    rows_ref[2:3, pl.ds(here, HALF)] = sums[:, :HALF]
    rows_ref[3:4, pl.ds(here, HALF)] = sums[:, 2 * HALF :]
    full = rows_ref[0:8, :]
    high = full.astype(BF16).astype(F32)
    rows_ref[0:8, :] = high
    rows_ref[16:24, :] = full - high
    message_ref[:, pl.ds(QKV, SMALL)] = (rows_ref[...].T + up_cols_ref[...]).astype(BF16)
    for part, at in zip((part_0, part_1, part_2, part_3), positions(core, place_ref[1])):
        part[...] = message_ref[pl.ds(pl.multiple_of(at * BLOCK, 64), BLOCK), :]


def tokens_kernel(place_ref, x_ref, own_x_ref, far_x_ref, gh_ref, vec_ref, out_ref):
    unit, scale = normalised(x_ref[0:OWN, :].astype(F32))
    grad = own_x_ref[...] + far_x_ref[...]
    out_ref[...] = (gh_ref[...] + norm_back(grad, unit, scale, vec_ref[0:1, :])).astype(BF16)


VMEM, ANY = pltpu.VMEM, pl.ANY


def call(kernel, place, args, outs, scratch=(), sems=(), in_any=None, out_any=(), limit=VMEM_LIMIT):
    specs = [pl.BlockSpec(memory_space=ANY if in_any is not None and i >= in_any else VMEM) for i in range(len(args))]
    if place is not None:
        args = (place,) + tuple(args)
        specs = [pl.BlockSpec(memory_space=pltpu.SMEM)] + specs
    return pl.pallas_call(
        kernel,
        out_shape=tuple(jax.ShapeDtypeStruct(s, d) for s, d in outs),
        in_specs=specs,
        out_specs=tuple(pl.BlockSpec(memory_space=ANY if i in out_any else VMEM) for i in range(len(outs))),
        scratch_shapes=[VMEM(s, d) for s, d in scratch] + [pltpu.SemaphoreType.DMA((n,)) for n in sems],
        compiler_params=pltpu.CompilerParams(vmem_limit_bytes=limit),
        cost_estimate=pl.CostEstimate(flops=1, bytes_accessed=1, transcendentals=0),
    )(*args)


def between_cores(values):
    return lax.ppermute(values, "c", [(0, 1), (1, 0)])


def between_chips(values):
    return lax.ppermute(values, "yl", [(0, 1), (1, 0)])


def swap_items(values):
    return lax.ppermute(values, ("c", "yl"), [(0, 0), (1, 2), (2, 1), (3, 3)])


def up_order():
    u = lax.optimization_barrier(jnp.arange(WIDTH, dtype=jnp.int32))
    z, x, yh, i = u // BLOCK, u % BLOCK // 48, u % 48 // 24, u % 24
    n = ((x * 2 + yh) * 4 + z) * 24 + i
    return (n[None, :] == lax.broadcasted_iota(jnp.int32, (WIDTH, WIDTH), 0)).astype(BF16)


def ring(values, axis, by):
    return lax.ppermute(values, axis, [(i, (i + by) % 4) for i in range(4)])


def ring_gather(block, axis):
    return [block, ring(block, axis, -1), ring(block, axis, 2), ring(block, axis, 1)]


def ring_order(blocks, at):
    return [lax.select_n(lax.rem(j - at + 4, 4), *blocks) for j in range(4)]


def ring_sent(blocks, axis):
    return [ring(blocks[1], axis, 1), ring(blocks[2], axis, 2), ring(blocks[3], axis, -1)]


def ring_total(blocks, got):
    return sum((g.astype(F32) for g in got), blocks[0].astype(F32))


def ring_reduce(blocks, axis):
    return ring_total(blocks, ring_sent(blocks, axis))


def ring_split(values, at, axis=0):
    size = values.shape[axis] // 4
    return [lax.dynamic_slice_in_dim(values, lax.rem(at + j, 4) * size, size, axis) for j in range(4)]


def along(axis, by):
    pairs = []
    for x, yh, z, c, yl in np.ndindex(*SIZES):
        at = {"x": x, "y": 2 * yh + yl, "z": z}
        at[axis] = (at[axis] + (by if c == 0 else -by)) % 4
        to = (at["x"], at["y"] // 2, at["z"], c, at["y"] % 2)
        pairs.append((int(np.ravel_multi_index((x, yh, z, c, yl), SIZES)), int(np.ravel_multi_index(to, SIZES))))
    return pairs


def send(values, axis, by):
    return lax.ppermute(values, AXES, along(axis, by))


def relay_gather(block, axis):
    behind = send(block, axis, 1)
    return [block, behind, send(block, axis, -1), send(behind, axis, 1)]


def relay_start(blocks, axis):
    return send(blocks[3], axis, 1), send(blocks[1], axis, -1)


def relay_ahead(blocks, got):
    return (blocks[2].astype(F32) + got[0].astype(F32)).astype(BF16)


def relay_end(blocks, got, far):
    return blocks[0].astype(F32) + got[1].astype(F32) + far.astype(F32)


def after(values, *others):
    tied = lax.optimization_barrier((*values, *others))
    return list(tied[: len(values)])


def by_place(place, first, second, axis=0):
    return jnp.where(
        place == 0, jnp.concatenate([first, second], axis), jnp.concatenate([second, first], axis)
    )


def other_half(values, place):
    rows = values.shape[0] // 2
    return (
        lax.dynamic_slice_in_dim(values, (1 - place) * rows, rows, 0),
        lax.dynamic_slice_in_dim(values, place * rows, rows, 0),
    )


def shards(
    tokens,
    segment_counts,
    ln1_gain,
    ln1_bias,
    w_qkv,
    q_bias,
    v_bias,
    w_out,
    out_bias,
    ln2_gain,
    ln2_bias,
    w_up,
    up_bias,
    w_down,
    down_bias,
    cotangent,
):
    core = lax.axis_index("c")
    x_at, z_at = lax.axis_index("x"), lax.axis_index("z")
    y_at = lax.axis_index(RING_Y)
    place = jnp.stack([core, x_at, y_at, z_at]).astype(jnp.int32)
    present = jnp.arange(SLOTS) < segment_counts[0]
    present_rows = jnp.repeat(present, HALFSEG)[:, None]
    cot = jnp.where(present_rows, cotangent.reshape(OWN, WIDTH), 0).astype(BF16)

    mine = swap_items(jnp.concatenate([tokens.reshape(OWN, WIDTH), cot], axis=1))
    (parts,) = call(
        halves_kernel,
        None,
        (
            w_qkv, w_out, w_up, ln1_gain, ln1_bias, q_bias, v_bias, out_bias, ln2_gain, ln2_bias, down_bias, up_bias,
        ),
        (((8, 6, ATTN + UP), BF16),),
        (((16, 128), F32), ((6, FF), F32), ((6, UP), F32)),
    )
    rows = lax.all_to_all(parts, EIGHT, 0, 0, tiled=True)
    rows = rows.reshape(2, 24, ATTN + UP)
    attn, ups = rows[:, :, :ATTN], rows[:, :, ATTN:].reshape(48, UP)

    attn = ring_gather(attn, "z")
    ups = ring_gather(ups, "x")
    (downs,) = after([w_down], *attn)
    downs = lax.all_to_all(jnp.broadcast_to(downs[None], (16, 24, WIDTH)), ("x", "z"), 0, 0, tiled=True)
    item = jnp.concatenate([mine, between_cores(mine)], axis=0)
    x, g = item[:, :WIDTH], item[:, WIDTH:]
    attn = jnp.concatenate(ring_order(attn, z_at), axis=1).reshape(BLOCK, ATTN)
    ups = jnp.concatenate(ring_order(ups, x_at), axis=0)

    attn = relay_gather(attn, "x")
    ups = relay_gather(ups, "z")
    (downs,) = after([downs.reshape(DOWN_ROWS, WIDTH)], attn[1])
    downs = relay_gather(downs, "y")

    order = up_order()
    (x,) = after([x], order)
    a1, qkv, own_o, lse, w_in, own_out, small_all, vectors = call(
        attend_kernel,
        place,
        (x, *attn),
        (
            ((ROWS, WIDTH), BF16),
            ((ROWS, QKV), BF16),
            ((ROWS, HALF), BF16),
            ((ROWS, 128), F32),
            ((WIDTH, QKV), BF16),
            ((WIDTH, HALF), BF16),
            ((WIDTH, SMALL), BF16),
            ((16, WIDTH), F32),
        ),
    )
    far_o, far_out = between_cores(own_o), between_cores(own_out)
    up_b = small_all[:, 8:12].reshape(4, 2, 4, 2, 2, 24)
    up_b = lax.dynamic_index_in_dim(up_b, core, 3, keepdims=False)
    up_b = up_b.transpose(1, 3, 0, 2, 4).reshape(1, UP).astype(F32)
    hidden, m_own, m_far, grad_a_own, grad_up_b, grad_down_b, *grads = call(
        mlp_kernel,
        place,
        (vectors, up_b, x, own_o, far_o, own_out, far_out, g, order, *ups, *downs),
        (
            ((ROWS, WIDTH), F32),
            ((OWN, WIDTH), F32),
            ((OWN, WIDTH), F32),
            ((ROWS, WIDTH), F32),
            ((1, UP), F32),
            ((1, WIDTH), F32),
        )
        + (((BLOCK, UP), BF16),) * 4
        + (((DOWN_ROWS, WIDTH), BF16),) * 4,
        (
            ((ROWS, WIDTH), BF16),
            ((WIDTH, WIDTH), BF16),
            ((ROWS, WIDTH), BF16),
            ((ROWS, WIDTH), BF16),
            ((WIDTH, WIDTH), BF16),
        )
        + (((2, WIDTH, WIDTH), BF16),) * 4,
        (28, 20),
        in_any=2,
        out_any=range(6, 14),
    )
    up_cols = grad_up_b.reshape(2, 2, 4, 4, 24).transpose(2, 0, 3, 1, 4)[:, :, :, None]
    up_cols = jnp.where((jnp.arange(2) == core)[:, None, None], up_cols, 0.0).reshape(WIDTH, 4)
    up_high = up_cols.astype(BF16).astype(F32)
    up_cols = jnp.pad(up_high, ((0, 0), (8, SMALL - 12))) + jnp.pad(up_cols - up_high, ((0, 0), (24, SMALL - 28)))

    (grad_a_far,) = after([between_cores(grad_a_own)], up_cols)
    grad_a_far, *grads = lax.optimization_barrier((grad_a_far, *grads))
    grad_ups, grad_downs = grads[:4], grads[4:]
    got_ups, got_downs = relay_start(grad_ups, "z"), relay_start(grad_downs, "y")
    block = (m_own + between_cores(m_far)).astype(BF16)
    *grad_attn, own_x, far_x, gh = call(
        back_kernel,
        place,
        (
            x, hidden, g, grad_a_own, grad_a_far, vectors, own_o, far_o, own_out, far_out, qkv, lse, a1, w_in,
            grad_down_b, up_cols,
        ),
        (((BLOCK, ATTN), BF16),) * 4 + (((OWN, WIDTH), F32),) * 3,
        (
            ((ROWS, WIDTH), BF16),
            ((ROWS, HALF), BF16),
            ((ROWS, QKV), BF16),
            ((128, WIDTH), F32),
            ((WIDTH, ATTN), BF16),
        ),
    )
    ups_ahead, downs_ahead = relay_ahead(grad_ups, got_ups), relay_ahead(grad_downs, got_downs)
    (far_x,) = after([between_cores(far_x)], ups_ahead, downs_ahead)
    (grad_x,) = call(tokens_kernel, place, (x, own_x, far_x, gh, vectors), (((OWN, WIDTH), BF16),))

    got_attn = relay_start(grad_attn, "x")
    got_attn = after(got_attn, grad_x, block)
    attn_ahead = relay_ahead(grad_attn, got_attn)
    far_ups, far_downs = after([send(ups_ahead, "z", 1), send(downs_ahead, "y", 1)], attn_ahead)
    up_sum = relay_end(grad_ups, got_ups, far_ups).astype(BF16)
    down_sum = relay_end(grad_downs, got_downs, far_downs).astype(BF16)
    (far_attn,) = after([send(attn_ahead, "x", 1)], up_sum)
    up_sum = ring_reduce(ring_split(up_sum, x_at), "x").reshape(2, 24, UP)
    attn_sum = relay_end(grad_attn, got_attn, far_attn).astype(BF16).reshape(2, 4, 24, ATTN)
    results = swap_items(after([jnp.concatenate([block, grad_x], axis=1)], attn_sum)[0])
    attn_parts = [a[:, 0] for a in ring_split(attn_sum, z_at, 1)]
    attn_got = ring_sent(attn_parts, "z")
    down_parts = [d.reshape(96, WIDTH) for d in ring_split(after([down_sum], attn_got[1])[0].reshape(4, 4, 24, WIDTH), z_at, 1)]
    down_sum = ring_total(down_parts, ring_sent(down_parts, "z")).astype(BF16)
    attn_sum = ring_total(attn_parts, attn_got)
    block_out = jnp.where(present_rows, results[:, :WIDTH], 0).reshape(tokens.shape)
    sums = jnp.concatenate([attn_sum.astype(BF16), up_sum.astype(BF16)], axis=2)
    sums = sums.reshape(8, 6, ATTN + UP)
    got = lax.all_to_all(sums, EIGHT, 0, 0, tiled=True)
    down_parts = ring_split(down_sum, x_at)
    down_sum = ring_total(down_parts, after(ring_sent(down_parts, "x"), got))
    out_qkv, out_out, out_up, out_down, grad_tokens, *vecs, out_up_b = call(
        outputs_kernel,
        None,
        (got, down_sum, results[:, WIDTH:]),
        (
            ((6, 3 * WIDTH), F32),
            ((6, WIDTH), F32),
            ((6, FF), F32),
            ((24, WIDTH), F32),
            ((OWN, WIDTH), BF16),
        )
        + (((6,), F32),) * 8
        + (((24,), F32),),
        (((128, 128), F32),),
        limit=8 * 1024 * 1024,
    )
    gain_1, bias_1, bias_q, bias_v, bias_out, gain_2, bias_2, bias_down = vecs
    return (
        block_out,
        grad_tokens.reshape(tokens.shape),
        gain_1,
        bias_1,
        out_qkv,
        bias_q,
        bias_v,
        out_out,
        bias_out,
        gain_2,
        bias_2,
        out_up,
        out_up_b,
        out_down,
        bias_down,
    )


def solution(mesh):
    torus = Mesh(np.asarray(mesh.devices).reshape(SIZES), AXES)
    items = P(("x", "yh", "z", "c"), None, "yl", None)
    part, rows = P(AXES), P(AXES, None)
    return jax.shard_map(
        shards,
        mesh=torus,
        in_specs=(
            items, P(("x", "yh", "z", "c")), part, part, rows, part, part, rows, part, part, part, rows, part, rows,
            part, items,
        ),
        out_specs=(
            items, items, part, part, rows, part, part, rows, part, part, part, rows, part, rows, part,
        ),
        check_vma=False,
    )
```

```python
import jax
import jax.numpy as jnp
import numpy as np
from jax import lax
from jax.experimental import pallas as pl
from jax.experimental.pallas import tpu as pltpu
from jax.sharding import Mesh
from jax.sharding import PartitionSpec as P

WIDTH = 768
HEAD = 64
NSUM = 16
SLOTS = 4
SEGLEN = 64
HALFSEG = 32
FF = 3072

EPSILON = 1e-05
MASKED = -1e30
SCALE = HEAD ** (-0.5)

AXES = ("x", "yh", "z", "c", "yl")
SIZES = (4, 2, 4, 2, 2)
QUAD_AXES = ("x", "yh", "z")
QUADS = 32
DEVICES = 128
ROWS = 256
OWN = 128
HALF = WIDTH // 2
QKV = 3 * HALF
UP = FF // 2
SMALL = 128
ATTN = QKV + SMALL + HALF
BLOCK = WIDTH // 4
DOWN_ROWS = UP // 4
RING_Y = ("yh", "yl")
EIGHT = ("yh", "c", "yl")
VMEM_LIMIT = 60 * 1024 * 1024

F32 = jnp.float32
BF16 = jnp.bfloat16


def dot_nn(left, right):
    return jnp.dot(left, right, preferred_element_type=F32)


def dot_tn(left, right):
    return lax.dot_general(left, right, (((0,), (0,)), ((), ())), preferred_element_type=F32)


def dot_nt(left, right):
    return lax.dot_general(left, right, (((1,), (1,)), ((), ())), preferred_element_type=F32)


def normalised(values):
    center = values - jnp.mean(values, axis=-1, keepdims=True)
    spread = jnp.mean(center * center, axis=-1, keepdims=True)
    scale = lax.rsqrt(spread + EPSILON)
    return center * scale, scale


def norm_back(grad, unit, scale, gain):
    inner = grad * gain
    mean = jnp.mean(inner, axis=-1, keepdims=True)
    along = jnp.mean(inner * unit, axis=-1, keepdims=True)
    return scale * (inner - mean - unit * along)


def total(values):
    return jnp.sum(values.astype(F32), axis=0, keepdims=True)


def swap_halves(values):
    return jnp.concatenate([values[OWN:], values[:OWN]], axis=0)


def masks(core):
    def place(dim):
        row = lax.broadcasted_iota(jnp.int32, (ROWS, ROWS), dim)
        second = (row >= OWN).astype(jnp.int32)
        inner = row - second * OWN
        half = core + second - 2 * core * second
        slot = inner // HALFSEG
        return slot, half * HALFSEG + inner - slot * HALFSEG

    query_slot, query_pos = place(0)
    key_slot, key_pos = place(1)
    same = (query_slot == key_slot) & (key_pos <= query_pos)
    earlier = (key_slot < query_slot) & (key_pos >= SEGLEN - NSUM)
    return same | earlier, key_slot >= query_slot - 2


def bring(copies, sems):
    started = [pltpu.make_async_copy(src, dst, sems.at[i]) for i, (src, dst) in enumerate(copies)]
    for copy in started:
        copy.start()
    return [copy.wait for copy in started]


def finish(waits):
    for wait in waits:
        wait()


def row_block(at, size):
    return pl.ds(pl.multiple_of(at * size, 64), size)


def positions(core, at):
    way = 1 - 2 * core
    return at, lax.rem(at + 4 - way, 4), lax.rem(at + 4 + way, 4), lax.rem(at + 2, 4)


def head_lanes(j):
    lane = lax.broadcasted_iota(jnp.int32, (1, 2 * HEAD), 1)
    return jnp.where(lane // HEAD == j, 1.0, 0.0).astype(BF16)


def up_runs(t):
    for yh, yl, x, z in np.ndindex(2, 2, 4, 4):
        yield 96 * ((x * 2 + yh) * 4 + z) + 48 * t + 24 * yl, 24 * (((yh * 2 + yl) * 4 + x) * 4 + z)


def halves_kernel(qkv_ref, out_ref, up_ref, *refs):
    *vec_refs, up_b_ref, parts_ref, rows_ref, wide_ref, half_ref = refs
    rows_ref[...] = jnp.zeros((16, 128), F32)
    for v, ref in enumerate(vec_refs):
        rows_ref[v : v + 1, 0:6] = ref[...].astype(F32).reshape(1, 6)
    rows_ref[8:9, 0:24] = up_b_ref[...].astype(F32).reshape(1, 24)
    row = lax.broadcasted_iota(jnp.int32, (8, 128), 0)
    lane = lax.broadcasted_iota(jnp.int32, (8, 128), 1)
    src = lax.broadcasted_iota(jnp.int32, (128, 128), 0)
    col = lax.broadcasted_iota(jnp.int32, (128, 128), 1)
    one = jnp.where(row == lane, 1.0, 0.0).astype(BF16)
    vecs = jnp.concatenate([rows_ref[0:8, :].astype(BF16), jnp.zeros((120, 128), BF16)], axis=0)
    up_b = jnp.where(lane // 4 == row, jnp.broadcast_to(rows_ref[8:9, :], (8, 128)), 0.0).astype(BF16)
    put = jnp.where((src < 24) & (8 + lax.rem(src, 4) == col), 1.0, 0.0).astype(BF16)
    small = (dot_nt(one, vecs) + dot_nn(up_b, put)).astype(BF16)
    wide_ref[...] = up_ref[...].astype(F32)
    for t in range(2):
        for src, to in up_runs(t):
            half_ref[:, to : to + 24] = wide_ref[:, src : src + 24]
        up = half_ref[...].astype(BF16)
        for at in (2 * t, 2 * t + 1, 2 * t + 4, 2 * t + 5):
            for j in range(3):
                parts_ref[at, :, j * HALF : (j + 1) * HALF] = qkv_ref[:, j * WIDTH + t * HALF : j * WIDTH + (t + 1) * HALF]
            parts_ref[at, :, QKV : QKV + SMALL] = small[:6]
            parts_ref[at, :, QKV + SMALL : ATTN] = out_ref[:, t * HALF : (t + 1) * HALF]
            parts_ref[at, :, ATTN:] = up


def outputs_kernel(
    got_ref, down_ref, tokens_ref,
    qkv_ref, out_ref, up_ref, out_down_ref, out_tokens_ref, *refs,
):
    *vec_refs, up_b_ref, rows_ref = refs
    out_down_ref[...] = down_ref[...]
    out_tokens_ref[...] = tokens_ref[...]
    small = jnp.zeros((6, SMALL), F32)
    for t in range(2):
        rows = [got_ref[at].astype(F32) for at in (2 * t, 2 * t + 1, 2 * t + 4, 2 * t + 5)]
        rows = (rows[0] + rows[1]) + (rows[2] + rows[3])
        for j in range(3):
            qkv_ref[:, j * WIDTH + t * HALF : j * WIDTH + (t + 1) * HALF] = rows[:, j * HALF : (j + 1) * HALF]
        small += rows[:, QKV : QKV + SMALL]
        out_ref[:, t * HALF : (t + 1) * HALF] = rows[:, QKV + SMALL : ATTN]
        for to, src in up_runs(t):
            up_ref[:, to : to + 24] = rows[:, ATTN + src : ATTN + src + 24]
    small = small[:, 0:12] + small[:, 16:28]
    rows_ref[...] = jnp.zeros((128, 128), F32)
    rows_ref[0:6, 0:12] = small
    flipped = rows_ref[...].T
    for v, ref in enumerate(vec_refs):
        ref[...] = flipped[v : v + 1, 0:6].reshape(6)
    up_b_ref[...] = jnp.concatenate([small[j : j + 1, 8:12] for j in range(6)], axis=1).reshape(24)


def attend_kernel(
    place_ref, x_ref, part_0, part_1, part_2, part_3,
    a_ref, qkv_ref, o_ref, lse_ref, w_ref, out_ref, small_ref, vec_ref,
):
    core = place_ref[0]
    for part, at in zip((part_0, part_1, part_2, part_3), positions(core, place_ref[1])):
        rows = pl.ds(pl.multiple_of(at * BLOCK, 64), BLOCK)
        w_ref[rows, :] = part[:, pl.ds(0, QKV)]
        small_ref[rows, :] = part[:, pl.ds(QKV, SMALL)]
        out_ref[rows, :] = part[:, pl.ds(QKV + SMALL, HALF)]
    vec_ref[...] = small_ref[...].astype(F32).T[:16]
    unit, _ = normalised(x_ref[...].astype(F32))
    a = (unit * vec_ref[0:1, :] + vec_ref[1:2, :]).astype(BF16)
    a_ref[...] = a
    here = pl.ds(pl.multiple_of(core * HALF, 128), HALF)
    shift = jnp.concatenate([vec_ref[2:3, here], jnp.zeros((1, HALF), F32), vec_ref[3:4, here]], axis=1)
    qkv_ref[...] = (dot_nn(a, w_ref[...]) + shift).astype(BF16)
    admitted, _ = masks(core)
    lane = lax.broadcasted_iota(jnp.int32, (ROWS, 128), 1)
    kept = jnp.zeros((ROWS, 128), F32)
    for pair in range(3):
        lanes = pl.ds(128 * pair, 128)
        query = qkv_ref[:, lanes]
        key = qkv_ref[:, pl.ds(HALF + 128 * pair, 128)]
        value = qkv_ref[:, pl.ds(2 * HALF + 128 * pair, 128)]
        out = jnp.zeros((ROWS, 128), F32)
        for j in range(2):
            only = head_lanes(j)
            scores = jnp.where(admitted, dot_nt(query * only, key) * SCALE, MASKED)
            top = jnp.max(scores, axis=-1, keepdims=True)
            grown = jnp.exp(scores - top)
            amount = jnp.sum(grown, axis=-1, keepdims=True)
            kept = jnp.where(lane == 2 * pair + j, top + jnp.log(amount), kept)
            probs = (grown * (1.0 / amount)).astype(BF16)
            out += dot_nn(probs, value * only)
        o_ref[:, lanes] = out.astype(BF16)
    lse_ref[...] = kept


def whole_copies(core, own_o, far_o, own_out, far_out, o_ref, out_ref):
    here = pl.ds(pl.multiple_of(core * HALF, 128), HALF)
    there = pl.ds(pl.multiple_of((1 - core) * HALF, 128), HALF)
    return [
        (own_o, o_ref.at[:, here]),
        (far_o.at[pl.ds(0, OWN)], o_ref.at[pl.ds(OWN, OWN), there]),
        (far_o.at[pl.ds(OWN, OWN)], o_ref.at[pl.ds(0, OWN), there]),
        (own_out, out_ref.at[:, here]),
        (far_out, out_ref.at[:, there]),
    ]


def mlp_kernel(
    place_ref, vec_ref, up_b_ref, x_hbm, own_o, far_o, own_out, far_out, g_hbm, order_hbm,
    up_0, up_1, up_2, up_3, down_0, down_1, down_2, down_3,
    h_ref, m_own_ref, m_far_ref, grad_a_ref, grad_up_b_ref, grad_down_b_ref,
    gup_0, gup_1, gup_2, gup_3, gdown_0, gdown_1, gdown_2, gdown_3,
    o_ref, out_ref, x_ref, g_ref, order_ref, up_ref, down_ref, grad_up_ref, grad_down_ref, sems, out_sems,
):
    core = place_ref[0]
    ups = list(zip((up_0, up_1, up_2, up_3), (gup_0, gup_1, gup_2, gup_3), positions(core, place_ref[3])))
    downs = list(zip((down_0, down_1, down_2, down_3), (gdown_0, gdown_1, gdown_2, gdown_3)))
    units = [pl.ds(pl.multiple_of(at * DOWN_ROWS, 128), DOWN_ROWS) for at in positions(core, place_ref[2])]
    pieces = [pl.ds(0, DOWN_ROWS), pl.ds(DOWN_ROWS, DOWN_ROWS)]
    copies = whole_copies(core, own_o, far_o, own_out, far_out, o_ref, out_ref)
    copies += [(x_hbm, x_ref), (order_hbm, order_ref)]
    for half in range(2):
        for e in range(2):
            unit = units[2 * half + e]
            copies += [(up.at[:, unit], up_ref.at[half, row_block(at, BLOCK), pieces[e]]) for up, _, at in ups]
        if half == 0:
            copies += [(g_hbm, g_ref)]
        copies += [(downs[2 * half + e][0], down_ref.at[half, pieces[e]]) for e in range(2)]
    waits = bring(copies, sems)
    finish(waits[:6])
    hidden = x_ref[...].astype(F32) + (dot_nn(o_ref[...], out_ref[...]) + vec_ref[4:5, :])
    h_ref[...] = hidden
    unit, _ = normalised(hidden)
    a = (unit * vec_ref[5:6, :] + vec_ref[6:7, :]).astype(BF16)
    finish(waits[6:7])
    a = dot_nn(a, order_ref[...]).astype(BF16)
    branch = jnp.zeros((ROWS, WIDTH), F32)
    grad_a = jnp.zeros((ROWS, WIDTH), F32)
    out_waits = []
    for half in range(2):
        finish(waits[7:18] if half == 0 else waits[18:])
        g = g_ref[...]
        up = up_ref[half]
        down = down_ref[half]
        first, second = units[2 * half], units[2 * half + 1]
        u = dot_nn(a, up) + jnp.concatenate([up_b_ref[:, first], up_b_ref[:, second]], axis=1)
        phi = 0.5 * (1.0 + lax.erf(u * (0.5**0.5)))
        z = (u * phi).astype(BF16)
        slope = phi + u * (jnp.exp(-0.5 * u * u) * (2.0 * jnp.pi) ** (-0.5))
        branch += dot_nn(z, down)
        gu = (dot_nt(g, down) * slope).astype(BF16)
        grad_down_ref[half] = dot_tn(z, g).astype(BF16)
        grad_up_ref[half] = dot_tn(a, gu).astype(BF16)
        copies = []
        for e in range(2):
            unit = units[2 * half + e]
            copies += [(grad_up_ref.at[half, row_block(at, BLOCK), pieces[e]], gup.at[:, unit]) for _, gup, at in ups]
            copies += [(grad_down_ref.at[half, pieces[e]], downs[2 * half + e][1])]
        out_waits += bring(copies, out_sems.at[pl.ds(10 * half, 10)])
        sums = total(gu)
        grad_up_b_ref[:, first] = sums[:, :DOWN_ROWS]
        grad_up_b_ref[:, second] = sums[:, DOWN_ROWS:]
        grad_a += dot_nt(gu, up)
    grad_a_ref[...] = dot_nt(grad_a.astype(BF16), order_ref[...]).astype(BF16)
    m_own_ref[...] = branch[:OWN] + h_ref[0:OWN, :] + vec_ref[7:8, :]
    m_far_ref[...] = branch[OWN:]
    grad_down_b_ref[...] = total(g_ref[0:OWN, :])
    finish(out_waits)


def back_kernel(
    place_ref, x_ref, h_ref, g_ref, own_grad_ref, far_grad_ref, vec_ref, own_o_ref, far_o_ref, own_out_ref, far_out_ref,
    qkv_ref, lse_ref, a_ref, w_ref, down_b_ref, up_cols_ref,
    part_0, part_1, part_2, part_3, own_x_ref, far_x_ref, gh_ref,
    gh_low_ref, go_ref, gqkv_ref, rows_ref, message_ref,
):
    core = place_ref[0]
    here = pl.multiple_of(core * HALF, 128)
    there = pl.multiple_of((1 - core) * HALF, 128)
    rows_ref[...] = jnp.zeros((128, WIDTH), F32)
    grad_a = own_grad_ref[...].astype(F32) + swap_halves(far_grad_ref[...]).astype(F32)
    unit, scale = normalised(h_ref[...])
    grad_h = g_ref[...].astype(F32) + norm_back(grad_a, unit, scale, vec_ref[5:6, :])
    gh_ref[...] = grad_h[:OWN]
    low = grad_h.astype(BF16)
    gh_low_ref[...] = low
    rows_ref[4:5, :] = total(low[:OWN])
    rows_ref[5:6, :] = total(grad_a[:OWN] * unit[:OWN])
    rows_ref[6:7, :] = total(grad_a[:OWN])
    rows_ref[7:8, :] = down_b_ref[...]
    low_here = gh_low_ref[:, pl.ds(here, HALF)]
    low_there = gh_low_ref[:, pl.ds(there, HALF)]
    rows = pl.ds(here, HALF)
    go_ref[...] = (dot_nt(low_here, own_out_ref[rows, :]) + dot_nt(low_there, far_out_ref[rows, :])).astype(BF16)
    outs = pl.ds(QKV + SMALL, HALF)
    message_ref[pl.ds(here, HALF), outs] = dot_tn(own_o_ref[...], low_here).astype(BF16)
    message_ref[pl.ds(there, HALF), outs] = dot_tn(swap_halves(far_o_ref[...]), low_here).astype(BF16)
    admitted, live = masks(core)
    live = jnp.where(live, 1.0, 0.0)
    lane = lax.broadcasted_iota(jnp.int32, (ROWS, 128), 1)
    for pair in range(3):
        query = qkv_ref[:, pl.ds(128 * pair, 128)]
        key = qkv_ref[:, pl.ds(HALF + 128 * pair, 128)]
        value = qkv_ref[:, pl.ds(2 * HALF + 128 * pair, 128)]
        go = go_ref[:, pl.ds(128 * pair, 128)]
        gq = jnp.zeros((ROWS, 128), F32)
        gk = jnp.zeros((ROWS, 128), F32)
        gv = jnp.zeros((ROWS, 128), F32)
        for j in range(2):
            only = head_lanes(j)
            lse = jnp.sum(jnp.where(lane == 2 * pair + j, lse_ref[...], 0.0), axis=-1, keepdims=True)
            scores = jnp.where(admitted, dot_nt(query * only, key) * SCALE, MASKED)
            probs = jnp.exp(scores - lse)
            grad_p = dot_nt(go * only, value)
            grad_s = probs * (grad_p - jnp.sum(probs * grad_p, axis=-1, keepdims=True))
            gq += dot_nn(grad_s.astype(BF16), key * only)
            gk += dot_tn((grad_s * live).astype(BF16), query * only)
            gv += dot_tn((probs * live).astype(BF16), go * only)
        gqkv_ref[:, pl.ds(128 * pair, 128)] = (gq * SCALE).astype(BF16)
        gqkv_ref[:, pl.ds(HALF + 128 * pair, 128)] = (gk * SCALE).astype(BF16)
        gqkv_ref[:, pl.ds(2 * HALF + 128 * pair, 128)] = gv.astype(BF16)
    gqkv = gqkv_ref[...]
    message_ref[:, pl.ds(0, QKV)] = dot_tn(a_ref[...], gqkv).astype(BF16)
    grad_x = dot_nt(gqkv, w_ref[...])
    own_x_ref[...] = grad_x[:OWN]
    far_x_ref[...] = grad_x[OWN:]
    unit, _ = normalised(x_ref[...].astype(F32))
    sums = total(gqkv)
    rows_ref[0:1, :] = total(grad_x * unit)
    rows_ref[1:2, :] = total(grad_x)
    rows_ref[2:3, pl.ds(here, HALF)] = sums[:, :HALF]
    rows_ref[3:4, pl.ds(here, HALF)] = sums[:, 2 * HALF :]
    full = rows_ref[0:8, :]
    high = full.astype(BF16).astype(F32)
    rows_ref[0:8, :] = high
    rows_ref[16:24, :] = full - high
    message_ref[:, pl.ds(QKV, SMALL)] = (rows_ref[...].T + up_cols_ref[...]).astype(BF16)
    for part, at in zip((part_0, part_1, part_2, part_3), positions(core, place_ref[1])):
        part[...] = message_ref[pl.ds(pl.multiple_of(at * BLOCK, 64), BLOCK), :]


def tokens_kernel(place_ref, x_ref, own_x_ref, far_x_ref, gh_ref, vec_ref, out_ref):
    unit, scale = normalised(x_ref[0:OWN, :].astype(F32))
    grad = own_x_ref[...] + far_x_ref[...]
    out_ref[...] = (gh_ref[...] + norm_back(grad, unit, scale, vec_ref[0:1, :])).astype(BF16)


VMEM, ANY = pltpu.VMEM, pl.ANY


def call(kernel, place, args, outs, scratch=(), sems=(), in_any=None, out_any=(), limit=VMEM_LIMIT):
    specs = [pl.BlockSpec(memory_space=ANY if in_any is not None and i >= in_any else VMEM) for i in range(len(args))]
    if place is not None:
        args = (place,) + tuple(args)
        specs = [pl.BlockSpec(memory_space=pltpu.SMEM)] + specs
    return pl.pallas_call(
        kernel,
        out_shape=tuple(jax.ShapeDtypeStruct(s, d) for s, d in outs),
        in_specs=specs,
        out_specs=tuple(pl.BlockSpec(memory_space=ANY if i in out_any else VMEM) for i in range(len(outs))),
        scratch_shapes=[VMEM(s, d) for s, d in scratch] + [pltpu.SemaphoreType.DMA((n,)) for n in sems],
        compiler_params=pltpu.CompilerParams(vmem_limit_bytes=limit),
        cost_estimate=pl.CostEstimate(flops=1, bytes_accessed=1, transcendentals=0),
    )(*args)


def between_cores(values):
    return lax.ppermute(values, "c", [(0, 1), (1, 0)])


def between_chips(values):
    return lax.ppermute(values, "yl", [(0, 1), (1, 0)])


def swap_items(values):
    return lax.ppermute(values, ("c", "yl"), [(0, 0), (1, 2), (2, 1), (3, 3)])


def up_order():
    u = lax.optimization_barrier(jnp.arange(WIDTH, dtype=jnp.int32))
    z, x, yh, i = u // BLOCK, u % BLOCK // 48, u % 48 // 24, u % 24
    n = ((x * 2 + yh) * 4 + z) * 24 + i
    return (n[None, :] == lax.broadcasted_iota(jnp.int32, (WIDTH, WIDTH), 0)).astype(BF16)


def ring(values, axis, by):
    return lax.ppermute(values, axis, [(i, (i + by) % 4) for i in range(4)])


def ring_gather(block, axis):
    return [block, ring(block, axis, -1), ring(block, axis, 2), ring(block, axis, 1)]


def ring_order(blocks, at):
    return [lax.select_n(lax.rem(j - at + 4, 4), *blocks) for j in range(4)]


def ring_sent(blocks, axis):
    return [ring(blocks[1], axis, 1), ring(blocks[2], axis, 2), ring(blocks[3], axis, -1)]


def ring_total(blocks, got):
    return sum((g.astype(F32) for g in got), blocks[0].astype(F32))


def ring_reduce(blocks, axis):
    return ring_total(blocks, ring_sent(blocks, axis))


def ring_split(values, at, axis=0):
    size = values.shape[axis] // 4
    return [lax.dynamic_slice_in_dim(values, lax.rem(at + j, 4) * size, size, axis) for j in range(4)]


def along(axis, by):
    pairs = []
    for x, yh, z, c, yl in np.ndindex(*SIZES):
        at = {"x": x, "y": 2 * yh + yl, "z": z}
        at[axis] = (at[axis] + (by if c == 0 else -by)) % 4
        to = (at["x"], at["y"] // 2, at["z"], c, at["y"] % 2)
        pairs.append((int(np.ravel_multi_index((x, yh, z, c, yl), SIZES)), int(np.ravel_multi_index(to, SIZES))))
    return pairs


def send(values, axis, by):
    return lax.ppermute(values, AXES, along(axis, by))


def relay_gather(block, axis):
    behind = send(block, axis, 1)
    return [block, behind, send(block, axis, -1), send(behind, axis, 1)]


def relay_start(blocks, axis):
    return send(blocks[3], axis, 1), send(blocks[1], axis, -1)


def relay_ahead(blocks, got):
    return (blocks[2].astype(F32) + got[0].astype(F32)).astype(BF16)


def relay_end(blocks, got, far):
    return blocks[0].astype(F32) + got[1].astype(F32) + far.astype(F32)


def after(values, *others):
    tied = lax.optimization_barrier((*values, *others))
    return list(tied[: len(values)])


def by_place(place, first, second, axis=0):
    return jnp.where(
        place == 0, jnp.concatenate([first, second], axis), jnp.concatenate([second, first], axis)
    )


def other_half(values, place):
    rows = values.shape[0] // 2
    return (
        lax.dynamic_slice_in_dim(values, (1 - place) * rows, rows, 0),
        lax.dynamic_slice_in_dim(values, place * rows, rows, 0),
    )


def shards(
    tokens,
    segment_counts,
    ln1_gain,
    ln1_bias,
    w_qkv,
    q_bias,
    v_bias,
    w_out,
    out_bias,
    ln2_gain,
    ln2_bias,
    w_up,
    up_bias,
    w_down,
    down_bias,
    cotangent,
):
    core = lax.axis_index("c")
    x_at, z_at = lax.axis_index("x"), lax.axis_index("z")
    y_at = lax.axis_index(RING_Y)
    place = jnp.stack([core, x_at, y_at, z_at]).astype(jnp.int32)
    present = jnp.arange(SLOTS) < segment_counts[0]
    present_rows = jnp.repeat(present, HALFSEG)[:, None]
    cot = jnp.where(present_rows, cotangent.reshape(OWN, WIDTH), 0).astype(BF16)

    mine = swap_items(jnp.concatenate([tokens.reshape(OWN, WIDTH), cot], axis=1))
    (parts,) = call(
        halves_kernel,
        None,
        (
            w_qkv, w_out, w_up, ln1_gain, ln1_bias, q_bias, v_bias, out_bias, ln2_gain, ln2_bias, down_bias, up_bias,
        ),
        (((8, 6, ATTN + UP), BF16),),
        (((16, 128), F32), ((6, FF), F32), ((6, UP), F32)),
    )
    rows = lax.all_to_all(parts, EIGHT, 0, 0, tiled=True)
    rows = rows.reshape(2, 24, ATTN + UP)
    attn, ups = rows[:, :, :ATTN], rows[:, :, ATTN:].reshape(48, UP)

    attn = ring_gather(attn, "z")
    ups = ring_gather(ups, "x")
    (downs,) = after([jnp.broadcast_to(w_down[None], (16, 24, WIDTH))], *attn[:3])
    downs = lax.all_to_all(downs, ("x", "z"), 0, 0, tiled=True)
    item = jnp.concatenate([mine, between_cores(mine)], axis=0)
    x, g = item[:, :WIDTH], item[:, WIDTH:]
    attn = jnp.concatenate(ring_order(attn, z_at), axis=1).reshape(BLOCK, ATTN)
    ups = jnp.concatenate(ring_order(ups, x_at), axis=0)

    attn = relay_gather(attn, "x")
    ups = relay_gather(ups, "z")
    (downs,) = after([downs.reshape(DOWN_ROWS, WIDTH)], attn[1])
    downs = relay_gather(downs, "y")

    order = up_order()
    (x,) = after([x], order)
    a1, qkv, own_o, lse, w_in, own_out, small_all, vectors = call(
        attend_kernel,
        place,
        (x, *attn),
        (
            ((ROWS, WIDTH), BF16),
            ((ROWS, QKV), BF16),
            ((ROWS, HALF), BF16),
            ((ROWS, 128), F32),
            ((WIDTH, QKV), BF16),
            ((WIDTH, HALF), BF16),
            ((WIDTH, SMALL), BF16),
            ((16, WIDTH), F32),
        ),
    )
    far_o, far_out = between_cores(own_o), between_cores(own_out)
    up_b = small_all[:, 8:12].reshape(4, 2, 4, 2, 2, 24)
    up_b = lax.dynamic_index_in_dim(up_b, core, 3, keepdims=False)
    up_b = up_b.transpose(1, 3, 0, 2, 4).reshape(1, UP).astype(F32)
    hidden, m_own, m_far, grad_a_own, grad_up_b, grad_down_b, *grads = call(
        mlp_kernel,
        place,
        (vectors, up_b, x, own_o, far_o, own_out, far_out, g, order, *ups, *downs),
        (
            ((ROWS, WIDTH), F32),
            ((OWN, WIDTH), F32),
            ((OWN, WIDTH), F32),
            ((ROWS, WIDTH), BF16),
            ((1, UP), F32),
            ((1, WIDTH), F32),
        )
        + (((BLOCK, UP), BF16),) * 4
        + (((DOWN_ROWS, WIDTH), BF16),) * 4,
        (
            ((ROWS, WIDTH), BF16),
            ((WIDTH, WIDTH), BF16),
            ((ROWS, WIDTH), BF16),
            ((ROWS, WIDTH), BF16),
            ((WIDTH, WIDTH), BF16),
        )
        + (((2, WIDTH, WIDTH), BF16),) * 4,
        (28, 20),
        in_any=2,
        out_any=range(6, 14),
    )
    up_cols = grad_up_b.reshape(2, 2, 4, 4, 24).transpose(2, 0, 3, 1, 4)[:, :, :, None]
    up_cols = jnp.where((jnp.arange(2) == core)[:, None, None], up_cols, 0.0).reshape(WIDTH, 4)
    up_high = up_cols.astype(BF16).astype(F32)
    up_cols = jnp.pad(up_high, ((0, 0), (8, SMALL - 12))) + jnp.pad(up_cols - up_high, ((0, 0), (24, SMALL - 28)))

    (grad_a_far,) = after([between_cores(grad_a_own)], up_cols)
    grad_a_far, *grads = lax.optimization_barrier((grad_a_far, *grads))
    grad_ups, grad_downs = grads[:4], grads[4:]
    got_ups, got_downs = relay_start(grad_ups, "z"), relay_start(grad_downs, "y")
    block = (m_own + between_cores(m_far)).astype(BF16)
    *grad_attn, own_x, far_x, gh = call(
        back_kernel,
        place,
        (
            x, hidden, g, grad_a_own, grad_a_far, vectors, own_o, far_o, own_out, far_out, qkv, lse, a1, w_in,
            grad_down_b, up_cols,
        ),
        (((BLOCK, ATTN), BF16),) * 4 + (((OWN, WIDTH), F32),) * 3,
        (
            ((ROWS, WIDTH), BF16),
            ((ROWS, HALF), BF16),
            ((ROWS, QKV), BF16),
            ((128, WIDTH), F32),
            ((WIDTH, ATTN), BF16),
        ),
    )
    ups_ahead, downs_ahead = relay_ahead(grad_ups, got_ups), relay_ahead(grad_downs, got_downs)
    (far_x,) = after([between_cores(far_x)], ups_ahead, downs_ahead)
    (grad_x,) = call(tokens_kernel, place, (x, own_x, far_x, gh, vectors), (((OWN, WIDTH), BF16),))

    got_attn = relay_start(grad_attn, "x")
    got_attn = after(got_attn, grad_x, block)
    attn_ahead = relay_ahead(grad_attn, got_attn)
    far_ups, far_downs = after([send(ups_ahead, "z", 1), send(downs_ahead, "y", 1)], attn_ahead)
    up_sum = relay_end(grad_ups, got_ups, far_ups).astype(BF16)
    down_sum = relay_end(grad_downs, got_downs, far_downs).astype(BF16)
    (far_attn,) = after([send(attn_ahead, "x", 1)], up_sum)
    up_sum = ring_reduce(ring_split(up_sum, x_at), "x").reshape(2, 24, UP)
    attn_sum = relay_end(grad_attn, got_attn, far_attn).astype(BF16).reshape(2, 4, 24, ATTN)
    results = swap_items(after([jnp.concatenate([block, grad_x], axis=1)], attn_sum)[0])
    attn_parts = [a[:, 0] for a in ring_split(attn_sum, z_at, 1)]
    attn_got = ring_sent(attn_parts, "z")
    down_parts = [d.reshape(96, WIDTH) for d in ring_split(after([down_sum], attn_got[1])[0].reshape(4, 4, 24, WIDTH), z_at, 1)]
    down_sum = ring_total(down_parts, ring_sent(down_parts, "z")).astype(BF16)
    attn_sum = ring_total(attn_parts, attn_got)
    block_out = jnp.where(present_rows, results[:, :WIDTH], 0).reshape(tokens.shape)
    sums = jnp.concatenate([attn_sum.astype(BF16), up_sum.astype(BF16)], axis=2)
    sums = sums.reshape(8, 6, ATTN + UP)
    got = lax.all_to_all(sums, EIGHT, 0, 0, tiled=True)
    down_parts = ring_split(down_sum, x_at)
    down_sum = ring_total(down_parts, after(ring_sent(down_parts, "x"), got))
    out_qkv, out_out, out_up, out_down, grad_tokens, *vecs, out_up_b = call(
        outputs_kernel,
        None,
        (got, down_sum, results[:, WIDTH:]),
        (
            ((6, 3 * WIDTH), F32),
            ((6, WIDTH), F32),
            ((6, FF), F32),
            ((24, WIDTH), F32),
            ((OWN, WIDTH), BF16),
        )
        + (((6,), F32),) * 8
        + (((24,), F32),),
        (((128, 128), F32),),
        limit=8 * 1024 * 1024,
    )
    gain_1, bias_1, bias_q, bias_v, bias_out, gain_2, bias_2, bias_down = vecs
    return (
        block_out,
        grad_tokens.reshape(tokens.shape),
        gain_1,
        bias_1,
        out_qkv,
        bias_q,
        bias_v,
        out_out,
        bias_out,
        gain_2,
        bias_2,
        out_up,
        out_up_b,
        out_down,
        bias_down,
    )


def solution(mesh):
    torus = Mesh(np.asarray(mesh.devices).reshape(SIZES), AXES)
    items = P(("x", "yh", "z", "c"), None, "yl", None)
    part, rows = P(AXES), P(AXES, None)
    return jax.shard_map(
        shards,
        mesh=torus,
        in_specs=(
            items, P(("x", "yh", "z", "c")), part, part, rows, part, part, rows, part, part, part, rows, part, rows,
            part, items,
        ),
        out_specs=(
            items, items, part, part, rows, part, part, rows, part, part, part, rows, part, rows, part,
        ),
        check_vma=False,
    )
```
